32 devices in a mesh: ctx: 8 (over y, x, core), head: 4 (over z).
Axes of the slice: x: 2, y: 2, z: 4, core: 2. Of those that a mesh axis runs over, the one named last changes fastest.
Arguments:
- query: bfloat16 [8192, 4096], P('ctx', 'head'), may hold values from -150 to 150
- keys: bfloat16 [8192, 4096], P('ctx', 'head'), may hold values from -5.5 to 5.5, as said below
- values: bfloat16 [8192, 4096], P('ctx', 'head'), may hold values from -6 to 6
- lr_code: int32 [8192, 8], P('ctx', 'head'), may hold values from 2048 to 26623, as said below
- fast_weights: bfloat16 [8, 3, 512, 512], P('head'), may hold values from -0.25 to 0.25
- out_weight: bfloat16 [4096, 4096], P('head'), may hold values from -0.09375 to 0.09375
Outputs:
- layer_out: bfloat16 [8192, 4096], P('ctx', 'head')
- new_weights: bfloat16 [8, 3, 512, 512], P('head')
The draws below stay inside these ranges and needn't reach their ends.
Inputs may be any that keep to these rules, and one draw needn't show every extreme that they name: `keys`: keys of order one. `lr_code`: Fixed-point learning-rate codes in units of 2**-14.
All inputs are finite; a program needn't handle non-finite values.
Results may differ from the reference program's by a relative error of at most 0.025.
Values may be sent and summed in bfloat16 or wider, within the bound.
No kernel may reach another device: no remote copies, remote signals or barrier semaphores. Data moves between devices by JAX's collectives and lax.ppermute only.
A program may use at most 192 MiB of HBM per device.

```python
import math
import jax
import jax.numpy as jnp
from jax import lax

D = 4096
FW = 512
FHEADS = 8
HEAD_DIM = 128
WINDOW = 256
TOKENS = 8192
N_HEAD = 4


def pair_draw(key):
    key_k = jax.random.fold_in(key, 101)
    key_q = jax.random.fold_in(key, 202)
    keys_drawn = jnp.clip(jax.random.normal(key_k, (TOKENS, D), jnp.float32), -5.0, 5.0)
    query_drawn = jnp.clip(jax.random.normal(key_q, (TOKENS, D), jnp.float32), -5.0, 5.0)
    return (query_drawn, keys_drawn)


def draw_query(key, part):
    return pair_draw(key)[0].astype(jnp.bfloat16)


def draw_keys(key, part):
    return pair_draw(key)[1].astype(jnp.bfloat16)


def draw_lr_code(key, part):
    position = jnp.arange(TOKENS, dtype=jnp.int32)[:, None]
    spread = jax.random.randint(jax.random.fold_in(key, 505), (TOKENS, FHEADS), 0, 8192, jnp.int32)
    return 2048 + spread + position * 16384 // TOKENS


def shard_levels(rng, shape, cuts, smallest, high):
    loudness = 1.0
    for dim, parts in cuts:
        steps = jax.random.uniform(jax.random.fold_in(jax.random.fold_in(rng, 6), dim), (parts,), jnp.float32, smallest / len(cuts), high / len(cuts))
        loudness = loudness * jnp.repeat(jnp.exp(steps), shape[dim] // parts).reshape((-1,) + (1,) * (len(shape) - 1 - dim))
    return loudness


def scatter_about(key, shape, width, limit, cuts=(), kind=jnp.bfloat16):
    loudness = shard_levels(key, shape, cuts, -0.22, 0.18) if cuts else 1.0
    values = jax.random.normal(key, shape, jnp.float32) * width * loudness
    return jnp.minimum(jnp.maximum(values, -limit), limit).astype(kind)


def setup_inputs(seed: int = 0) -> dict:
    streams_of = jax.random.split(jax.random.key(seed), 7)
    return {
        "query": draw_query(jax.random.fold_in(streams_of[6], 71), 0),
        "keys": draw_keys(jax.random.fold_in(streams_of[6], 71), 0),
        "values": scatter_about(streams_of[2], (TOKENS, D), 1.0, 6.0, ((0, 8), (1, 4))),
        "lr_code": draw_lr_code(jax.random.fold_in(streams_of[6], 71), 0),
        "fast_weights": scatter_about(streams_of[4], (FHEADS, 3, FW, FW), FW ** -0.5, 0.25, ((0, 4),)),
        "out_weight": scatter_about(streams_of[5], (D, D), D ** -0.5, 0.09375, ((0, 4),)),
    }


base_rate = 0.05

def attention(query, keys, values):
    head_count = D // HEAD_DIM
    block_rows = math.gcd(512, TOKENS)
    q_all = query.reshape(TOKENS, head_count, HEAD_DIM)
    zero_pad = jnp.zeros((WINDOW, head_count, HEAD_DIM), keys.dtype)
    key_all = jnp.concatenate([zero_pad, keys.reshape(TOKENS, head_count, HEAD_DIM)], 0)
    val_all = jnp.concatenate([zero_pad, values.reshape(TOKENS, head_count, HEAD_DIM)], 0)
    score_scale = 1.0 / math.sqrt(HEAD_DIM)

    def one_block(blk_index):
        row_start = blk_index * block_rows
        q_block = lax.dynamic_slice_in_dim(q_all, row_start, block_rows, 0).astype(jnp.float32)
        k_block = lax.dynamic_slice_in_dim(key_all, row_start, block_rows + WINDOW, 0).astype(jnp.float32)
        v_block = lax.dynamic_slice_in_dim(val_all, row_start, block_rows + WINDOW, 0).astype(jnp.float32)
        scores = jnp.einsum('qhd,khd->hqk', q_block, k_block) * score_scale
        q_pos = row_start + jnp.arange(block_rows, dtype=jnp.int32)[:, None]
        k_pos = row_start - WINDOW + jnp.arange(block_rows + WINDOW, dtype=jnp.int32)[None, :]
        live = (k_pos <= q_pos) & (k_pos > q_pos - WINDOW) & (k_pos >= 0)
        scores = jnp.where(live[None], scores, jnp.float32(-1e+30))
        top_score = lax.optimization_barrier(jnp.max(scores, axis=-1, keepdims=True))
        exps = jnp.exp(scores - top_score)
        probs = (exps / lax.optimization_barrier(jnp.sum(exps, axis=-1, keepdims=True))).astype(jnp.bfloat16)
        head_out = jnp.einsum('hqk,khd->qhd', probs.astype(jnp.float32), v_block)
        return head_out.reshape(block_rows, D)
    blocks_out = lax.map(one_block, jnp.arange(TOKENS // block_rows, dtype=jnp.int32))
    return blocks_out.reshape(TOKENS, D)

def contract_rows(left, right):
    return lax.dot_general(left, right, (((0,), (0,)), ((), ())), preferred_element_type=jnp.float32)

def train_head(keys_h, values_h, rate_h, weights):
    gate_in = jnp.dot(keys_h, weights[0], preferred_element_type=jnp.float32)
    up_in = jnp.dot(keys_h, weights[1], preferred_element_type=jnp.float32)
    sigmoid_val = jax.nn.sigmoid(gate_in)
    gated_act = (gate_in * sigmoid_val * up_in).astype(jnp.bfloat16)
    pushed = (rate_h[:, None] * values_h.astype(jnp.float32)).astype(jnp.bfloat16)
    back_grad = lax.dot_general(pushed, weights[2], (((1,), (1,)), ((), ())), preferred_element_type=jnp.float32)
    d_gate = (back_grad * up_in * sigmoid_val * (1.0 + gate_in * (1.0 - sigmoid_val))).astype(jnp.bfloat16)
    d_up = (back_grad * gate_in * sigmoid_val).astype(jnp.bfloat16)
    return jnp.stack([contract_rows(keys_h, d_gate), contract_rows(keys_h, d_up), contract_rows(gated_act, pushed)])

def renorm(start_w, grad_pull, step_size):
    base_w = start_w.astype(jnp.float32)
    updated = base_w + step_size[:, None, None, None] * grad_pull
    old_norm = jnp.sqrt(lax.optimization_barrier(jnp.sum(base_w * base_w, axis=2, keepdims=True)) + 1e-06)
    new_norm = jnp.sqrt(lax.optimization_barrier(jnp.sum(updated * updated, axis=2, keepdims=True)) + 1e-06)
    return (updated * (old_norm / new_norm)).astype(jnp.bfloat16)

def apply_head(query_h, weights):
    gate_in = jnp.dot(query_h, weights[0], preferred_element_type=jnp.float32)
    up_in = jnp.dot(query_h, weights[1], preferred_element_type=jnp.float32)
    gated_q = (gate_in * jax.nn.sigmoid(gate_in) * up_in).astype(jnp.bfloat16)
    head_out = jnp.dot(gated_q, weights[2], preferred_element_type=jnp.float32)
    return head_out * lax.rsqrt(lax.optimization_barrier(jnp.mean(head_out * head_out, axis=-1, keepdims=True)) + 1e-06)

def reference(query, keys, values, lr_code, fast_weights, out_weight):
    attended = attention(query, keys, values)
    rate = lr_code.astype(jnp.float32) * 2.0 ** (-14)
    step_size = base_rate / (math.sqrt(TOKENS) * (lax.optimization_barrier(jnp.sum(rate, axis=0)) / TOKENS))
    grad_pull = jnp.stack([train_head(keys[:, head_idx * FW:(head_idx + 1) * FW], values[:, head_idx * FW:(head_idx + 1) * FW], rate[:, head_idx], fast_weights[head_idx]) for head_idx in range(FHEADS)])
    new_weights = renorm(fast_weights, grad_pull, step_size)
    fast_out = jnp.concatenate([apply_head(query[:, head_idx * FW:(head_idx + 1) * FW], new_weights[head_idx]) for head_idx in range(FHEADS)], 1)
    merged = (attended + fast_out).astype(jnp.bfloat16)
    group_width = D // N_HEAD
    layer_sum = jnp.zeros((TOKENS, D), jnp.float32)
    for group_idx in range(N_HEAD):
        part_out = jnp.dot(merged[:, group_idx * group_width:(group_idx + 1) * group_width], out_weight[group_idx * group_width:(group_idx + 1) * group_width], preferred_element_type=jnp.float32).astype(jnp.bfloat16)
        layer_sum = layer_sum + part_out.astype(jnp.float32)
    return (layer_sum.astype(jnp.bfloat16), new_weights)
```

```python
import functools
import math

import jax
import jax.numpy as jnp
from jax import lax
from jax.experimental import pallas as pl
from jax.experimental.pallas import tpu as pltpu
from jax.sharding import PartitionSpec as P

FW = 512
HEAD_DIM = 128
WINDOW = 256
LANES = 128
BLOCKS = 3 * FW // LANES
HALF = BLOCKS // 2
THIRD = BLOCKS // 4
VMEM = 56 * 2**20

base_rate = 0.05
BF = jnp.bfloat16
F32 = jnp.float32


def mm(a, b):
    return jnp.dot(a, b, preferred_element_type=F32)


def shift(block, axis, distance):
    n = lax.axis_size(axis)
    return lax.ppermute(block, axis, [(i, i + distance) for i in range(n) if 0 <= i + distance < n])


def rotate(block, axis, distance):
    n = lax.axis_size(axis)
    return lax.ppermute(block, axis, [(i, (i + distance) % n) for i in range(n)])


def swap(block, bit):
    n = lax.axis_size("ctx")
    return lax.ppermute(block, "ctx", [(i, i ^ bit) for i in range(n)])


def sigmoid(x):
    return 1.0 / (1.0 + jnp.exp(-x))


def grads_kernel(bit_ref, rate_ref, k_ref, v_ref, w_ref, keep_ref, send_ref, dgu, gated, pushed):
    rows = k_ref.shape[0]
    tile = min(256, rows)
    w0, w1, w2 = w_ref[0, 0], w_ref[0, 1], w_ref[0, 2]
    w2t = w2.T
    for t in range(rows // tile):
        sl = pl.ds(t * tile, tile)
        k = k_ref[sl, :]
        gate = mm(k, w0)
        up = mm(k, w1)
        s = sigmoid(gate)
        rate = jnp.broadcast_to(rate_ref[0, :, sl], (LANES, tile)).T
        rate = jnp.concatenate([rate] * (FW // LANES), axis=1)
        push = (rate * v_ref[sl, :].astype(F32)).astype(BF)
        pushed[sl, :] = push
        back = mm(push, w2t)
        gs = gate * s
        gated[sl, :] = (gs * up).astype(BF)
        dgu[sl, :FW] = (back * up * s * (1.0 + gate * (1.0 - s))).astype(BF)
        dgu[sl, FW:] = (back * gs).astype(BF)
    bit = bit_ref[0]
    kt = k_ref[...].T
    gt = gated[...].T
    wide = 2 * LANES
    for b in range(BLOCKS // 2):
        if b * wide < 2 * FW:
            r = mm(kt, dgu[:, b * wide : (b + 1) * wide])
        else:
            r = mm(gt, pushed[:, b * wide - 2 * FW : (b + 1) * wide - 2 * FW])
        r = r.astype(BF)
        half, pos = (2 * b) // HALF, (2 * b) % HALF

        @pl.when(bit == half)
        def _():
            keep_ref[0, pos] = r[:, :LANES]
            keep_ref[0, pos + 1] = r[:, LANES:]

        @pl.when(bit != half)
        def _():
            send_ref[0, pos] = r[:, :LANES]
            send_ref[0, pos + 1] = r[:, LANES:]


def grads(bit, rate, keys, values, fast_weights):
    heads = fast_weights.shape[0]
    rows = keys.shape[0]
    out = jax.ShapeDtypeStruct((heads, HALF, FW, LANES), BF)
    col = pl.BlockSpec((rows, FW), lambda h: (0, h))
    blk = pl.BlockSpec((1, HALF, FW, LANES), lambda h: (h, 0, 0, 0))
    return pl.pallas_call(
        grads_kernel,
        grid=(heads,),
        in_specs=[
            pl.BlockSpec(memory_space=pltpu.SMEM),
            pl.BlockSpec((1, 1, rows), lambda h: (h, 0, 0)),
            col,
            col,
            pl.BlockSpec((1, 3, FW, FW), lambda h: (h, 0, 0, 0)),
        ],
        out_specs=[blk, blk],
        out_shape=[out, out],
        scratch_shapes=[
            pltpu.VMEM((rows, 2 * FW), BF),
            pltpu.VMEM((rows, FW), BF),
            pltpu.VMEM((rows, FW), BF),
        ],
        compiler_params=pltpu.CompilerParams(vmem_limit_bytes=VMEM),
        cost_estimate=pl.CostEstimate(
            flops=heads * 12 * rows * FW * FW,
            bytes_accessed=heads * (2 * rows * FW * 2 + 12 * FW * FW),
            transcendentals=heads * rows * FW,
        ),
    )(bit, rate, keys, values, fast_weights)


def attn_kernel(first_ref, q_ref, k_ref, v_ref, rk_ref, rv_ref, o_ref):
    rows = q_ref.shape[0]
    w = WINDOW
    row = lax.broadcasted_iota(jnp.int32, (w, w), 0)
    col = lax.broadcasted_iota(jnp.int32, (w, w), 1)
    own = col <= row
    scale = 1.0 / math.sqrt(HEAD_DIM)
    has_prev = first_ref[0] == 0
    nt = (((1,), (1,)), ((), ()))
    for b in range(rows // w):
        sl = pl.ds(b * w, w)
        q = q_ref[sl, :]
        if b == 0:
            kp, vp = rk_ref[...], rv_ref[...]
        else:
            kp, vp = k_ref[pl.ds((b - 1) * w, w), :], v_ref[pl.ds((b - 1) * w, w), :]
        s_own = lax.dot_general(q, k_ref[sl, :], nt, preferred_element_type=F32)
        s_prev = lax.dot_general(q, kp, nt, preferred_element_type=F32)
        if b == 0:
            s_prev = jnp.where(has_prev, s_prev, -1e30)
        s = jnp.where(own, s_own, s_prev) * scale
        e = jnp.exp(s - jnp.max(s, axis=1, keepdims=True))
        inv = 1.0 / jnp.sum(e, axis=1, keepdims=True)
        p = (e * inv).astype(BF)
        zero = jnp.zeros_like(p)
        o = mm(jnp.where(own, p, zero), v_ref[sl, :]) + mm(jnp.where(own, zero, p), vp)
        o_ref[sl, :] = o.astype(o_ref.dtype)


def attention(first, query, keys, values, rim_keys, rim_values):
    rows, feats = query.shape
    col = pl.BlockSpec((rows, HEAD_DIM), lambda h: (0, h))
    rim = pl.BlockSpec((WINDOW, HEAD_DIM), lambda h: (0, h))
    return pl.pallas_call(
        attn_kernel,
        grid=(feats // HEAD_DIM,),
        in_specs=[pl.BlockSpec(memory_space=pltpu.SMEM), col, col, col, rim, rim],
        out_specs=col,
        out_shape=jax.ShapeDtypeStruct((rows, feats), BF),
        compiler_params=pltpu.CompilerParams(vmem_limit_bytes=VMEM),
        cost_estimate=pl.CostEstimate(
            flops=8 * rows * feats * WINDOW,
            bytes_accessed=4 * rows * feats * 2,
            transcendentals=rows * feats // HEAD_DIM * WINDOW,
        ),
    )(first, query, keys, values, rim_keys, rim_values)


def renorm_kernel(start_ref, step_ref, base_ref, pull_ref, out_ref):
    base = base_ref[0].astype(F32)
    updated = base + step_ref[0] * pull_ref[0].astype(F32)
    old = jnp.sqrt(jnp.sum(base * base, axis=0, keepdims=True) + 1e-06)
    new = jnp.sqrt(jnp.sum(updated * updated, axis=0, keepdims=True) + 1e-06)
    out_ref[0] = (updated * (old / new)).astype(BF)


def renorm(start, step, base, pull):
    per = FW // LANES
    return pl.pallas_call(
        renorm_kernel,
        grid_spec=pltpu.PrefetchScalarGridSpec(
            num_scalar_prefetch=1,
            grid=(pull.shape[0],),
            in_specs=[
                pl.BlockSpec(memory_space=pltpu.SMEM),
                pl.BlockSpec((1, FW, LANES), lambda i, s: ((s[0] + i) // per, 0, (s[0] + i) % per)),
                pl.BlockSpec((1, FW, LANES), lambda i, s: (i, 0, 0)),
            ],
            out_specs=pl.BlockSpec((1, FW, LANES), lambda i, s: (i, 0, 0)),
        ),
        out_shape=jax.ShapeDtypeStruct(pull.shape, BF),
        cost_estimate=pl.CostEstimate(
            flops=10 * pull.size, bytes_accessed=6 * pull.size, transcendentals=0
        ),
    )(start, step, base, pull)


def apply_tile(q, att, weights):
    outs = []
    for h in range(len(weights)):
        n0, n1, n2 = weights[h]
        qh = q[:, h * FW : (h + 1) * FW]
        gate = mm(qh, n0)
        up = mm(qh, n1)
        act = (gate * sigmoid(gate) * up).astype(BF)
        y = mm(act, n2)
        y = y * lax.rsqrt(jnp.mean(y * y, axis=1, keepdims=True) + 1e-06)
        outs.append(att[:, h * FW : (h + 1) * FW].astype(F32) + y)
    return jnp.concatenate(outs, axis=1).astype(BF)


def apply_first_kernel(ids_ref, q_ref, att_ref, mine_ref, mate_ref, o_ref, nw_ref, sem):
    heads = nw_ref.shape[0]

    @pl.when(pl.program_id(0) == 0)
    def _():
        def each(act):
            for h in range(heads):
                for b in range(BLOCKS):
                    half, third, i = b // HALF, (b % HALF) // THIRD, b % THIRD
                    m, j = b // (FW // LANES), b % (FW // LANES)
                    slot = jnp.bitwise_xor(ids_ref[1 + h], third)
                    dst = nw_ref.at[h, m, :, pl.ds(j * LANES, LANES)]
                    own = ids_ref[0] == half

                    @pl.when(own)
                    def _():
                        act(pltpu.make_async_copy(mine_ref.at[h, slot, i], dst, sem.at[h, b]))

                    @pl.when(jnp.logical_not(own))
                    def _():
                        act(pltpu.make_async_copy(mate_ref.at[h, slot, i], dst, sem.at[h, b]))

        each(lambda c: c.start())
        each(lambda c: c.wait())

    weights = [[nw_ref[h, m] for m in range(3)] for h in range(heads)]
    o_ref[...] = apply_tile(q_ref[...], att_ref[...], weights)


def apply_next_kernel(q_ref, att_ref, nw_ref, o_ref):
    weights = [[nw_ref[h, m] for m in range(3)] for h in range(nw_ref.shape[0])]
    o_ref[...] = apply_tile(q_ref[...], att_ref[...], weights)


def apply_cost(rows, heads):
    return pl.CostEstimate(
        flops=heads * 6 * rows * FW * FW,
        bytes_accessed=heads * (6 * rows * FW + 12 * FW * FW),
        transcendentals=heads * rows * FW,
    )


def apply_first(ids, query, attended, mine, mate, rows):
    feats = query.shape[1]
    heads = mine.shape[0]
    tile = min(256, rows)
    row = pl.BlockSpec((tile, feats), lambda r: (r, 0))
    whole = (heads, 3, FW, FW)
    return pl.pallas_call(
        apply_first_kernel,
        grid=(rows // tile,),
        in_specs=[
            pl.BlockSpec(memory_space=pltpu.SMEM),
            row,
            row,
            pl.BlockSpec(memory_space=pl.ANY),
            pl.BlockSpec(memory_space=pl.ANY),
        ],
        out_specs=[row, pl.BlockSpec(whole, lambda r: (0, 0, 0, 0))],
        out_shape=[
            jax.ShapeDtypeStruct((rows, feats), BF),
            jax.ShapeDtypeStruct(whole, BF),
        ],
        scratch_shapes=[pltpu.SemaphoreType.DMA((heads, BLOCKS))],
        compiler_params=pltpu.CompilerParams(vmem_limit_bytes=VMEM),
        cost_estimate=apply_cost(rows, heads),
    )(ids, query, attended, mine, mate)


def apply_next(query, attended, weights, start):
    rows, feats = query.shape[0] - start, query.shape[1]
    tile = min(256, rows)
    off = start // tile
    row = pl.BlockSpec((tile, feats), lambda r: (r + off, 0))
    return pl.pallas_call(
        apply_next_kernel,
        grid=(rows // tile,),
        in_specs=[row, row, pl.BlockSpec(weights.shape, lambda r: (0, 0, 0, 0))],
        out_specs=pl.BlockSpec((tile, feats), lambda r: (r, 0)),
        out_shape=jax.ShapeDtypeStruct((rows, feats), BF),
        compiler_params=pltpu.CompilerParams(vmem_limit_bytes=VMEM),
        cost_estimate=apply_cost(rows, weights.shape[0]),
    )(query, attended, weights)


def scalars(*xs):
    return jnp.stack([jnp.asarray(x, jnp.int32) for x in xs])


def part(x, i, size):
    return lax.dynamic_slice_in_dim(x, i * size, size, 0)


def shards(query, keys, values, lr_code, fast_weights, out_weight):
    rows, feats = query.shape
    contexts, groups = lax.axis_size("ctx"), lax.axis_size("head")
    c, z = lax.axis_index("ctx"), lax.axis_index("head")
    tokens_all = rows * contexts
    heads = fast_weights.shape[0]
    bits = [1 << i for i in range(contexts.bit_length() - 1)]
    bit_of = {b: (c // b) % 2 for b in bits}

    rim_keys = shift(keys[rows - WINDOW :], "ctx", 1)
    rim_values = shift(values[rows - WINDOW :], "ctx", 1)

    rate = lr_code.T.astype(F32) * 2.0 ** (-14)
    rate_sum = lax.psum(jnp.sum(rate, axis=1), "ctx")
    step_size = base_rate / (math.sqrt(tokens_all) * (rate_sum / tokens_all))
    keep, send = grads(scalars(bit_of[1]), rate[:, None, :], keys, values, fast_weights)
    other = swap(send, 1)

    share = feats // contexts
    strip = part(out_weight, c, share)
    width = out_weight.shape[1] // groups

    def block_for(s):
        return lax.dynamic_slice_in_dim(strip, ((z + s) % groups) * width, width, 1)

    strips = jnp.stack([rotate(block_for(s), "head", s) for s in range(1, groups)])

    attended = attention(scalars(c == 0), query, keys, values, rim_keys, rim_values)

    mine = []
    second = [2, 4]
    slots = []
    for h in range(heads):
        near = second[h % 2]
        rest = [b for b in bits[1:] if b != near]
        me = bit_of[near]
        slots.append(me)
        away = swap(part(keep[h], 1 - me, THIRD) + part(other[h], 1 - me, THIRD), near)
        pull = part(keep[h], me, THIRD) + part(other[h], me, THIRD) + away
        for b in rest:
            pull = pull + swap(pull, b)
        start = bit_of[1] * HALF + me * THIRD
        new = renorm(scalars(start), step_size[h : h + 1], fast_weights[h], pull)
        mine.append(jnp.stack([new, swap(new, near)]))
    mine = jnp.stack(mine)
    mate = swap(mine, 1)

    cut = rows // 2
    ids = scalars(bit_of[1], *slots)
    merged_a, new_weights = apply_first(ids, query, attended, mine, mate, cut)

    strips, merged_a = lax.optimization_barrier((strips, merged_a))
    pieces, order = strips[None], [0]
    for b in reversed(bits):
        pieces = jnp.concatenate([pieces, swap(pieces, b)])
        order = order + [o ^ b for o in order]
    cols = jnp.zeros((groups - 1, feats, width), BF)
    for i, o in enumerate(order):
        cols = lax.dynamic_update_slice(cols, pieces[i], (0, (c ^ o) * share, 0))

    to_right, to_left = [shift(merged_a, "head", 1)], [shift(merged_a, "head", -1)]
    merged_r = apply_next(query, attended, new_weights, cut)
    partial = mm(merged_r, out_weight).astype(BF)

    def partial_for(d):
        return lax.dynamic_slice_in_dim(partial, (d % groups) * width, width, 1)

    zero = jnp.zeros((), BF)
    for t in range(1, groups):
        right = to_right[-1] + jnp.where(t <= z, zero, partial_for(z - t + groups))
        left = to_left[-1] + jnp.where(t <= groups - 1 - z, zero, partial_for(z + t))
        to_right.append(shift(right, "head", 1))
        to_left.append(shift(left, "head", -1))
    own_cols = lax.dynamic_slice_in_dim(out_weight, z * width, width, 1)
    out_a = mm(merged_a, own_cols)
    for t in range(groups - 1):
        x = jnp.where(t <= z - 1, to_right[t], to_left[groups - 2 - t])
        out_a = out_a + mm(x, cols[t])
    out_r = partial_for(z).astype(F32) + to_right[-1].astype(F32) + to_left[-1].astype(F32)
    layer_out = jnp.concatenate([out_a.astype(BF), out_r.astype(BF)])
    return (layer_out, new_weights)


def solution(mesh):
    placed = (
        P("ctx", "head"),
        P("ctx", "head"),
        P("ctx", "head"),
        P("ctx", "head"),
        P("head", None, None, None),
        P("head", None),
    )
    return jax.shard_map(
        shards,
        mesh=mesh,
        in_specs=placed,
        out_specs=(P("ctx", "head"), P("head", None, None, None)),
        check_vma=False,
    )
```

```python
import functools
import math

import jax
import jax.numpy as jnp
from jax import lax
from jax.experimental import pallas as pl
from jax.experimental.pallas import tpu as pltpu
from jax.sharding import PartitionSpec as P

FW = 512
HEAD_DIM = 128
WINDOW = 256
LANES = 128
PER = FW // LANES
BLOCKS = 3 * PER
HALF = BLOCKS // 2
THIRD = BLOCKS // 4
TAIL = 16
VMEM = 56 * 2**20

base_rate = 0.05
BF = jnp.bfloat16
F32 = jnp.float32
NT = (((1,), (1,)), ((), ()))

ANY = pl.BlockSpec(memory_space=pl.ANY)
SMEM = pl.BlockSpec(memory_space=pltpu.SMEM)
PARAMS = pltpu.CompilerParams(vmem_limit_bytes=VMEM)


def mm(a, b):
    return jnp.dot(a, b, preferred_element_type=F32)


def shift(block, axis, distance):
    n = lax.axis_size(axis)
    return lax.ppermute(block, axis, [(i, i + distance) for i in range(n) if 0 <= i + distance < n])


def rotate(block, axis, distance):
    n = lax.axis_size(axis)
    return lax.ppermute(block, axis, [(i, (i + distance) % n) for i in range(n)])


def swap(block, bit):
    n = lax.axis_size("ctx")
    return lax.ppermute(block, "ctx", [(i, i ^ bit) for i in range(n)])


def sigmoid(x):
    return 0.5 * jnp.tanh(0.5 * x) + 0.5


def full(shape):
    return pl.BlockSpec(shape, lambda *_: (0,) * len(shape))


def cost(flops, bytes_accessed, transcendentals=0):
    return pl.CostEstimate(
        flops=int(flops), bytes_accessed=int(bytes_accessed), transcendentals=int(transcendentals)
    )


def split_rows(x):
    hi = x.astype(BF).astype(F32)
    mid = (x - hi).astype(BF).astype(F32)
    lo = x - hi - mid
    row = lax.broadcasted_iota(jnp.int32, (TAIL, LANES), 0)
    return jnp.where(row == 0, hi, jnp.where(row == 1, mid, jnp.where(row == 2, lo, 0.0))).astype(BF)


def join_rows(tail):
    return jnp.sum(tail.astype(F32), axis=0, keepdims=True)


def grads_kernel(bit_ref, rate_ref, k_ref, v_ref, w_ref, keep_ref, send_ref, dgu, gated, pushed):
    rows = k_ref.shape[0]
    tile = min(256, rows)
    wide = 2 * LANES
    for t in range(rows // tile):
        sl = pl.ds(t * tile, tile)
        k = k_ref[sl, :]
        rate = jnp.broadcast_to(rate_ref[0, :, sl], (LANES, tile)).T
        rate = jnp.concatenate([rate] * PER, axis=1)
        push = (rate * v_ref[sl, :].astype(F32)).astype(BF)
        pushed[sl, :] = push
        for j in range(FW // wide):
            cs = slice(j * wide, (j + 1) * wide)
            gate = mm(k, w_ref[0, 0, :, cs])
            up = mm(k, w_ref[0, 1, :, cs])
            back = lax.dot_general(push, w_ref[0, 2, cs, :], NT, preferred_element_type=F32)
            s = sigmoid(gate)
            gs = gate * s
            gated[sl, cs] = (gs * up).astype(BF)
            dgu[sl, cs] = (back * up * (s + gs * (1.0 - s))).astype(BF)
            dgu[sl, FW + j * wide : FW + (j + 1) * wide] = (back * gs).astype(BF)
    bit = bit_ref[0]
    tail = split_rows(jnp.broadcast_to(jnp.sum(rate_ref[0], axis=1, keepdims=True), (1, LANES)))
    keep_ref[pl.ds(HALF * FW, TAIL), :] = tail
    send_ref[pl.ds(HALF * FW, TAIL), :] = tail
    kt = k_ref[...].T
    gt = gated[...].T
    for b in range(BLOCKS // 2):
        if b * wide < 2 * FW:
            r = mm(kt, dgu[:, b * wide : (b + 1) * wide])
        else:
            r = mm(gt, pushed[:, b * wide - 2 * FW : (b + 1) * wide - 2 * FW])
        r = r.astype(BF)
        half, pos = (2 * b) // HALF, (2 * b) % HALF

        @pl.when(bit == half)
        def _():
            keep_ref[pl.ds(pos * FW, FW), :] = r[:, :LANES]
            keep_ref[pl.ds((pos + 1) * FW, FW), :] = r[:, LANES:]

        @pl.when(bit != half)
        def _():
            send_ref[pl.ds(pos * FW, FW), :] = r[:, :LANES]
            send_ref[pl.ds((pos + 1) * FW, FW), :] = r[:, LANES:]


def grads(h, bit, rate, keys, values, fast_weights):
    rows = keys.shape[0]
    shape = (HALF * FW + TAIL, LANES)
    out = jax.ShapeDtypeStruct(shape, BF)
    col = pl.BlockSpec((rows, FW), lambda i: (0, h))
    return pl.pallas_call(
        grads_kernel,
        grid=(1,),
        in_specs=[
            SMEM,
            pl.BlockSpec((1, 1, rows), lambda i: (h, 0, 0)),
            col,
            col,
            pl.BlockSpec((1, 3, FW, FW), lambda i: (h, 0, 0, 0)),
        ],
        out_specs=[full(shape), full(shape)],
        out_shape=[out, out],
        scratch_shapes=[
            pltpu.VMEM((rows, 2 * FW), BF),
            pltpu.VMEM((rows, FW), BF),
            pltpu.VMEM((rows, FW), BF),
        ],
        compiler_params=PARAMS,
        cost_estimate=cost(12 * rows * FW * FW, 4 * rows * FW + 12 * FW * FW, rows * FW),
    )(bit, rate, keys, values, fast_weights)


def split_kernel(bit_ref, keep_ref, other_ref, keep_out, send_out):
    n = THIRD * FW
    mine = pl.ds(pl.multiple_of(bit_ref[0] * n, n), n)
    theirs = pl.ds(pl.multiple_of((1 - bit_ref[0]) * n, n), n)
    keep_out[pl.ds(0, n), :] = keep_ref[mine, :] + other_ref[mine, :]
    send_out[pl.ds(0, n), :] = keep_ref[theirs, :] + other_ref[theirs, :]
    tail = pl.ds(HALF * FW, TAIL)
    rate = split_rows(join_rows(keep_ref[tail, :]) + join_rows(other_ref[tail, :]))
    keep_out[pl.ds(n, TAIL), :] = rate
    send_out[pl.ds(n, TAIL), :] = rate


def split(bit, keep, other):
    shape = (THIRD * FW + TAIL, LANES)
    out = jax.ShapeDtypeStruct(shape, BF)
    return pl.pallas_call(
        split_kernel,
        grid=(1,),
        in_specs=[SMEM, full(keep.shape), full(keep.shape)],
        out_specs=[full(shape), full(shape)],
        out_shape=[out, out],
        compiler_params=PARAMS,
        cost_estimate=cost(keep.size, 6 * keep.size),
    )(bit, keep, other)


def total_kernel(a_ref, b_ref, *rest):
    o_ref = rest[-1]
    n = THIRD * FW
    o_ref[pl.ds(0, n), :] = a_ref[pl.ds(0, n), :] + b_ref[pl.ds(0, n), :]
    tail = pl.ds(n, TAIL)
    o_ref[tail, :] = split_rows(join_rows(a_ref[tail, :]) + join_rows(b_ref[tail, :]))


def total(a, b, after):
    return pl.pallas_call(
        total_kernel,
        grid=(1,),
        in_specs=[full(a.shape), full(a.shape)] + [ANY] * len(after),
        out_specs=full(a.shape),
        out_shape=jax.ShapeDtypeStruct(a.shape, BF),
        compiler_params=PARAMS,
        cost_estimate=cost(a.size, 6 * a.size),
    )(a, b, *after)


def renorm_kernel(tokens_all, start_ref, base_ref, a_ref, b_ref, *rest):
    o_ref = rest[-1]
    tail = pl.ds(THIRD * FW, TAIL)
    rate_sum = join_rows(a_ref[tail, :]) + join_rows(b_ref[tail, :])
    step = base_rate / (math.sqrt(tokens_all) * (rate_sum / tokens_all))
    for i in range(THIRD):
        sl = pl.ds(i * FW, FW)
        pull = a_ref[sl, :].astype(F32) + b_ref[sl, :].astype(F32)
        at = start_ref[0] + i
        col = pl.ds(pl.multiple_of((at % PER) * LANES, LANES), LANES)
        base = base_ref[0, at // PER, :, col].astype(F32)
        updated = base + step * pull
        old = jnp.sqrt(jnp.sum(base * base, axis=0, keepdims=True) + 1e-06)
        new = jnp.sqrt(jnp.sum(updated * updated, axis=0, keepdims=True) + 1e-06)
        o_ref[i] = (updated * (old / new)).astype(BF)


def renorm(h, start, tokens_all, fast_weights, a, b, after):
    shape = (THIRD, FW, LANES)
    return pl.pallas_call(
        functools.partial(renorm_kernel, tokens_all),
        grid=(1,),
        in_specs=[
            SMEM,
            pl.BlockSpec((1, 3, FW, FW), lambda i: (h, 0, 0, 0)),
            full(a.shape),
            full(a.shape),
        ]
        + [ANY] * len(after),
        out_specs=full(shape),
        out_shape=jax.ShapeDtypeStruct(shape, BF),
        compiler_params=PARAMS,
        cost_estimate=cost(10 * a.size, 6 * FW * FW + 6 * a.size),
    )(start, fast_weights, a, b, *after)


def attn_kernel(first_ref, q_ref, k_ref, v_ref, rk_ref, rv_ref, *rest):
    o_ref = rest[-1]
    rows = q_ref.shape[0]
    w, d = WINDOW, HEAD_DIM
    row = lax.broadcasted_iota(jnp.int32, (w, w), 0)
    col = lax.broadcasted_iota(jnp.int32, (w, w), 1)
    own = col <= row
    factor = math.log2(math.e) / math.sqrt(d)
    has_prev = first_ref[0] == 0
    ones = jnp.ones((2 * w, LANES), BF)
    for h in range(q_ref.shape[1] // d):
        cs = slice(h * d, (h + 1) * d)
        for b in range(rows // w):
            sl = pl.ds(b * w, w)
            if b == 0:
                k2 = jnp.concatenate([rk_ref[:, cs], k_ref[sl, cs]], axis=0)
                v2 = jnp.concatenate([rv_ref[:, cs], v_ref[sl, cs]], axis=0)
            else:
                both = pl.ds((b - 1) * w, 2 * w)
                k2, v2 = k_ref[both, cs], v_ref[both, cs]
            s2 = lax.dot_general(q_ref[sl, cs], k2, NT, preferred_element_type=F32)
            prev = s2[:, :w]
            if b == 0:
                prev = jnp.where(has_prev, prev, -1e30)
            s = jnp.where(own, s2[:, w:], prev)
            e = jnp.exp2((s - jnp.max(s, axis=1, keepdims=True)) * factor).astype(BF)
            zero = jnp.zeros_like(e)
            e2 = jnp.concatenate([jnp.where(own, zero, e), jnp.where(own, e, zero)], axis=1)
            o = mm(e2, jnp.concatenate([v2, ones], axis=1))
            o_ref[sl, cs] = (o[:, :d] / o[:, d:]).astype(o_ref.dtype)


def attention(piece, width, first, query, keys, values, rim_keys, rim_values, after):
    rows = query.shape[0]
    col = pl.BlockSpec((rows, width), lambda i: (0, piece))
    rim = pl.BlockSpec((WINDOW, width), lambda i: (0, piece))
    return pl.pallas_call(
        attn_kernel,
        grid=(1,),
        in_specs=[SMEM, col, col, col, rim, rim] + [ANY] * len(after),
        out_specs=full((rows, width)),
        out_shape=jax.ShapeDtypeStruct((rows, width), BF),
        compiler_params=PARAMS,
        cost_estimate=cost(
            8 * rows * width * WINDOW, 8 * rows * width, rows * width // HEAD_DIM * WINDOW
        ),
    )(first, query, keys, values, rim_keys, rim_values, *after)


def apply_tile(q, att, w_ref, act):
    wide = 2 * LANES
    for j in range(FW // wide):
        cs = slice(j * wide, (j + 1) * wide)
        gate = mm(q, w_ref[0, :, cs])
        up = mm(q, w_ref[1, :, cs])
        act[:, cs] = (gate * sigmoid(gate) * up).astype(BF)
    y = mm(act[...], w_ref[2])
    y = y * lax.rsqrt(jnp.mean(y * y, axis=1, keepdims=True) + 1e-06)
    return (att.astype(F32) + y).astype(BF)


def joined(refs):
    return jnp.concatenate([r[...] for r in refs], axis=1)


def apply_first_kernel(pieces, ids_ref, q_ref, *rest):
    att_refs, rest = rest[:pieces], rest[pieces:]
    mine_ref, mate_ref = rest[:2]
    o_ref, nw_ref, act, sem = rest[-4:]

    @pl.when(pl.program_id(0) == 0)
    def _():
        def each(do):
            for b in range(BLOCKS):
                half, third, i = b // HALF, (b % HALF) // THIRD, b % THIRD
                slot = jnp.bitwise_xor(ids_ref[1], third)
                dst = nw_ref.at[b // PER, :, pl.ds((b % PER) * LANES, LANES)]
                own = ids_ref[0] == half

                @pl.when(own)
                def _():
                    do(pltpu.make_async_copy(mine_ref.at[slot, i], dst, sem.at[b]))

                @pl.when(jnp.logical_not(own))
                def _():
                    do(pltpu.make_async_copy(mate_ref.at[slot, i], dst, sem.at[b]))

        each(lambda c: c.start())
        each(lambda c: c.wait())

    o_ref[...] = apply_tile(q_ref[...], joined(att_refs), nw_ref, act)


def apply_next_kernel(pieces, q_ref, *rest):
    nw_ref, o_ref, act = rest[pieces:]
    o_ref[...] = apply_tile(q_ref[...], joined(rest[:pieces]), nw_ref, act)


def apply_cost(rows):
    return cost(6 * rows * FW * FW, 6 * rows * FW + 6 * FW * FW, rows * FW)


def apply_first(h, ids, query, attended, mine, mate, rows, after):
    tile = min(256, rows)
    att = pl.BlockSpec((tile, attended[0].shape[1]), lambda r: (r, 0))
    whole = (3, FW, FW)
    return pl.pallas_call(
        functools.partial(apply_first_kernel, len(attended)),
        grid=(rows // tile,),
        in_specs=[SMEM, pl.BlockSpec((tile, FW), lambda r: (r, h))]
        + [att] * len(attended)
        + [ANY] * (2 + len(after)),
        out_specs=[pl.BlockSpec((tile, FW), lambda r: (r, 0)), full(whole)],
        out_shape=[jax.ShapeDtypeStruct((rows, FW), BF), jax.ShapeDtypeStruct(whole, BF)],
        scratch_shapes=[pltpu.VMEM((tile, FW), BF), pltpu.SemaphoreType.DMA((BLOCKS,))],
        compiler_params=PARAMS,
        cost_estimate=apply_cost(rows),
    )(ids, query, *attended, mine, mate, *after)


def apply_next(h, query, attended, weights, start):
    rows = query.shape[0] - start
    tile = min(256, rows)
    off = start // tile
    att = pl.BlockSpec((tile, attended[0].shape[1]), lambda r: (r + off, 0))
    return pl.pallas_call(
        functools.partial(apply_next_kernel, len(attended)),
        grid=(rows // tile,),
        in_specs=[pl.BlockSpec((tile, FW), lambda r: (r + off, h))]
        + [att] * len(attended)
        + [full(weights.shape)],
        out_specs=pl.BlockSpec((tile, FW), lambda r: (r, 0)),
        out_shape=jax.ShapeDtypeStruct((rows, FW), BF),
        scratch_shapes=[pltpu.VMEM((tile, FW), BF)],
        compiler_params=PARAMS,
        cost_estimate=apply_cost(rows),
    )(query, *attended, weights)


def partial_kernel(heads, *refs):
    x_refs, w_ref, o_ref = refs[:heads], refs[heads], refs[heads + 1]
    for j in range(w_ref.shape[1] // FW):
        cs = pl.ds(j * FW, FW)
        o_ref[0, :, cs] = mm(joined(x_refs), w_ref[:, cs]).astype(BF)


def partials(merged, out_weight, groups):
    rows = merged[0].shape[0]
    depth, width = out_weight.shape[0], out_weight.shape[1] // groups
    return pl.pallas_call(
        functools.partial(partial_kernel, len(merged)),
        grid=(groups,),
        in_specs=[full(m.shape) for m in merged]
        + [pl.BlockSpec((depth, width), lambda d: (0, d))],
        out_specs=pl.BlockSpec((1, rows, width), lambda d: (d, 0, 0)),
        out_shape=jax.ShapeDtypeStruct((groups, rows, width), BF),
        compiler_params=PARAMS,
        cost_estimate=cost(
            2 * rows * depth * width * groups, 2 * (rows * width + depth * width) * groups
        ),
    )(*merged, out_weight)


def ring_kernel(ids_ref, right_ref, left_ref, pr_ref, pl_ref, ro_ref, lo_ref):
    zero = jnp.zeros((), BF)
    ro_ref[...] = right_ref[...] + jnp.where(ids_ref[2] > 0, pr_ref[0], zero)
    lo_ref[...] = left_ref[...] + jnp.where(ids_ref[3] > 0, pl_ref[0], zero)


def ring_step(ids, wave, right, left, partial):
    rows, width = right.shape
    out = jax.ShapeDtypeStruct(right.shape, BF)
    own = pl.BlockSpec((rows, width), lambda i, s: (0, 0))
    return pl.pallas_call(
        ring_kernel,
        grid_spec=pltpu.PrefetchScalarGridSpec(
            num_scalar_prefetch=1,
            grid=(1,),
            in_specs=[
                own,
                own,
                pl.BlockSpec((1, rows, width), lambda i, s: (s[0], 0, wave)),
                pl.BlockSpec((1, rows, width), lambda i, s: (s[1], 0, wave)),
            ],
            out_specs=[own, own],
        ),
        out_shape=[out, out],
        compiler_params=PARAMS,
        cost_estimate=cost(2 * right.size, 12 * right.size),
    )(ids, right, left, partial, partial)


def gathered_kernel(n, heads, parts, ids_ref, pos_ref, *refs):
    own_refs, refs = refs[:heads], refs[heads:]
    rights, refs = refs[: (n - 1) * heads], refs[(n - 1) * heads :]
    lefts, refs = refs[: (n - 1) * heads], refs[(n - 1) * heads :]
    w_ref, near_ref, far_ref, o_ref, x, cols, acc, xsem, wsem = refs
    share = near_ref.shape[2]
    near = near_ref.shape[0]

    def each(do):
        for t in range(n - 1):
            for h in range(heads):
                dst = x.at[t, :, pl.ds(h * FW, FW)]
                sem = xsem.at[t, h]
                from_left = ids_ref[t] > 0

                @pl.when(from_left)
                def _():
                    do(pltpu.make_async_copy(rights[t * heads + h], dst, sem))

                @pl.when(jnp.logical_not(from_left))
                def _():
                    do(pltpu.make_async_copy(lefts[(n - 2 - t) * heads + h], dst, sem))

        for p in range(parts):
            src = near_ref.at[p] if p < near else far_ref.at[p - near]
            to = pl.ds(pl.multiple_of(pos_ref[p] * share, share), share)
            do(pltpu.make_async_copy(src, cols.at[:, to, :], wsem.at[p]))

    each(lambda c: c.start())
    acc[...] = mm(joined(own_refs), w_ref[...])
    each(lambda c: c.wait())
    for t in range(n - 1):
        acc[...] += mm(x[t], cols[t])
    o_ref[...] = acc[...].astype(BF)


def gathered(z, from_left, positions, merged, rights, lefts, out_weight, near, far, rows_all):
    n, heads, parts = len(rights) + 1, len(merged), near.shape[0] + far.shape[0]
    rows, feats = merged[0].shape[0], out_weight.shape[0]
    width = out_weight.shape[1] // n
    ids = jnp.concatenate([from_left, z[None]])
    flat = lambda xs: [x for step in xs for x in step]
    return pl.pallas_call(
        functools.partial(gathered_kernel, n, heads, parts),
        grid_spec=pltpu.PrefetchScalarGridSpec(
            num_scalar_prefetch=2,
            grid=(1,),
            in_specs=[full(m.shape) for m in merged]
            + [ANY] * (2 * (n - 1) * heads)
            + [pl.BlockSpec((feats, width), lambda i, s, p: (0, s[n - 1])), ANY, ANY],
            out_specs=pl.BlockSpec((rows, width), lambda i, s, p: (0, 0)),
            scratch_shapes=[
                pltpu.VMEM((n - 1, rows, feats), BF),
                pltpu.VMEM((n - 1, feats, width), BF),
                pltpu.VMEM((rows, width), F32),
                pltpu.SemaphoreType.DMA((n - 1, heads)),
                pltpu.SemaphoreType.DMA((parts,)),
            ],
        ),
        out_shape=jax.ShapeDtypeStruct((rows_all, width), BF),
        compiler_params=PARAMS,
        cost_estimate=cost(2 * rows * feats * n * width, 2 * n * (rows * feats + feats * width)),
    )(ids, positions, *merged, *flat(rights), *flat(lefts), out_weight, near, far)


def finish_kernel(ids_ref, out_ref, p_ref, right_ref, left_ref, o_ref):
    o_ref[...] = (
        p_ref[0].astype(F32) + right_ref[...].astype(F32) + left_ref[...].astype(F32)
    ).astype(BF)


def finish(z, wave, out, partial, right, left):
    rows, width = right.shape
    own = pl.BlockSpec((rows, width), lambda i, s: (0, 0))
    off = out.shape[0] // rows - 1
    return pl.pallas_call(
        finish_kernel,
        grid_spec=pltpu.PrefetchScalarGridSpec(
            num_scalar_prefetch=1,
            grid=(1,),
            in_specs=[
                ANY,
                pl.BlockSpec((1, rows, width), lambda i, s: (s[0], 0, wave)),
                own,
                own,
            ],
            out_specs=pl.BlockSpec((rows, width), lambda i, s: (off, wave)),
        ),
        out_shape=jax.ShapeDtypeStruct(out.shape, BF),
        input_output_aliases={1: 0},
        compiler_params=PARAMS,
        cost_estimate=cost(2 * right.size, 8 * right.size),
    )(z[None], out, partial, right, left)


def scalars(*xs):
    return jnp.stack([jnp.asarray(x, jnp.int32) for x in xs])


def shards(query, keys, values, lr_code, fast_weights, out_weight):
    rows, feats = query.shape
    contexts, groups = lax.axis_size("ctx"), lax.axis_size("head")
    c, z = lax.axis_index("ctx"), lax.axis_index("head")
    tokens_all = rows * contexts
    heads = fast_weights.shape[0]
    bits = [1 << i for i in range(contexts.bit_length() - 1)]
    bit_of = {b: (c // b) % 2 for b in bits}

    rim_keys = shift(keys[rows - WINDOW :], "ctx", 1)
    rim_values = shift(values[rows - WINDOW :], "ctx", 1)

    share, width = feats // contexts, out_weight.shape[1] // groups

    def block_for(s):
        return lax.dynamic_slice(
            out_weight, (c * share, ((z + s) % groups) * width), (share, width)
        )

    strips = [rotate(block_for(s), "head", s) for s in range(1, groups)]

    rate = lr_code.T.astype(F32)[:, None, :] * 2.0 ** (-14)
    order = [[bits[1 + h % 2]] for h in range(heads)]
    order = [o + [b for b in bits[1:] if b != o[0]] for o in order]
    core = scalars(bit_of[1])
    keep, other = [], []
    for h in range(heads):
        k, s = grads(h, core, rate, keys, values, fast_weights)
        keep.append(k)
        other.append(swap(s, 1))
    split_up = [split(scalars(bit_of[order[h][0]]), keep[h], other[h]) for h in range(heads)]
    away = [swap(split_up[h][1], order[h][0]) for h in range(heads)]

    per_head = 2
    piece_width = FW // per_head
    pieces = []

    def attend(after):
        pieces.append(
            attention(
                len(pieces),
                piece_width,
                scalars(c == 0),
                query,
                keys,
                values,
                rim_keys,
                rim_values,
                after,
            )
        )
        return pieces[-1]

    att = attend([split_up[h][1] for h in range(heads)])
    pull, far = [], []
    for h in range(heads):
        p = total(split_up[h][0], away[h], [att])
        for b in order[h][1:-1]:
            p = total(p, swap(p, b), [])
        pull.append(p)
        far.append(swap(p, order[h][-1]))
        att = attend([p])
    new = []
    for h in range(heads):
        start = scalars(bit_of[1] * HALF + bit_of[order[h][0]] * THIRD)
        after = [att] + (strips if h == 0 else [])
        new.append(renorm(h, start, tokens_all, fast_weights, pull[h], far[h], after))
    while len(pieces) < per_head * heads:
        att = attend(new)
    mine = [jnp.stack([new[h], swap(new[h], order[h][0])]) for h in range(heads)]
    mate = [swap(mine[h], 1) for h in range(heads)]

    cut = rows // 2
    merged, weights = [], []
    for h in range(heads):
        ids = scalars(bit_of[1], bit_of[order[h][0]])
        own = pieces[h * per_head : (h + 1) * per_head]
        m, w = apply_first(h, ids, query, own, mine[h], mate[h], cut, [att])
        merged.append(m)
        weights.append(w)
    to_right = [[shift(m, "head", 1) for m in merged]]
    to_left = [[shift(m, "head", -1) for m in merged]]
    rest = [
        apply_next(h, query, pieces[h * per_head : (h + 1) * per_head], weights[h], cut)
        for h in range(heads)
    ]
    partial = partials(rest, out_weight, groups)
    for t in range(1, groups):
        ids = scalars((z - t) % groups, (z + t) % groups, t > z, t > groups - 1 - z)
        sent = [
            ring_step(ids, h, to_right[-1][h], to_left[-1][h], partial) for h in range(heads)
        ]
        to_right.append([shift(s[0], "head", 1) for s in sent])
        to_left.append([shift(s[1], "head", -1) for s in sent])

    near = jnp.stack(strips)[None]
    places = [0]
    for b in reversed(bits[1:]):
        near = jnp.concatenate([near, swap(near, b)])
        places = places + [p ^ b for p in places]
    other_half = swap(near, 1)
    places = places + [p ^ 1 for p in places]
    positions = jnp.bitwise_xor(c, jnp.array(places, jnp.int32))
    from_left = scalars(*[t <= z - 1 for t in range(groups - 1)])
    out = gathered(
        z, from_left, positions, merged, to_right[:-1], to_left[:-1], out_weight, near, other_half, rows
    )
    for h in range(heads):
        out = finish(z, h, out, partial, to_right[-1][h], to_left[-1][h])
    return (out, jnp.stack(weights))


def solution(mesh):
    placed = (
        P("ctx", "head"),
        P("ctx", "head"),
        P("ctx", "head"),
        P("ctx", "head"),
        P("head", None, None, None),
        P("head", None),
    )
    return jax.shard_map(
        shards,
        mesh=mesh,
        in_specs=placed,
        out_specs=(P("ctx", "head"), P("head", None, None, None)),
        check_vma=False,
    )
```

```python
import functools
import math

import jax
import jax.numpy as jnp
from jax import lax
from jax.experimental import pallas as pl
from jax.experimental.pallas import tpu as pltpu
from jax.sharding import PartitionSpec as P

FW = 512
HEAD_DIM = 128
WINDOW = 256
LANES = 128
PER = FW // LANES
BLOCKS = 3 * PER
HALF = BLOCKS // 2
THIRD = BLOCKS // 4
TAIL = 16

base_rate = 0.05
BF = jnp.bfloat16
F32 = jnp.float32
NT = (((1,), (1,)), ((), ()))

CORE, FIRST, NEAR = 0, 1, 2

ANY = pl.BlockSpec(memory_space=pl.ANY)
HBM = pl.BlockSpec(memory_space=pltpu.HBM)
SMEM = pl.BlockSpec(memory_space=pltpu.SMEM)


def room(mib):
    return pltpu.CompilerParams(vmem_limit_bytes=mib * 2**20)


def mm(a, b):
    return jnp.dot(a, b, preferred_element_type=F32)


def shift(block, axis, distance):
    n = lax.axis_size(axis)
    return lax.ppermute(block, axis, [(i, i + distance) for i in range(n) if 0 <= i + distance < n])


def rotate(block, axis, distance):
    n = lax.axis_size(axis)
    return lax.ppermute(block, axis, [(i, (i + distance) % n) for i in range(n)])


def swap(block, bit):
    n = lax.axis_size("ctx")
    return lax.ppermute(block, "ctx", [(i, i ^ bit) for i in range(n)])


def sigmoid(x):
    return 0.5 * jnp.tanh(0.5 * x) + 0.5


def full(shape):
    return pl.BlockSpec(shape, lambda *_: (0,) * len(shape))


def cost(microseconds):
    return pl.CostEstimate(
        flops=int(microseconds * 0.12e9), bytes_accessed=0, transcendentals=0
    )


def strip_copy(ids_ref, at, w_hbm, o_ref, sem):
    share, width = o_ref.shape
    rows = pl.ds(pl.multiple_of(ids_ref[at] * share, share), share)
    cols = pl.ds(pl.multiple_of(ids_ref[at + 1] * width, width), width)
    return pltpu.make_async_copy(w_hbm.at[rows, cols], o_ref, sem)


def split_rows(x):
    hi = x.astype(BF).astype(F32)
    mid = (x - hi).astype(BF).astype(F32)
    lo = x - hi - mid
    row = lax.broadcasted_iota(jnp.int32, (TAIL, LANES), 0)
    return jnp.where(row == 0, hi, jnp.where(row == 1, mid, jnp.where(row == 2, lo, 0.0))).astype(BF)


def join_rows(tail):
    return jnp.sum(tail.astype(F32), axis=0, keepdims=True)


def grads_kernel(h, at, ids_ref, code_ref, k_hbm, v_hbm, w_hbm, *refs):
    k_ref, v_ref, w_ref, lhs, rhs, sem, ksem, vsem = refs[-8:]
    cols = pl.ds(h * FW, FW)
    rows = k_ref.shape[0]
    tile = min(256, rows)
    copies = [[pltpu.make_async_copy(w_hbm.at[pl.ds(h, 1)], w_ref, sem.at[0])]]
    for t in range(rows // tile):
        sl = pl.ds(t * tile, tile)
        copies.append(
            [
                pltpu.make_async_copy(k_hbm.at[sl, cols], k_ref.at[sl, :], ksem.at[t]),
                pltpu.make_async_copy(v_hbm.at[sl, cols], v_ref.at[sl, :], vsem.at[t]),
            ]
        )
    later = []
    if h == 0:
        ow_hbm, keep_ref, send_ref, rim_ref = refs[:4]
        strip_refs = refs[4:-8]
        last = pl.ds(k_hbm.shape[0] - WINDOW, WINDOW)
        later = [
            pltpu.make_async_copy(k_hbm.at[last, :], rim_ref.at[pl.ds(0, WINDOW), :], sem.at[3]),
            pltpu.make_async_copy(
                v_hbm.at[last, :], rim_ref.at[pl.ds(WINDOW, WINDOW), :], sem.at[4]
            ),
        ] + [
            strip_copy(ids_ref, at + 2 * i, ow_hbm, strip_ref, sem.at[5 + i])
            for i, strip_ref in enumerate(strip_refs)
        ]
    else:
        keep_ref, send_ref = refs[-10:-8]
    for copy in sum(copies, []) + later:
        copy.start()
    copies[0][0].wait()
    wide = 2 * LANES
    codes = code_ref[h : h + 1, :].astype(F32) * 2.0 ** (-14)
    for t in range(rows // tile):
        for copy in copies[1 + t]:
            copy.wait()
        sl = pl.ds(t * tile, tile)
        k = k_ref[sl, :]
        rate = jnp.broadcast_to(codes[:, t * tile : (t + 1) * tile], (LANES, tile)).T
        rate = jnp.concatenate([rate] * PER, axis=1)
        push = (rate * v_ref[sl, :].astype(F32)).astype(BF)
        rhs[sl, 2 * FW :] = push
        for j in range(FW // wide):
            cs = slice(j * wide, (j + 1) * wide)
            gate = mm(k, w_ref[0, 0, :, cs])
            up = mm(k, w_ref[0, 1, :, cs])
            back = lax.dot_general(push, w_ref[0, 2, cs, :], NT, preferred_element_type=F32)
            s = sigmoid(gate)
            gs = gate * s
            lhs[FW + j * wide : FW + (j + 1) * wide, sl] = (gs * up).astype(BF).T
            rhs[sl, cs] = (back * up * (s + gs * (1.0 - s))).astype(BF)
            rhs[sl, FW + j * wide : FW + (j + 1) * wide] = (back * gs).astype(BF)
    lhs[:FW, :] = k_ref[...].T
    tail = split_rows(jnp.broadcast_to(jnp.sum(codes, axis=1, keepdims=True), (1, LANES)))
    pairs = HALF // 2
    for ref, half in ((send_ref, 1 - ids_ref[CORE]), (keep_ref, ids_ref[CORE])):
        ref[pl.ds(HALF * FW, TAIL), :] = tail
        for i in range(pairs):
            pair = half * pairs + i
            left = (pair >= 2 * FW // wide).astype(jnp.int32) * FW
            left = lhs[pl.ds(pl.multiple_of(left, FW), FW), :]
            right = rhs[:, pl.ds(pl.multiple_of(pair * wide, wide), wide)]
            r = mm(left, right).astype(BF)
            ref[pl.ds(2 * i * FW, FW), :] = r[:, :LANES]
            ref[pl.ds((2 * i + 1) * FW, FW), :] = r[:, LANES:]
    for copy in later:
        copy.wait()


def grads(h, at, ids, codes, keys, values, fast_weights, out_weight, strips, after):
    rows, feats = keys.shape
    shape = (HALF * FW + TAIL, LANES)
    outs = [shape, shape] + ([(2 * WINDOW, feats)] + strips if h == 0 else [])
    more = [out_weight] if h == 0 else after
    return pl.pallas_call(
        functools.partial(grads_kernel, h, at),
        grid=(1,),
        in_specs=[SMEM, full(codes.shape), HBM, HBM, HBM]
        + ([HBM] if h == 0 else [ANY] * len(more)),
        out_specs=[full(x) for x in outs],
        out_shape=[jax.ShapeDtypeStruct(x, BF) for x in outs],
        scratch_shapes=[
            pltpu.VMEM((rows, FW), BF),
            pltpu.VMEM((rows, FW), BF),
            pltpu.VMEM((1, 3, FW, FW), BF),
            pltpu.VMEM((2 * FW, rows), BF),
            pltpu.VMEM((rows, 3 * FW), BF),
            pltpu.SemaphoreType.DMA((5 + len(strips),)),
            pltpu.SemaphoreType.DMA((rows // min(256, rows),)),
            pltpu.SemaphoreType.DMA((rows // min(256, rows),)),
        ],
        compiler_params=room(58),
        cost_estimate=cost(8 * rows / 1024),
    )(ids, codes, keys, values, fast_weights, *more)


def fetch(refs, scratch, sem):
    copies = [pltpu.make_async_copy(r, scratch.at[i], sem.at[i]) for i, r in enumerate(refs)]
    for c in copies:
        c.start()
    for c in copies:
        c.wait()


def pair(x):
    return [pltpu.VMEM((2,) + x.shape, x.dtype), pltpu.SemaphoreType.DMA((2,))]


def split_kernel(h, ids_ref, keep_hbm, other_hbm, *refs):
    keep_out, send_out, both, sem = refs[-4:]
    fetch((keep_hbm, other_hbm), both, sem)
    keep_ref, other_ref = both.at[0], both.at[1]
    n = THIRD * FW
    bit = ids_ref[NEAR + h]
    mine = pl.ds(pl.multiple_of(bit * n, n), n)
    theirs = pl.ds(pl.multiple_of((1 - bit) * n, n), n)
    keep_out[pl.ds(0, n), :] = keep_ref[mine, :] + other_ref[mine, :]
    send_out[pl.ds(0, n), :] = keep_ref[theirs, :] + other_ref[theirs, :]
    tail = pl.ds(HALF * FW, TAIL)
    rate = split_rows(join_rows(keep_ref[tail, :]) + join_rows(other_ref[tail, :]))
    keep_out[pl.ds(n, TAIL), :] = rate
    send_out[pl.ds(n, TAIL), :] = rate


def split(h, ids, keep, other, after):
    shape = (THIRD * FW + TAIL, LANES)
    out = jax.ShapeDtypeStruct(shape, BF)
    return pl.pallas_call(
        functools.partial(split_kernel, h),
        grid=(1,),
        in_specs=[SMEM] + [ANY] * (2 + len(after)),
        out_specs=[full(shape), full(shape)],
        out_shape=[out, out],
        scratch_shapes=pair(keep),
        compiler_params=room(12),
        cost_estimate=cost(0.9),
    )(ids, keep, other, *after)


def total_kernel(a_hbm, b_hbm, *rest):
    o_ref, both, sem = rest[-3:]
    fetch((a_hbm, b_hbm), both, sem)
    a_ref, b_ref = both.at[0], both.at[1]
    n = THIRD * FW
    o_ref[pl.ds(0, n), :] = a_ref[pl.ds(0, n), :] + b_ref[pl.ds(0, n), :]
    tail = pl.ds(n, TAIL)
    o_ref[tail, :] = split_rows(join_rows(a_ref[tail, :]) + join_rows(b_ref[tail, :]))


def total(a, b, after):
    return pl.pallas_call(
        total_kernel,
        grid=(1,),
        in_specs=[ANY] * (2 + len(after)),
        out_specs=full(a.shape),
        out_shape=jax.ShapeDtypeStruct(a.shape, BF),
        scratch_shapes=pair(a),
        compiler_params=room(8),
        cost_estimate=cost(0.5),
    )(a, b, *after)


def renorm_kernel(heads, tokens_all, ids_ref, base_ref, *refs):
    outs, (both, sem) = refs[-2 - heads : -2], refs[-2:]
    fetch(refs[: 2 * heads], both, sem)
    tail = pl.ds(THIRD * FW, TAIL)
    for h in range(heads):
        a_ref, b_ref = both.at[2 * h], both.at[2 * h + 1]
        start = ids_ref[CORE] * HALF + ids_ref[NEAR + h] * THIRD
        rate_sum = join_rows(a_ref[tail, :]) + join_rows(b_ref[tail, :])
        step = base_rate / (math.sqrt(tokens_all) * (rate_sum / tokens_all))
        for i in range(THIRD):
            sl = pl.ds(i * FW, FW)
            pull = a_ref[sl, :].astype(F32) + b_ref[sl, :].astype(F32)
            at = start + i
            col = pl.ds(pl.multiple_of((at % PER) * LANES, LANES), LANES)
            base = base_ref[h, at // PER, :, col].astype(F32)
            updated = base + step * pull
            old = jnp.sqrt(jnp.sum(base * base, axis=0, keepdims=True) + 1e-06)
            new = jnp.sqrt(jnp.sum(updated * updated, axis=0, keepdims=True) + 1e-06)
            outs[h][i] = (updated * (old / new)).astype(BF)


def renorm(ids, tokens_all, fast_weights, pulls, after):
    heads, one = fast_weights.shape[0], pulls[0].shape
    shape = (THIRD, FW, LANES)
    return pl.pallas_call(
        functools.partial(renorm_kernel, heads, tokens_all),
        grid=(1,),
        in_specs=[SMEM, full(fast_weights.shape)] + [ANY] * (len(pulls) + len(after)),
        out_specs=[full(shape)] * heads,
        out_shape=[jax.ShapeDtypeStruct(shape, BF)] * heads,
        scratch_shapes=[
            pltpu.VMEM((2 * heads,) + one, BF),
            pltpu.SemaphoreType.DMA((2 * heads,)),
        ],
        compiler_params=room(24),
        cost_estimate=cost(2.1),
    )(ids, fast_weights, *pulls, *after)


def attn_kernel(ids_ref, q_ref, k_ref, v_ref, rim_ref, *rest):
    o_ref = rest[-1]
    rows = q_ref.shape[0]
    w, d = WINDOW, HEAD_DIM
    row = lax.broadcasted_iota(jnp.int32, (w, w), 0)
    col = lax.broadcasted_iota(jnp.int32, (w, w), 1)
    own = col <= row
    factor = math.log2(math.e) / math.sqrt(d)
    has_prev = ids_ref[FIRST] == 0
    ones = jnp.ones((2 * w, LANES), BF)
    for h in range(q_ref.shape[1] // d):
        cs = slice(h * d, (h + 1) * d)
        for b in range(rows // w):
            sl = pl.ds(b * w, w)
            if b == 0:
                k2 = jnp.concatenate([rim_ref[:w, cs], k_ref[sl, cs]], axis=0)
                v2 = jnp.concatenate([rim_ref[w:, cs], v_ref[sl, cs]], axis=0)
            else:
                both = pl.ds((b - 1) * w, 2 * w)
                k2, v2 = k_ref[both, cs], v_ref[both, cs]
            s2 = lax.dot_general(q_ref[sl, cs], k2, NT, preferred_element_type=F32)
            prev = s2[:, :w]
            if b == 0:
                prev = jnp.where(has_prev, prev, -1e30)
            s = jnp.where(own, s2[:, w:], prev)
            e = jnp.exp2((s - jnp.max(s, axis=1, keepdims=True)) * factor).astype(BF)
            zero = jnp.zeros_like(e)
            e2 = jnp.concatenate([jnp.where(own, zero, e), jnp.where(own, e, zero)], axis=1)
            o = mm(e2, jnp.concatenate([v2, ones], axis=1))
            o_ref[sl, cs] = (o[:, :d] / o[:, d:]).astype(o_ref.dtype)


def attention(piece, width, ids, query, keys, values, rim, after):
    rows = query.shape[0]
    col = pl.BlockSpec((rows, width), lambda i: (0, piece))
    of_rim = pl.BlockSpec((2 * WINDOW, width), lambda i: (0, piece))
    return pl.pallas_call(
        attn_kernel,
        grid=(1,),
        in_specs=[SMEM, col, col, col, of_rim] + [ANY] * len(after),
        out_specs=full((rows, width)),
        out_shape=jax.ShapeDtypeStruct((rows, width), BF),
        compiler_params=room(16),
        cost_estimate=cost(2.1 * rows * width / 2**18),
    )(ids, query, keys, values, rim, *after)


def apply_tile(q, att, weights, act):
    wide = 2 * LANES
    rows = q.shape[0]
    for j in range(FW // wide):
        cs = slice(j * wide, (j + 1) * wide)
        gate = mm(q, weights[0, :, cs])
        up = mm(q, weights[1, :, cs])
        act[:rows, cs] = (gate * sigmoid(gate) * up).astype(BF)
    y = mm(act[:rows, :], weights[2])
    y = y * lax.rsqrt(jnp.mean(y * y, axis=1, keepdims=True) + 1e-06)
    return (att.astype(F32) + y).astype(BF)


def apply_kernel(h, pieces, ids_ref, q_hbm, *refs):
    att_hbm, refs = refs[:pieces], refs[pieces:]
    blocks = refs[:4]
    lo_ref, hi_ref, nw_hbm, q, att, nw, act, sem, bsem, osem = refs[-10:]
    rows = q.shape[0]
    core, near = ids_ref[CORE], ids_ref[NEAR + h]
    copies = [pltpu.make_async_copy(q_hbm.at[:, pl.ds(h * FW, FW)], q, sem.at[0])]
    for i, a in enumerate(att_hbm):
        to = att.at[:, pl.ds(i * a.shape[1], a.shape[1])]
        copies.append(pltpu.make_async_copy(a, to, sem.at[1 + i]))
    for n, src in enumerate(blocks):
        half, third = core ^ (n // 2), near ^ (n % 2)
        for i in range(THIRD):
            b = half * HALF + third * THIRD + i
            col = pl.ds(pl.multiple_of((b % PER) * LANES, LANES), LANES)
            dst = nw.at[b // PER, :, col]
            copies.append(pltpu.make_async_copy(src.at[i], dst, bsem.at[n, i]))
    for c in copies:
        c.start()
    for c in copies:
        c.wait()
    out = pltpu.make_async_copy(nw, nw_hbm.at[h], osem)
    out.start()
    cut = lo_ref.shape[0]
    for ref, start in ((lo_ref, 0), (hi_ref, cut)):
        sl = pl.ds(start, ref.shape[0])
        ref[...] = apply_tile(q[sl, :], att[sl, :], nw, act)
    out.wait()


def apply(h, heads, ids, query, attended, blocks, cut, whole, after):
    rows, pieces = query.shape[0], len(attended)
    shape = (heads, 3, FW, FW)
    extra = ([] if whole is None else [whole]) + after
    alias = {} if whole is None else {2 + pieces + len(blocks): 2}
    sizes = [(cut, FW), (rows - cut, FW)]
    return pl.pallas_call(
        functools.partial(apply_kernel, h, pieces),
        grid=(1,),
        in_specs=[SMEM] + [ANY] * (1 + pieces + len(blocks) + len(extra)),
        out_specs=[full(x) for x in sizes] + [ANY],
        out_shape=[jax.ShapeDtypeStruct(x, BF) for x in sizes + [shape]],
        input_output_aliases=alias,
        scratch_shapes=[
            pltpu.VMEM((rows, FW), BF),
            pltpu.VMEM((rows, FW), BF),
            pltpu.VMEM((3, FW, FW), BF),
            pltpu.VMEM((max(cut, rows - cut), FW), BF),
            pltpu.SemaphoreType.DMA((1 + pieces,)),
            pltpu.SemaphoreType.DMA((4, THIRD)),
            pltpu.SemaphoreType.DMA,
        ],
        compiler_params=room(20),
        cost_estimate=cost(3.3 * rows / 1024),
    )(ids, query, *attended, *blocks, *extra)


def joined(refs):
    return jnp.concatenate([r[...] for r in refs], axis=1)


def partial_kernel(heads, *refs):
    x_refs, w_ref = refs[:heads], refs[heads]
    o_ref, x = refs[-2:]

    @pl.when(pl.program_id(0) == 0)
    def _():
        for h in range(heads):
            x[:, h * FW : (h + 1) * FW] = x_refs[h][...]

    o_ref[0] = mm(x[...], w_ref[...]).astype(BF)


def partials(merged, out_weight, groups, after):
    rows, heads = merged[0].shape[0], len(merged)
    feats, width = out_weight.shape[0], out_weight.shape[1] // groups
    return pl.pallas_call(
        functools.partial(partial_kernel, heads),
        grid=(groups,),
        in_specs=[full(m.shape) for m in merged]
        + [pl.BlockSpec((feats, width), lambda d: (0, d))]
        + [ANY] * len(after),
        out_specs=pl.BlockSpec((1, rows, width), lambda d: (d, 0, 0)),
        out_shape=jax.ShapeDtypeStruct((groups, rows, width), BF),
        scratch_shapes=[pltpu.VMEM((rows, feats), BF)],
        compiler_params=room(24),
        cost_estimate=cost(1 * rows / 512),
    )(*merged, out_weight, *after)


def stack_kernel(n, *refs):
    o_ref = refs[-1]
    at = 0
    for r in refs[:n]:
        o_ref[pl.ds(at, r.shape[0])] = r[...]
        at += r.shape[0]


def stack(parts, after):
    shape = (sum(p.shape[0] for p in parts),) + parts[0].shape[1:]
    return pl.pallas_call(
        functools.partial(stack_kernel, len(parts)),
        grid=(1,),
        in_specs=[full(p.shape) for p in parts] + [ANY] * len(after),
        out_specs=full(shape),
        out_shape=jax.ShapeDtypeStruct(shape, BF),
        compiler_params=room(20),
        cost_estimate=cost(0.1),
    )(*parts, *after)


def ring_kernel(t, n, at, tail, wave, ids_ref, right_hbm, left_hbm, p_hbm, *refs):
    ro_ref, lo_ref, x_hbm, got, own, sem, xsem = refs[-7:]
    width = right_hbm.shape[1]
    cols = pl.ds(wave * width, width)
    copies = [
        pltpu.make_async_copy(right_hbm, got.at[0], sem.at[0]),
        pltpu.make_async_copy(p_hbm.at[ids_ref[at], :, cols], own.at[0], sem.at[1]),
        pltpu.make_async_copy(left_hbm, got.at[1], sem.at[2]),
        pltpu.make_async_copy(p_hbm.at[ids_ref[at + 1], :, cols], own.at[1], sem.at[3]),
    ]
    for c in copies:
        c.start()
    zero = jnp.zeros((), BF)
    for i, ref in enumerate((ro_ref, lo_ref)):
        copies[2 * i].wait()
        copies[2 * i + 1].wait()
        ref[...] = got[i] + jnp.where(ids_ref[at + 2 + i] > 0, own[i], zero)
    for i, (slot, here) in enumerate(((t - 1, t <= ids_ref[tail]), (n - 1 - t, t < n - ids_ref[tail]))):

        @pl.when(here)
        def _():
            keep = pltpu.make_async_copy(got.at[i], x_hbm.at[slot, :, cols], xsem.at[i])
            keep.start()
            keep.wait()


def ring_step(t, n, ids, at, tail, wave, right, left, partial, x, after):
    out = jax.ShapeDtypeStruct(right.shape, BF)
    kept = jax.ShapeDtypeStruct((n - 1, right.shape[0], partial.shape[2]), BF)
    more = ([] if x is None else [x]) + after
    return pl.pallas_call(
        functools.partial(ring_kernel, t, n, at, tail, wave),
        grid=(1,),
        in_specs=[SMEM] + [ANY] * (3 + len(more)),
        out_specs=[full(right.shape)] * 2 + [ANY],
        out_shape=[out, out, kept],
        input_output_aliases={} if x is None else {4: 2},
        scratch_shapes=[
            pltpu.VMEM((2,) + right.shape, BF),
            pltpu.VMEM((2,) + right.shape, BF),
            pltpu.SemaphoreType.DMA((4,)),
            pltpu.SemaphoreType.DMA((2,)),
        ],
        compiler_params=room(12),
        cost_estimate=cost(30),
    )(ids, right, left, partial, *more)


def gathered_kernel(n, heads, parts, at, ids_ref, *refs):
    own_refs, refs = refs[:heads], refs[heads:]
    x_hbm, refs = refs[0], refs[1:]
    w_ref, near_ref, far_ref = refs[:3]
    o_ref, x, cols, acc, xsem, wsem = refs[-6:]
    share = near_ref.shape[2]
    near = near_ref.shape[0]

    def each(steps, do):
        for t in steps:
            do(t, pltpu.make_async_copy(x_hbm.at[t], x.at[t], xsem.at[t]))
            for p in range(parts):
                src = near_ref.at[p, t] if p < near else far_ref.at[p - near, t]
                to = ids_ref[at + 1 + p] * share
                to = pl.ds(pl.multiple_of(to, share), share)
                do(t, pltpu.make_async_copy(src, cols.at[t, to, :], wsem.at[t, p]))

    each(range(n - 1), lambda t, c: c.start())
    acc[...] = mm(joined(own_refs), w_ref[...])
    for t in range(n - 1):
        each((t,), lambda t, c: c.wait())
        if t < n - 2:
            acc[...] += mm(x[t], cols[t])
        else:
            o_ref[...] = (acc[...] + mm(x[t], cols[t])).astype(BF)


def gathered(ids, at, merged, x, out_weight, near, far, rows_all, after):
    n, heads, parts = x.shape[0] + 1, len(merged), near.shape[0] + far.shape[0]
    rows, feats = merged[0].shape[0], out_weight.shape[0]
    width = out_weight.shape[1] // n
    return pl.pallas_call(
        functools.partial(gathered_kernel, n, heads, parts, at),
        grid_spec=pltpu.PrefetchScalarGridSpec(
            num_scalar_prefetch=1,
            grid=(1,),
            in_specs=[full(m.shape) for m in merged]
            + [ANY]
            + [pl.BlockSpec((feats, width), lambda i, s: (0, s[at])), ANY, ANY]
            + [ANY] * len(after),
            out_specs=pl.BlockSpec((rows, width), lambda i, s: (0, 0)),
            scratch_shapes=[
                pltpu.VMEM((n - 1, rows, feats), BF),
                pltpu.VMEM((n - 1, feats, width), BF),
                pltpu.VMEM((rows, width), F32),
                pltpu.SemaphoreType.DMA((n - 1,)),
                pltpu.SemaphoreType.DMA((n - 1, parts)),
            ],
        ),
        out_shape=jax.ShapeDtypeStruct((rows_all, width), BF),
        compiler_params=room(48),
        cost_estimate=cost(9 * rows / 512),
    )(
        ids, *merged, x, out_weight, near, far, *after
    )


def finish_kernel(at, wave, ids_ref, right_hbm, left_hbm, p_hbm, out_in, o_hbm, got, own, sem):
    del out_in
    rows, width = own.shape
    cols = pl.ds(wave * width, width)
    copies = [
        pltpu.make_async_copy(right_hbm, got.at[0], sem.at[0]),
        pltpu.make_async_copy(left_hbm, got.at[1], sem.at[1]),
        pltpu.make_async_copy(p_hbm.at[ids_ref[at], :, cols], own, sem.at[2]),
    ]
    for c in copies:
        c.start()
    for c in copies:
        c.wait()
    total = own[...].astype(F32) + (got[0].astype(F32) + got[1].astype(F32))
    own[...] = total.astype(BF)
    last = pl.ds(o_hbm.shape[0] - rows, rows)
    out = pltpu.make_async_copy(own, o_hbm.at[last, cols], sem.at[3])
    out.start()
    out.wait()


def finish(ids, at, wave, right, left, partial, out):
    return pl.pallas_call(
        functools.partial(finish_kernel, at, wave),
        grid=(1,),
        in_specs=[SMEM] + [ANY] * 4,
        out_specs=ANY,
        out_shape=jax.ShapeDtypeStruct(out.shape, BF),
        input_output_aliases={4: 0},
        scratch_shapes=[
            pltpu.VMEM((2,) + right.shape, BF),
            pltpu.VMEM(right.shape, BF),
            pltpu.SemaphoreType.DMA((4,)),
        ],
        compiler_params=room(12),
        cost_estimate=cost(30),
    )(ids, right, left, partial, out)


def scalars(*xs):
    return jnp.stack([jnp.asarray(x, jnp.int32) for x in xs])


def shards(query, keys, values, lr_code, fast_weights, out_weight):
    rows, feats = query.shape
    contexts, groups = lax.axis_size("ctx"), lax.axis_size("head")
    c, z = lax.axis_index("ctx"), lax.axis_index("head")
    tokens_all = rows * contexts
    heads = fast_weights.shape[0]
    bits = [1 << i for i in range(contexts.bit_length() - 1)]
    bit_of = {b: (c // b) % 2 for b in bits}
    order = [[bits[1 + h % 2]] for h in range(heads)]
    order = [o + [b for b in bits[1:] if b != o[0]] for o in order]
    spread = bits[2::-1]
    places = [0]
    for b in spread:
        places = places + [p ^ b for p in places]
    share, width = feats // len(places), out_weight.shape[1] // groups
    ids = [bit_of[1], c == 0] + [bit_of[o[0]] for o in order]
    step_at = [len(ids) + 4 * (t - 1) for t in range(groups)]
    for t in range(1, groups):
        ids += [(z - t) % groups, (z + t) % groups, t > z, t > groups - 1 - z]
    tail_at = len(ids)
    ids += [z] + [(c % len(places)) ^ p for p in places]
    strip_at = len(ids)
    for s in range(1, groups):
        ids += [c % len(places), (z + s) % groups]
    ids = scalars(*ids)

    keep, other = [], []
    for h in range(heads):
        g = grads(
            h,
            strip_at,
            ids,
            lr_code.T,
            keys,
            values,
            fast_weights,
            out_weight,
            [(share, width)] * (groups - 1),
            keep[-1:],
        )
        keep.append(g[0])
        other.append(swap(g[1], 1))
        if h == 0:
            rim = shift(g[2], "ctx", 1)
            strips = [rotate(x, "head", s + 1) for s, x in enumerate(g[3:])]
    split_up = []
    for h in range(heads):
        before = [s[1] for s in split_up[-1:]] or [rim]
        split_up.append(split(h, ids, keep[h], other[h], before))
    away = [swap(split_up[h][1], order[h][0]) for h in range(heads)]

    per_head = 2
    pieces = []

    def attend(after):
        i = len(pieces)
        pieces.append(attention(i, FW // per_head, ids, query, keys, values, rim, after))
        return pieces[-1]

    att = attend([s[1] for s in split_up])
    pull, far = [], []
    for h in range(heads):
        more = strips[1:2] if h == heads - 1 else []
        p = total(split_up[h][0], away[h], [att] + pull + more)
        for b in order[h][1:-1]:
            p = total(p, swap(p, b), [])
        pull.append(p)
        far.append(swap(p, order[h][-1]))
        att = attend([p])
    while len(pieces) < per_head * heads:
        att = attend([att])
    both = [x for h in range(heads) for x in (pull[h], far[h])]
    new = renorm(ids, tokens_all, fast_weights, both, [att] + strips[:1])

    cut = rows // 2
    merged, rest, weights = [], [], None
    for h in range(heads):
        b = order[h][0]
        near = swap(new[h], b)
        blocks = [new[h], near, swap(new[h], 1), swap(near, 1)]
        own = pieces[h * per_head : (h + 1) * per_head]
        m, r, weights = apply(h, heads, ids, query, own, blocks, cut, weights, strips)
        merged.append(m)
        rest.append(r)
    to_right = [[shift(m, "head", 1) for m in merged]]
    to_left = [[shift(m, "head", -1) for m in merged]]

    near = stack([s[None] for s in strips], [merged[-1]])
    partial = partials(rest, out_weight, groups, [near])
    near = near.reshape((1,) + near.shape)
    after = near
    x = None
    for t in range(1, groups):
        right, left = [], []
        for h in range(heads):
            r, l, x = ring_step(
                t,
                groups,
                ids,
                step_at[t],
                tail_at,
                h,
                to_right[t - 1][h],
                to_left[t - 1][h],
                partial,
                x,
                [after],
            )
            after = l
            right.append(shift(r, "head", 1))
            left.append(shift(l, "head", -1))
        to_right.append(right)
        to_left.append(left)
        due = spread[:1] if t == 1 else spread[1:-1] if t == groups - 1 else []
        for b in due:
            near = stack([near, swap(near, b)], [after])
    out = gathered(
        ids,
        tail_at,
        merged,
        x,
        out_weight,
        near,
        swap(near, 1),
        rows,
        [after],
    )
    for h in range(heads):
        out = finish(ids, tail_at, h, to_right[-1][h], to_left[-1][h], partial, out)
    return (out, weights)


def solution(mesh):
    placed = (
        P("ctx", "head"),
        P("ctx", "head"),
        P("ctx", "head"),
        P("ctx", "head"),
        P("head", None, None, None),
        P("head", None),
    )
    return jax.shard_map(
        shards,
        mesh=mesh,
        in_specs=placed,
        out_specs=(P("ctx", "head"), P("head", None, None, None)),
        check_vma=False,
    )
```

```python
import functools
import math

import jax
import jax.numpy as jnp
from jax import lax
from jax.experimental import pallas as pl
from jax.experimental.pallas import tpu as pltpu
from jax.sharding import PartitionSpec as P

FW = 512
HEAD_DIM = 128
WINDOW = 256
LANES = 128
PER = FW // LANES
BLOCKS = 3 * PER
HALF = BLOCKS // 2
THIRD = BLOCKS // 4
TAIL = 16

base_rate = 0.05
BF = jnp.bfloat16
F32 = jnp.float32
NT = (((1,), (1,)), ((), ()))

CORE, FIRST, NEAR = 0, 1, 2

ANY = pl.BlockSpec(memory_space=pl.ANY)
SMEM = pl.BlockSpec(memory_space=pltpu.SMEM)


def room(mib):
    return pltpu.CompilerParams(vmem_limit_bytes=mib * 2**20)


def mm(a, b):
    return jnp.dot(a, b, preferred_element_type=F32)


def shift(block, axis, distance):
    n = lax.axis_size(axis)
    return lax.ppermute(block, axis, [(i, i + distance) for i in range(n) if 0 <= i + distance < n])


def rotate(block, axis, distance):
    n = lax.axis_size(axis)
    return lax.ppermute(block, axis, [(i, (i + distance) % n) for i in range(n)])


def swap(block, bit):
    n = lax.axis_size("ctx")
    return lax.ppermute(block, "ctx", [(i, i ^ bit) for i in range(n)])


def sigmoid(x):
    return 0.5 * jnp.tanh(0.5 * x) + 0.5


def full(shape):
    return pl.BlockSpec(shape, lambda *_: (0,) * len(shape))


def cost(microseconds):
    return pl.CostEstimate(
        flops=int(microseconds * 0.12e9), bytes_accessed=0, transcendentals=0
    )


def strip_copy(ids_ref, at, w_hbm, o_ref, sem):
    share, width = o_ref.shape
    rows = pl.ds(pl.multiple_of(ids_ref[at] * share, share), share)
    cols = pl.ds(pl.multiple_of(ids_ref[at + 1] * width, width), width)
    return pltpu.make_async_copy(w_hbm.at[rows, cols], o_ref, sem)


def split_rows(x):
    hi = x.astype(BF).astype(F32)
    mid = (x - hi).astype(BF).astype(F32)
    lo = x - hi - mid
    row = lax.broadcasted_iota(jnp.int32, (TAIL, LANES), 0)
    return jnp.where(row == 0, hi, jnp.where(row == 1, mid, jnp.where(row == 2, lo, 0.0))).astype(BF)


def join_rows(tail):
    return jnp.sum(tail.astype(F32), axis=0, keepdims=True)


def grads_kernel(h, at, ids_ref, code_ref, k_ref, v_ref, w_ref, *refs):
    lhs, rhs, sem = refs[-3:]
    copies = []
    if h == 0:
        k_hbm, v_hbm, ow_hbm, keep_ref, send_ref, rim_ref = refs[:6]
        last = pl.ds(k_hbm.shape[0] - WINDOW, WINDOW)
        copies = [
            pltpu.make_async_copy(k_hbm.at[last, :], rim_ref.at[pl.ds(0, WINDOW), :], sem.at[0]),
            pltpu.make_async_copy(
                v_hbm.at[last, :], rim_ref.at[pl.ds(WINDOW, WINDOW), :], sem.at[1]
            ),
        ] + [
            strip_copy(ids_ref, at + 2 * i, ow_hbm, strip_ref, sem.at[2 + i])
            for i, strip_ref in enumerate(refs[6:-3])
        ]
    else:
        keep_ref, send_ref = refs[-5:-3]
    for copy in copies:
        copy.start()
    rows = k_ref.shape[0]
    tile = min(256, rows)
    wide = 2 * LANES
    codes = code_ref[h : h + 1, :].astype(F32) * 2.0 ** (-14)
    for t in range(rows // tile):
        sl = pl.ds(t * tile, tile)
        k = k_ref[sl, :]
        rate = jnp.broadcast_to(codes[:, t * tile : (t + 1) * tile], (LANES, tile)).T
        rate = jnp.concatenate([rate] * PER, axis=1)
        push = (rate * v_ref[sl, :].astype(F32)).astype(BF)
        rhs[sl, 2 * FW :] = push
        for j in range(FW // wide):
            cs = slice(j * wide, (j + 1) * wide)
            gate = mm(k, w_ref[0, 0, :, cs])
            up = mm(k, w_ref[0, 1, :, cs])
            back = lax.dot_general(push, w_ref[0, 2, cs, :], NT, preferred_element_type=F32)
            s = sigmoid(gate)
            gs = gate * s
            lhs[FW + j * wide : FW + (j + 1) * wide, sl] = (gs * up).astype(BF).T
            rhs[sl, cs] = (back * up * (s + gs * (1.0 - s))).astype(BF)
            rhs[sl, FW + j * wide : FW + (j + 1) * wide] = (back * gs).astype(BF)
    lhs[:FW, :] = k_ref[...].T
    tail = split_rows(jnp.broadcast_to(jnp.sum(codes, axis=1, keepdims=True), (1, LANES)))
    pairs = HALF // 2
    for ref, half in ((send_ref, 1 - ids_ref[CORE]), (keep_ref, ids_ref[CORE])):
        ref[pl.ds(HALF * FW, TAIL), :] = tail
        for i in range(pairs):
            pair = half * pairs + i
            left = (pair >= 2 * FW // wide).astype(jnp.int32) * FW
            left = lhs[pl.ds(pl.multiple_of(left, FW), FW), :]
            right = rhs[:, pl.ds(pl.multiple_of(pair * wide, wide), wide)]
            r = mm(left, right).astype(BF)
            ref[pl.ds(2 * i * FW, FW), :] = r[:, :LANES]
            ref[pl.ds((2 * i + 1) * FW, FW), :] = r[:, LANES:]
    for copy in copies:
        copy.wait()


def grads(h, at, ids, codes, keys, values, fast_weights, out_weight, strips, after):
    rows, feats = keys.shape
    shape = (HALF * FW + TAIL, LANES)
    outs = [shape, shape] + ([(2 * WINDOW, feats)] + strips if h == 0 else [])
    more = [keys, values, out_weight] if h == 0 else after
    col = pl.BlockSpec((rows, FW), lambda i: (0, h))
    return pl.pallas_call(
        functools.partial(grads_kernel, h, at),
        grid=(1,),
        in_specs=[
            SMEM,
            full(codes.shape),
            col,
            col,
            pl.BlockSpec((1, 3, FW, FW), lambda i: (h, 0, 0, 0)),
        ]
        + [ANY] * len(more),
        out_specs=[full(x) for x in outs],
        out_shape=[jax.ShapeDtypeStruct(x, BF) for x in outs],
        scratch_shapes=[
            pltpu.VMEM((2 * FW, rows), BF),
            pltpu.VMEM((rows, 3 * FW), BF),
            pltpu.SemaphoreType.DMA((2 + len(strips),)),
        ],
        compiler_params=room(58),
        cost_estimate=cost(8 * rows / 1024),
    )(ids, codes, keys, values, fast_weights, *more)


def fetch(refs, scratch, sem):
    copies = [pltpu.make_async_copy(r, scratch.at[i], sem.at[i]) for i, r in enumerate(refs)]
    for c in copies:
        c.start()
    for c in copies:
        c.wait()


def pair(x):
    return [pltpu.VMEM((2,) + x.shape, x.dtype), pltpu.SemaphoreType.DMA((2,))]


def split_kernel(h, ids_ref, keep_hbm, other_hbm, *refs):
    keep_out, send_out, both, sem = refs[-4:]
    fetch((keep_hbm, other_hbm), both, sem)
    keep_ref, other_ref = both.at[0], both.at[1]
    n = THIRD * FW
    bit = ids_ref[NEAR + h]
    mine = pl.ds(pl.multiple_of(bit * n, n), n)
    theirs = pl.ds(pl.multiple_of((1 - bit) * n, n), n)
    keep_out[pl.ds(0, n), :] = keep_ref[mine, :] + other_ref[mine, :]
    send_out[pl.ds(0, n), :] = keep_ref[theirs, :] + other_ref[theirs, :]
    tail = pl.ds(HALF * FW, TAIL)
    rate = split_rows(join_rows(keep_ref[tail, :]) + join_rows(other_ref[tail, :]))
    keep_out[pl.ds(n, TAIL), :] = rate
    send_out[pl.ds(n, TAIL), :] = rate


def split(h, ids, keep, other, after):
    shape = (THIRD * FW + TAIL, LANES)
    out = jax.ShapeDtypeStruct(shape, BF)
    return pl.pallas_call(
        functools.partial(split_kernel, h),
        grid=(1,),
        in_specs=[SMEM] + [ANY] * (2 + len(after)),
        out_specs=[full(shape), full(shape)],
        out_shape=[out, out],
        scratch_shapes=pair(keep),
        compiler_params=room(12),
        cost_estimate=cost(0.9),
    )(ids, keep, other, *after)


def total_kernel(a_hbm, b_hbm, *rest):
    o_ref, both, sem = rest[-3:]
    fetch((a_hbm, b_hbm), both, sem)
    a_ref, b_ref = both.at[0], both.at[1]
    n = THIRD * FW
    o_ref[pl.ds(0, n), :] = a_ref[pl.ds(0, n), :] + b_ref[pl.ds(0, n), :]
    tail = pl.ds(n, TAIL)
    o_ref[tail, :] = split_rows(join_rows(a_ref[tail, :]) + join_rows(b_ref[tail, :]))


def total(a, b, after):
    return pl.pallas_call(
        total_kernel,
        grid=(1,),
        in_specs=[ANY] * (2 + len(after)),
        out_specs=full(a.shape),
        out_shape=jax.ShapeDtypeStruct(a.shape, BF),
        scratch_shapes=pair(a),
        compiler_params=room(8),
        cost_estimate=cost(0.5),
    )(a, b, *after)


def renorm_kernel(heads, tokens_all, ids_ref, base_ref, *refs):
    outs, (both, sem) = refs[-2 - heads : -2], refs[-2:]
    fetch(refs[: 2 * heads], both, sem)
    tail = pl.ds(THIRD * FW, TAIL)
    for h in range(heads):
        a_ref, b_ref = both.at[2 * h], both.at[2 * h + 1]
        start = ids_ref[CORE] * HALF + ids_ref[NEAR + h] * THIRD
        rate_sum = join_rows(a_ref[tail, :]) + join_rows(b_ref[tail, :])
        step = base_rate / (math.sqrt(tokens_all) * (rate_sum / tokens_all))
        for i in range(THIRD):
            sl = pl.ds(i * FW, FW)
            pull = a_ref[sl, :].astype(F32) + b_ref[sl, :].astype(F32)
            at = start + i
            col = pl.ds(pl.multiple_of((at % PER) * LANES, LANES), LANES)
            base = base_ref[h, at // PER, :, col].astype(F32)
            updated = base + step * pull
            old = jnp.sqrt(jnp.sum(base * base, axis=0, keepdims=True) + 1e-06)
            new = jnp.sqrt(jnp.sum(updated * updated, axis=0, keepdims=True) + 1e-06)
            outs[h][i] = (updated * (old / new)).astype(BF)


def renorm(ids, tokens_all, fast_weights, pulls, after):
    heads, one = fast_weights.shape[0], pulls[0].shape
    shape = (THIRD, FW, LANES)
    return pl.pallas_call(
        functools.partial(renorm_kernel, heads, tokens_all),
        grid=(1,),
        in_specs=[SMEM, full(fast_weights.shape)] + [ANY] * (len(pulls) + len(after)),
        out_specs=[full(shape)] * heads,
        out_shape=[jax.ShapeDtypeStruct(shape, BF)] * heads,
        scratch_shapes=[
            pltpu.VMEM((2 * heads,) + one, BF),
            pltpu.SemaphoreType.DMA((2 * heads,)),
        ],
        compiler_params=room(24),
        cost_estimate=cost(2.1),
    )(ids, fast_weights, *pulls, *after)


def attn_kernel(ids_ref, q_ref, k_ref, v_ref, rim_ref, *rest):
    o_ref = rest[-1]
    rows = q_ref.shape[0]
    w, d = WINDOW, HEAD_DIM
    row = lax.broadcasted_iota(jnp.int32, (w, w), 0)
    col = lax.broadcasted_iota(jnp.int32, (w, w), 1)
    own = col <= row
    factor = math.log2(math.e) / math.sqrt(d)
    has_prev = ids_ref[FIRST] == 0
    ones = jnp.ones((2 * w, LANES), BF)
    for h in range(q_ref.shape[1] // d):
        cs = slice(h * d, (h + 1) * d)
        for b in range(rows // w):
            sl = pl.ds(b * w, w)
            if b == 0:
                k2 = jnp.concatenate([rim_ref[:w, cs], k_ref[sl, cs]], axis=0)
                v2 = jnp.concatenate([rim_ref[w:, cs], v_ref[sl, cs]], axis=0)
            else:
                both = pl.ds((b - 1) * w, 2 * w)
                k2, v2 = k_ref[both, cs], v_ref[both, cs]
            s2 = lax.dot_general(q_ref[sl, cs], k2, NT, preferred_element_type=F32)
            prev = s2[:, :w]
            if b == 0:
                prev = jnp.where(has_prev, prev, -1e30)
            s = jnp.where(own, s2[:, w:], prev)
            e = jnp.exp2((s - jnp.max(s, axis=1, keepdims=True)) * factor).astype(BF)
            zero = jnp.zeros_like(e)
            e2 = jnp.concatenate([jnp.where(own, zero, e), jnp.where(own, e, zero)], axis=1)
            o = mm(e2, jnp.concatenate([v2, ones], axis=1))
            o_ref[sl, cs] = (o[:, :d] / o[:, d:]).astype(o_ref.dtype)


def attention(piece, width, ids, query, keys, values, rim, after):
    rows = query.shape[0]
    col = pl.BlockSpec((rows, width), lambda i: (0, piece))
    of_rim = pl.BlockSpec((2 * WINDOW, width), lambda i: (0, piece))
    return pl.pallas_call(
        attn_kernel,
        grid=(1,),
        in_specs=[SMEM, col, col, col, of_rim] + [ANY] * len(after),
        out_specs=full((rows, width)),
        out_shape=jax.ShapeDtypeStruct((rows, width), BF),
        compiler_params=room(16),
        cost_estimate=cost(2.1 * rows * width / 2**18),
    )(ids, query, keys, values, rim, *after)


def apply_tile(q, att, weights, act):
    wide = 2 * LANES
    rows = q.shape[0]
    for j in range(FW // wide):
        cs = slice(j * wide, (j + 1) * wide)
        gate = mm(q, weights[0, :, cs])
        up = mm(q, weights[1, :, cs])
        act[:rows, cs] = (gate * sigmoid(gate) * up).astype(BF)
    y = mm(act[:rows, :], weights[2])
    y = y * lax.rsqrt(jnp.mean(y * y, axis=1, keepdims=True) + 1e-06)
    return (att.astype(F32) + y).astype(BF)


def apply_kernel(h, pieces, ids_ref, q_hbm, *refs):
    att_hbm, refs = refs[:pieces], refs[pieces:]
    blocks = refs[:4]
    lo_ref, hi_ref, nw_hbm, q, att, nw, act, sem, bsem, osem = refs[-10:]
    rows = q.shape[0]
    core, near = ids_ref[CORE], ids_ref[NEAR + h]
    copies = [pltpu.make_async_copy(q_hbm.at[:, pl.ds(h * FW, FW)], q, sem.at[0])]
    for i, a in enumerate(att_hbm):
        to = att.at[:, pl.ds(i * a.shape[1], a.shape[1])]
        copies.append(pltpu.make_async_copy(a, to, sem.at[1 + i]))
    for n, src in enumerate(blocks):
        half, third = core ^ (n // 2), near ^ (n % 2)
        for i in range(THIRD):
            b = half * HALF + third * THIRD + i
            col = pl.ds(pl.multiple_of((b % PER) * LANES, LANES), LANES)
            dst = nw.at[b // PER, :, col]
            copies.append(pltpu.make_async_copy(src.at[i], dst, bsem.at[n, i]))
    for c in copies:
        c.start()
    for c in copies:
        c.wait()
    out = pltpu.make_async_copy(nw, nw_hbm.at[h], osem)
    out.start()
    cut = lo_ref.shape[0]
    for ref, start in ((lo_ref, 0), (hi_ref, cut)):
        sl = pl.ds(start, ref.shape[0])
        ref[...] = apply_tile(q[sl, :], att[sl, :], nw, act)
    out.wait()


def apply(h, heads, ids, query, attended, blocks, cut, whole, after):
    rows, pieces = query.shape[0], len(attended)
    shape = (heads, 3, FW, FW)
    extra = ([] if whole is None else [whole]) + after
    alias = {} if whole is None else {2 + pieces + len(blocks): 2}
    sizes = [(cut, FW), (rows - cut, FW)]
    return pl.pallas_call(
        functools.partial(apply_kernel, h, pieces),
        grid=(1,),
        in_specs=[SMEM] + [ANY] * (1 + pieces + len(blocks) + len(extra)),
        out_specs=[full(x) for x in sizes] + [ANY],
        out_shape=[jax.ShapeDtypeStruct(x, BF) for x in sizes + [shape]],
        input_output_aliases=alias,
        scratch_shapes=[
            pltpu.VMEM((rows, FW), BF),
            pltpu.VMEM((rows, FW), BF),
            pltpu.VMEM((3, FW, FW), BF),
            pltpu.VMEM((max(cut, rows - cut), FW), BF),
            pltpu.SemaphoreType.DMA((1 + pieces,)),
            pltpu.SemaphoreType.DMA((4, THIRD)),
            pltpu.SemaphoreType.DMA,
        ],
        compiler_params=room(20),
        cost_estimate=cost(3.3 * rows / 1024),
    )(ids, query, *attended, *blocks, *extra)


def joined(refs):
    return jnp.concatenate([r[...] for r in refs], axis=1)


def partial_kernel(heads, *refs):
    x_refs, w_ref = refs[:heads], refs[heads]
    o_ref, x = refs[-2:]

    @pl.when(pl.program_id(0) == 0)
    def _():
        for h in range(heads):
            x[:, h * FW : (h + 1) * FW] = x_refs[h][...]

    o_ref[0] = mm(x[...], w_ref[...]).astype(BF)


def partials(merged, out_weight, groups, after):
    rows, heads = merged[0].shape[0], len(merged)
    feats, width = out_weight.shape[0], out_weight.shape[1] // groups
    return pl.pallas_call(
        functools.partial(partial_kernel, heads),
        grid=(groups,),
        in_specs=[full(m.shape) for m in merged]
        + [pl.BlockSpec((feats, width), lambda d: (0, d))]
        + [ANY] * len(after),
        out_specs=pl.BlockSpec((1, rows, width), lambda d: (d, 0, 0)),
        out_shape=jax.ShapeDtypeStruct((groups, rows, width), BF),
        scratch_shapes=[pltpu.VMEM((rows, feats), BF)],
        compiler_params=room(24),
        cost_estimate=cost(1 * rows / 512),
    )(*merged, out_weight, *after)


def stack_kernel(n, *refs):
    o_ref = refs[-1]
    at = 0
    for r in refs[:n]:
        o_ref[pl.ds(at, r.shape[0])] = r[...]
        at += r.shape[0]


def stack(parts, after):
    shape = (sum(p.shape[0] for p in parts),) + parts[0].shape[1:]
    return pl.pallas_call(
        functools.partial(stack_kernel, len(parts)),
        grid=(1,),
        in_specs=[full(p.shape) for p in parts] + [ANY] * len(after),
        out_specs=full(shape),
        out_shape=jax.ShapeDtypeStruct(shape, BF),
        compiler_params=room(20),
        cost_estimate=cost(0.1),
    )(*parts, *after)


def ring_kernel(t, n, at, tail, wave, ids_ref, right_hbm, left_hbm, p_hbm, *refs):
    ro_ref, lo_ref, x_hbm, got, own, sem, xsem = refs[-7:]
    width = right_hbm.shape[1]
    cols = pl.ds(wave * width, width)
    copies = [
        pltpu.make_async_copy(right_hbm, got.at[0], sem.at[0]),
        pltpu.make_async_copy(p_hbm.at[ids_ref[at], :, cols], own.at[0], sem.at[1]),
        pltpu.make_async_copy(left_hbm, got.at[1], sem.at[2]),
        pltpu.make_async_copy(p_hbm.at[ids_ref[at + 1], :, cols], own.at[1], sem.at[3]),
    ]
    for c in copies:
        c.start()
    zero = jnp.zeros((), BF)
    for i, ref in enumerate((ro_ref, lo_ref)):
        copies[2 * i].wait()
        copies[2 * i + 1].wait()
        ref[...] = got[i] + jnp.where(ids_ref[at + 2 + i] > 0, own[i], zero)
    for i, (slot, here) in enumerate(((t - 1, t <= ids_ref[tail]), (n - 1 - t, t < n - ids_ref[tail]))):

        @pl.when(here)
        def _():
            keep = pltpu.make_async_copy(got.at[i], x_hbm.at[slot, :, cols], xsem.at[i])
            keep.start()
            keep.wait()


def ring_step(t, n, ids, at, tail, wave, right, left, partial, x, after):
    out = jax.ShapeDtypeStruct(right.shape, BF)
    kept = jax.ShapeDtypeStruct((n - 1, right.shape[0], partial.shape[2]), BF)
    more = ([] if x is None else [x]) + after
    return pl.pallas_call(
        functools.partial(ring_kernel, t, n, at, tail, wave),
        grid=(1,),
        in_specs=[SMEM] + [ANY] * (3 + len(more)),
        out_specs=[full(right.shape)] * 2 + [ANY],
        out_shape=[out, out, kept],
        input_output_aliases={} if x is None else {4: 2},
        scratch_shapes=[
            pltpu.VMEM((2,) + right.shape, BF),
            pltpu.VMEM((2,) + right.shape, BF),
            pltpu.SemaphoreType.DMA((4,)),
            pltpu.SemaphoreType.DMA((2,)),
        ],
        compiler_params=room(12),
        cost_estimate=cost(30),
    )(ids, right, left, partial, *more)


def gathered_kernel(n, heads, parts, at, ids_ref, *refs):
    own_refs, refs = refs[:heads], refs[heads:]
    x_hbm, refs = refs[0], refs[1:]
    w_ref, near_ref, far_ref = refs[:3]
    o_ref, x, cols, acc, xsem, wsem = refs[-6:]
    share = near_ref.shape[2]
    near = near_ref.shape[0]

    def each(steps, do):
        for t in steps:
            do(t, pltpu.make_async_copy(x_hbm.at[t], x.at[t], xsem.at[t]))
            for p in range(parts):
                src = near_ref.at[p, t] if p < near else far_ref.at[p - near, t]
                to = ids_ref[at + 1 + p] * share
                to = pl.ds(pl.multiple_of(to, share), share)
                do(t, pltpu.make_async_copy(src, cols.at[t, to, :], wsem.at[t, p]))

    each(range(n - 1), lambda t, c: c.start())
    acc[...] = mm(joined(own_refs), w_ref[...])
    for t in range(n - 1):
        each((t,), lambda t, c: c.wait())
        if t < n - 2:
            acc[...] += mm(x[t], cols[t])
        else:
            o_ref[...] = (acc[...] + mm(x[t], cols[t])).astype(BF)


def gathered(ids, at, merged, x, out_weight, near, far, rows_all, after):
    n, heads, parts = x.shape[0] + 1, len(merged), near.shape[0] + far.shape[0]
    rows, feats = merged[0].shape[0], out_weight.shape[0]
    width = out_weight.shape[1] // n
    return pl.pallas_call(
        functools.partial(gathered_kernel, n, heads, parts, at),
        grid_spec=pltpu.PrefetchScalarGridSpec(
            num_scalar_prefetch=1,
            grid=(1,),
            in_specs=[full(m.shape) for m in merged]
            + [ANY]
            + [pl.BlockSpec((feats, width), lambda i, s: (0, s[at])), ANY, ANY]
            + [ANY] * len(after),
            out_specs=pl.BlockSpec((rows, width), lambda i, s: (0, 0)),
            scratch_shapes=[
                pltpu.VMEM((n - 1, rows, feats), BF),
                pltpu.VMEM((n - 1, feats, width), BF),
                pltpu.VMEM((rows, width), F32),
                pltpu.SemaphoreType.DMA((n - 1,)),
                pltpu.SemaphoreType.DMA((n - 1, parts)),
            ],
        ),
        out_shape=jax.ShapeDtypeStruct((rows_all, width), BF),
        compiler_params=room(48),
        cost_estimate=cost(9 * rows / 512),
    )(
        ids, *merged, x, out_weight, near, far, *after
    )


def finish_kernel(at, wave, ids_ref, right_hbm, left_hbm, p_hbm, out_in, o_hbm, got, own, sem):
    del out_in
    rows, width = own.shape
    cols = pl.ds(wave * width, width)
    copies = [
        pltpu.make_async_copy(right_hbm, got.at[0], sem.at[0]),
        pltpu.make_async_copy(left_hbm, got.at[1], sem.at[1]),
        pltpu.make_async_copy(p_hbm.at[ids_ref[at], :, cols], own, sem.at[2]),
    ]
    for c in copies:
        c.start()
    for c in copies:
        c.wait()
    total = own[...].astype(F32) + (got[0].astype(F32) + got[1].astype(F32))
    own[...] = total.astype(BF)
    last = pl.ds(o_hbm.shape[0] - rows, rows)
    out = pltpu.make_async_copy(own, o_hbm.at[last, cols], sem.at[3])
    out.start()
    out.wait()


def finish(ids, at, wave, right, left, partial, out):
    return pl.pallas_call(
        functools.partial(finish_kernel, at, wave),
        grid=(1,),
        in_specs=[SMEM] + [ANY] * 4,
        out_specs=ANY,
        out_shape=jax.ShapeDtypeStruct(out.shape, BF),
        input_output_aliases={4: 0},
        scratch_shapes=[
            pltpu.VMEM((2,) + right.shape, BF),
            pltpu.VMEM(right.shape, BF),
            pltpu.SemaphoreType.DMA((4,)),
        ],
        compiler_params=room(12),
        cost_estimate=cost(30),
    )(ids, right, left, partial, out)


def scalars(*xs):
    return jnp.stack([jnp.asarray(x, jnp.int32) for x in xs])


def shards(query, keys, values, lr_code, fast_weights, out_weight):
    rows, feats = query.shape
    contexts, groups = lax.axis_size("ctx"), lax.axis_size("head")
    c, z = lax.axis_index("ctx"), lax.axis_index("head")
    tokens_all = rows * contexts
    heads = fast_weights.shape[0]
    bits = [1 << i for i in range(contexts.bit_length() - 1)]
    bit_of = {b: (c // b) % 2 for b in bits}
    order = [[bits[1 + h % 2]] for h in range(heads)]
    order = [o + [b for b in bits[1:] if b != o[0]] for o in order]
    spread = bits[2::-1]
    places = [0]
    for b in spread:
        places = places + [p ^ b for p in places]
    share, width = feats // len(places), out_weight.shape[1] // groups
    ids = [bit_of[1], c == 0] + [bit_of[o[0]] for o in order]
    step_at = [len(ids) + 4 * (t - 1) for t in range(groups)]
    for t in range(1, groups):
        ids += [(z - t) % groups, (z + t) % groups, t > z, t > groups - 1 - z]
    tail_at = len(ids)
    ids += [z] + [(c % len(places)) ^ p for p in places]
    strip_at = len(ids)
    for s in range(1, groups):
        ids += [c % len(places), (z + s) % groups]
    ids = scalars(*ids)

    keep, other = [], []
    for h in range(heads):
        g = grads(
            h,
            strip_at,
            ids,
            lr_code.T,
            keys,
            values,
            fast_weights,
            out_weight,
            [(share, width)] * (groups - 1),
            keep[-1:],
        )
        keep.append(g[0])
        other.append(swap(g[1], 1))
        if h == 0:
            rim = shift(g[2], "ctx", 1)
            strips = [rotate(x, "head", s + 1) for s, x in enumerate(g[3:])]
    split_up = []
    for h in range(heads):
        before = [split_up[0][1], rim] if h else []
        split_up.append(split(h, ids, keep[h], other[h], before))
    away = [swap(split_up[h][1], order[h][0]) for h in range(heads)]

    per_head = 2
    pieces = []

    def attend(after):
        i = len(pieces)
        pieces.append(attention(i, FW // per_head, ids, query, keys, values, rim, after))
        return pieces[-1]

    att = attend([s[1] for s in split_up])
    pull, far = [], []
    for h in range(heads):
        more = strips[1:2] if h == heads - 1 else []
        p = total(split_up[h][0], away[h], [att] + pull + more)
        for b in order[h][1:-1]:
            p = total(p, swap(p, b), [])
        pull.append(p)
        far.append(swap(p, order[h][-1]))
        att = attend([p])
    while len(pieces) < per_head * heads:
        att = attend([att])
    both = [x for h in range(heads) for x in (pull[h], far[h])]
    new = renorm(ids, tokens_all, fast_weights, both, [att] + strips[:1])

    cut = rows // 2
    merged, rest, weights = [], [], None
    for h in range(heads):
        b = order[h][0]
        near = swap(new[h], b)
        blocks = [new[h], near, swap(new[h], 1), swap(near, 1)]
        own = pieces[h * per_head : (h + 1) * per_head]
        m, r, weights = apply(h, heads, ids, query, own, blocks, cut, weights, strips[2:] if h else [])
        merged.append(m)
        rest.append(r)
    to_right = [[shift(m, "head", 1) for m in merged]]
    to_left = [[shift(m, "head", -1) for m in merged]]

    near = stack([s[None] for s in strips], [merged[-1]])
    partial = partials(rest, out_weight, groups, [near])
    near = near.reshape((1,) + near.shape)
    after = near
    x = None
    for t in range(1, groups):
        right, left = [], []
        for h in range(heads):
            r, l, x = ring_step(
                t,
                groups,
                ids,
                step_at[t],
                tail_at,
                h,
                to_right[t - 1][h],
                to_left[t - 1][h],
                partial,
                x,
                [after],
            )
            after = l
            right.append(shift(r, "head", 1))
            left.append(shift(l, "head", -1))
            due = {(1, heads - 1): spread[:1], (groups - 1, heads - 1): spread[1:-1]}
            for b in due.get((t, h), []):
                near = stack([near, swap(near, b)], [after])
        to_right.append(right)
        to_left.append(left)
    out = gathered(
        ids,
        tail_at,
        merged,
        x,
        out_weight,
        near,
        swap(near, 1),
        rows,
        [after],
    )
    for h in range(heads):
        out = finish(ids, tail_at, h, to_right[-1][h], to_left[-1][h], partial, out)
    return (out, weights)


def solution(mesh):
    placed = (
        P("ctx", "head"),
        P("ctx", "head"),
        P("ctx", "head"),
        P("ctx", "head"),
        P("head", None, None, None),
        P("head", None),
    )
    return jax.shard_map(
        shards,
        mesh=mesh,
        in_specs=placed,
        out_specs=(P("ctx", "head"), P("head", None, None, None)),
        check_vma=False,
    )
```

```python
import functools
import math

import jax
import jax.numpy as jnp
from jax import lax
from jax.experimental import pallas as pl
from jax.experimental.pallas import tpu as pltpu
from jax.sharding import PartitionSpec as P

FW = 512
HEAD_DIM = 128
WINDOW = 256
LANES = 128
PER = FW // LANES
BLOCKS = 3 * PER
HALF = BLOCKS // 2
THIRD = BLOCKS // 4
TAIL = 16

base_rate = 0.05
BF = jnp.bfloat16
F32 = jnp.float32
NT = (((1,), (1,)), ((), ()))

CORE, FIRST, NEAR = 0, 1, 2

ANY = pl.BlockSpec(memory_space=pl.ANY)
SMEM = pl.BlockSpec(memory_space=pltpu.SMEM)


def room(mib):
    return pltpu.CompilerParams(vmem_limit_bytes=mib * 2**20)


def mm(a, b):
    return jnp.dot(a, b, preferred_element_type=F32)


def shift(block, axis, distance):
    n = lax.axis_size(axis)
    return lax.ppermute(block, axis, [(i, i + distance) for i in range(n) if 0 <= i + distance < n])


def rotate(block, axis, distance):
    n = lax.axis_size(axis)
    return lax.ppermute(block, axis, [(i, (i + distance) % n) for i in range(n)])


def swap(block, bit):
    n = lax.axis_size("ctx")
    return lax.ppermute(block, "ctx", [(i, i ^ bit) for i in range(n)])


def sigmoid(x):
    return 0.5 * jnp.tanh(0.5 * x) + 0.5


def full(shape):
    return pl.BlockSpec(shape, lambda *_: (0,) * len(shape))


def cost(microseconds):
    return pl.CostEstimate(
        flops=int(microseconds * 0.12e9), bytes_accessed=0, transcendentals=0
    )


def strip_copy(ids_ref, at, w_hbm, o_ref, sem):
    share, width = o_ref.shape
    rows = pl.ds(pl.multiple_of(ids_ref[at] * share, share), share)
    cols = pl.ds(pl.multiple_of(ids_ref[at + 1] * width, width), width)
    return pltpu.make_async_copy(w_hbm.at[rows, cols], o_ref, sem)


def split_rows(x):
    hi = x.astype(BF).astype(F32)
    mid = (x - hi).astype(BF).astype(F32)
    lo = x - hi - mid
    row = lax.broadcasted_iota(jnp.int32, (TAIL, LANES), 0)
    return jnp.where(row == 0, hi, jnp.where(row == 1, mid, jnp.where(row == 2, lo, 0.0))).astype(BF)


def join_rows(tail):
    return jnp.sum(tail.astype(F32), axis=0, keepdims=True)


def grads_kernel(h, at, ids_ref, code_ref, k_ref, v_ref, w_ref, *refs):
    lhs, rhs, sem = refs[-3:]
    copies = []
    if h == 0:
        k_hbm, v_hbm, ow_hbm, keep_ref, send_ref, rim_ref = refs[:6]
        last = pl.ds(k_hbm.shape[0] - WINDOW, WINDOW)
        copies = [
            pltpu.make_async_copy(k_hbm.at[last, :], rim_ref.at[pl.ds(0, WINDOW), :], sem.at[0]),
            pltpu.make_async_copy(
                v_hbm.at[last, :], rim_ref.at[pl.ds(WINDOW, WINDOW), :], sem.at[1]
            ),
        ] + [
            strip_copy(ids_ref, at + 2 * i, ow_hbm, strip_ref, sem.at[2 + i])
            for i, strip_ref in enumerate(refs[6:-3])
        ]
    else:
        keep_ref, send_ref = refs[-5:-3]
    for copy in copies:
        copy.start()
    rows = k_ref.shape[0]
    tile = min(256, rows)
    wide = 2 * LANES
    codes = code_ref[h : h + 1, :].astype(F32) * 2.0 ** (-14)
    for t in range(rows // tile):
        sl = pl.ds(t * tile, tile)
        k = k_ref[sl, :]
        rate = jnp.broadcast_to(codes[:, t * tile : (t + 1) * tile], (LANES, tile)).T
        rate = jnp.concatenate([rate] * PER, axis=1)
        push = (rate * v_ref[sl, :].astype(F32)).astype(BF)
        rhs[sl, 2 * FW :] = push
        for j in range(FW // wide):
            cs = slice(j * wide, (j + 1) * wide)
            gate = mm(k, w_ref[0, 0, :, cs])
            up = mm(k, w_ref[0, 1, :, cs])
            back = lax.dot_general(push, w_ref[0, 2, cs, :], NT, preferred_element_type=F32)
            s = sigmoid(gate)
            gs = gate * s
            lhs[FW + j * wide : FW + (j + 1) * wide, sl] = (gs * up).astype(BF).T
            rhs[sl, cs] = (back * up * (s + gs * (1.0 - s))).astype(BF)
            rhs[sl, FW + j * wide : FW + (j + 1) * wide] = (back * gs).astype(BF)
    lhs[:FW, :] = k_ref[...].T
    tail = split_rows(jnp.broadcast_to(jnp.sum(codes, axis=1, keepdims=True), (1, LANES)))
    pairs = HALF // 2
    for ref, half in ((send_ref, 1 - ids_ref[CORE]), (keep_ref, ids_ref[CORE])):
        ref[pl.ds(HALF * FW, TAIL), :] = tail
        for i in range(pairs):
            pair = half * pairs + i
            left = (pair >= 2 * FW // wide).astype(jnp.int32) * FW
            left = lhs[pl.ds(pl.multiple_of(left, FW), FW), :]
            right = rhs[:, pl.ds(pl.multiple_of(pair * wide, wide), wide)]
            r = mm(left, right).astype(BF)
            ref[pl.ds(2 * i * FW, FW), :] = r[:, :LANES]
            ref[pl.ds((2 * i + 1) * FW, FW), :] = r[:, LANES:]
    for copy in copies:
        copy.wait()


def grads(h, at, ids, codes, keys, values, fast_weights, out_weight, strips, after):
    rows, feats = keys.shape
    shape = (HALF * FW + TAIL, LANES)
    outs = [shape, shape] + ([(2 * WINDOW, feats)] + strips if h == 0 else [])
    more = [keys, values, out_weight] if h == 0 else after
    col = pl.BlockSpec((rows, FW), lambda i: (0, h))
    return pl.pallas_call(
        functools.partial(grads_kernel, h, at),
        grid=(1,),
        in_specs=[
            SMEM,
            full(codes.shape),
            col,
            col,
            pl.BlockSpec((1, 3, FW, FW), lambda i: (h, 0, 0, 0)),
        ]
        + [ANY] * len(more),
        out_specs=[full(x) for x in outs],
        out_shape=[jax.ShapeDtypeStruct(x, BF) for x in outs],
        scratch_shapes=[
            pltpu.VMEM((2 * FW, rows), BF),
            pltpu.VMEM((rows, 3 * FW), BF),
            pltpu.SemaphoreType.DMA((2 + len(strips),)),
        ],
        compiler_params=room(58),
        cost_estimate=cost(8 * rows / 1024),
    )(ids, codes, keys, values, fast_weights, *more)


def fetch(refs, scratch, sem):
    copies = [pltpu.make_async_copy(r, scratch.at[i], sem.at[i]) for i, r in enumerate(refs)]
    for c in copies:
        c.start()
    for c in copies:
        c.wait()


def pair(x):
    return [pltpu.VMEM((2,) + x.shape, x.dtype), pltpu.SemaphoreType.DMA((2,))]


def split_kernel(h, ids_ref, keep_hbm, other_hbm, *refs):
    keep_out, send_out, both, sem = refs[-4:]
    fetch((keep_hbm, other_hbm), both, sem)
    keep_ref, other_ref = both.at[0], both.at[1]
    n = THIRD * FW
    bit = ids_ref[NEAR + h]
    mine = pl.ds(pl.multiple_of(bit * n, n), n)
    theirs = pl.ds(pl.multiple_of((1 - bit) * n, n), n)
    keep_out[pl.ds(0, n), :] = keep_ref[mine, :] + other_ref[mine, :]
    send_out[pl.ds(0, n), :] = keep_ref[theirs, :] + other_ref[theirs, :]
    tail = pl.ds(HALF * FW, TAIL)
    rate = split_rows(join_rows(keep_ref[tail, :]) + join_rows(other_ref[tail, :]))
    keep_out[pl.ds(n, TAIL), :] = rate
    send_out[pl.ds(n, TAIL), :] = rate


def split(h, ids, keep, other, after):
    shape = (THIRD * FW + TAIL, LANES)
    out = jax.ShapeDtypeStruct(shape, BF)
    return pl.pallas_call(
        functools.partial(split_kernel, h),
        grid=(1,),
        in_specs=[SMEM] + [ANY] * (2 + len(after)),
        out_specs=[full(shape), full(shape)],
        out_shape=[out, out],
        scratch_shapes=pair(keep),
        compiler_params=room(12),
        cost_estimate=cost(0.9),
    )(ids, keep, other, *after)


def total_kernel(a_hbm, b_hbm, *rest):
    o_ref, both, sem = rest[-3:]
    fetch((a_hbm, b_hbm), both, sem)
    a_ref, b_ref = both.at[0], both.at[1]
    n = THIRD * FW
    o_ref[pl.ds(0, n), :] = a_ref[pl.ds(0, n), :] + b_ref[pl.ds(0, n), :]
    tail = pl.ds(n, TAIL)
    o_ref[tail, :] = split_rows(join_rows(a_ref[tail, :]) + join_rows(b_ref[tail, :]))


def total(a, b, after):
    return pl.pallas_call(
        total_kernel,
        grid=(1,),
        in_specs=[ANY] * (2 + len(after)),
        out_specs=full(a.shape),
        out_shape=jax.ShapeDtypeStruct(a.shape, BF),
        scratch_shapes=pair(a),
        compiler_params=room(8),
        cost_estimate=cost(0.5),
    )(a, b, *after)


def renorm_kernel(heads, tokens_all, ids_ref, base_ref, *refs):
    outs, (both, sem) = refs[-2 - heads : -2], refs[-2:]
    fetch(refs[: 2 * heads], both, sem)
    tail = pl.ds(THIRD * FW, TAIL)
    for h in range(heads):
        a_ref, b_ref = both.at[2 * h], both.at[2 * h + 1]
        start = ids_ref[CORE] * HALF + ids_ref[NEAR + h] * THIRD
        rate_sum = join_rows(a_ref[tail, :]) + join_rows(b_ref[tail, :])
        step = base_rate / (math.sqrt(tokens_all) * (rate_sum / tokens_all))
        for i in range(THIRD):
            sl = pl.ds(i * FW, FW)
            pull = a_ref[sl, :].astype(F32) + b_ref[sl, :].astype(F32)
            at = start + i
            col = pl.ds(pl.multiple_of((at % PER) * LANES, LANES), LANES)
            base = base_ref[h, at // PER, :, col].astype(F32)
            updated = base + step * pull
            old = jnp.sqrt(jnp.sum(base * base, axis=0, keepdims=True) + 1e-06)
            new = jnp.sqrt(jnp.sum(updated * updated, axis=0, keepdims=True) + 1e-06)
            outs[h][i] = (updated * (old / new)).astype(BF)


def renorm(ids, tokens_all, fast_weights, pulls, after):
    heads, one = fast_weights.shape[0], pulls[0].shape
    shape = (THIRD, FW, LANES)
    return pl.pallas_call(
        functools.partial(renorm_kernel, heads, tokens_all),
        grid=(1,),
        in_specs=[SMEM, full(fast_weights.shape)] + [ANY] * (len(pulls) + len(after)),
        out_specs=[full(shape)] * heads,
        out_shape=[jax.ShapeDtypeStruct(shape, BF)] * heads,
        scratch_shapes=[
            pltpu.VMEM((2 * heads,) + one, BF),
            pltpu.SemaphoreType.DMA((2 * heads,)),
        ],
        compiler_params=room(24),
        cost_estimate=cost(2.1),
    )(ids, fast_weights, *pulls, *after)


def attn_kernel(ids_ref, q_ref, k_ref, v_ref, rim_ref, *rest):
    o_ref = rest[-1]
    rows = q_ref.shape[0]
    w, d = WINDOW, HEAD_DIM
    row = lax.broadcasted_iota(jnp.int32, (w, w), 0)
    col = lax.broadcasted_iota(jnp.int32, (w, w), 1)
    own = col <= row
    factor = math.log2(math.e) / math.sqrt(d)
    has_prev = ids_ref[FIRST] == 0
    ones = jnp.ones((2 * w, LANES), BF)
    for h in range(q_ref.shape[1] // d):
        cs = slice(h * d, (h + 1) * d)
        for b in range(rows // w):
            sl = pl.ds(b * w, w)
            if b == 0:
                k2 = jnp.concatenate([rim_ref[:w, cs], k_ref[sl, cs]], axis=0)
                v2 = jnp.concatenate([rim_ref[w:, cs], v_ref[sl, cs]], axis=0)
            else:
                both = pl.ds((b - 1) * w, 2 * w)
                k2, v2 = k_ref[both, cs], v_ref[both, cs]
            s2 = lax.dot_general(q_ref[sl, cs], k2, NT, preferred_element_type=F32)
            prev = s2[:, :w]
            if b == 0:
                prev = jnp.where(has_prev, prev, -1e30)
            s = jnp.where(own, s2[:, w:], prev)
            e = jnp.exp2((s - jnp.max(s, axis=1, keepdims=True)) * factor).astype(BF)
            zero = jnp.zeros_like(e)
            e2 = jnp.concatenate([jnp.where(own, zero, e), jnp.where(own, e, zero)], axis=1)
            o = mm(e2, jnp.concatenate([v2, ones], axis=1))
            o_ref[sl, cs] = (o[:, :d] / o[:, d:]).astype(o_ref.dtype)


def attention(piece, width, ids, query, keys, values, rim, after):
    rows = query.shape[0]
    col = pl.BlockSpec((rows, width), lambda i: (0, piece))
    of_rim = pl.BlockSpec((2 * WINDOW, width), lambda i: (0, piece))
    return pl.pallas_call(
        attn_kernel,
        grid=(1,),
        in_specs=[SMEM, col, col, col, of_rim] + [ANY] * len(after),
        out_specs=full((rows, width)),
        out_shape=jax.ShapeDtypeStruct((rows, width), BF),
        compiler_params=room(16),
        cost_estimate=cost(2.1 * rows * width / 2**18),
    )(ids, query, keys, values, rim, *after)


def apply_tile(q, att, weights, act):
    wide = 2 * LANES
    rows = q.shape[0]
    for j in range(FW // wide):
        cs = slice(j * wide, (j + 1) * wide)
        gate = mm(q, weights[0, :, cs])
        up = mm(q, weights[1, :, cs])
        act[:rows, cs] = (gate * sigmoid(gate) * up).astype(BF)
    y = mm(act[:rows, :], weights[2])
    y = y * lax.rsqrt(jnp.mean(y * y, axis=1, keepdims=True) + 1e-06)
    return (att.astype(F32) + y).astype(BF)


def apply_kernel(h, pieces, ids_ref, q_hbm, *refs):
    att_hbm, refs = refs[:pieces], refs[pieces:]
    blocks = refs[:4]
    lo_ref, hi_ref, nw_hbm, q, att, nw, act, sem, bsem, osem = refs[-10:]
    rows = q.shape[0]
    core, near = ids_ref[CORE], ids_ref[NEAR + h]
    copies = [pltpu.make_async_copy(q_hbm.at[:, pl.ds(h * FW, FW)], q, sem.at[0])]
    for i, a in enumerate(att_hbm):
        to = att.at[:, pl.ds(i * a.shape[1], a.shape[1])]
        copies.append(pltpu.make_async_copy(a, to, sem.at[1 + i]))
    for n, src in enumerate(blocks):
        half, third = core ^ (n // 2), near ^ (n % 2)
        for i in range(THIRD):
            b = half * HALF + third * THIRD + i
            col = pl.ds(pl.multiple_of((b % PER) * LANES, LANES), LANES)
            dst = nw.at[b // PER, :, col]
            copies.append(pltpu.make_async_copy(src.at[i], dst, bsem.at[n, i]))
    for c in copies:
        c.start()
    for c in copies:
        c.wait()
    out = pltpu.make_async_copy(nw, nw_hbm.at[h], osem)
    out.start()
    cut = lo_ref.shape[0]
    for ref, start in ((lo_ref, 0), (hi_ref, cut)):
        sl = pl.ds(start, ref.shape[0])
        ref[...] = apply_tile(q[sl, :], att[sl, :], nw, act)
    out.wait()


def apply(h, heads, ids, query, attended, blocks, cut, whole, after):
    rows, pieces = query.shape[0], len(attended)
    shape = (heads, 3, FW, FW)
    extra = ([] if whole is None else [whole]) + after
    alias = {} if whole is None else {2 + pieces + len(blocks): 2}
    sizes = [(cut, FW), (rows - cut, FW)]
    return pl.pallas_call(
        functools.partial(apply_kernel, h, pieces),
        grid=(1,),
        in_specs=[SMEM] + [ANY] * (1 + pieces + len(blocks) + len(extra)),
        out_specs=[full(x) for x in sizes] + [ANY],
        out_shape=[jax.ShapeDtypeStruct(x, BF) for x in sizes + [shape]],
        input_output_aliases=alias,
        scratch_shapes=[
            pltpu.VMEM((rows, FW), BF),
            pltpu.VMEM((rows, FW), BF),
            pltpu.VMEM((3, FW, FW), BF),
            pltpu.VMEM((max(cut, rows - cut), FW), BF),
            pltpu.SemaphoreType.DMA((1 + pieces,)),
            pltpu.SemaphoreType.DMA((4, THIRD)),
            pltpu.SemaphoreType.DMA,
        ],
        compiler_params=room(20),
        cost_estimate=cost(3.3 * rows / 1024),
    )(ids, query, *attended, *blocks, *extra)


def joined(refs):
    return jnp.concatenate([r[...] for r in refs], axis=1)


def partial_kernel(heads, *refs):
    x_refs, w_ref = refs[:heads], refs[heads]
    o_ref, x = refs[-2:]

    @pl.when(pl.program_id(0) == 0)
    def _():
        for h in range(heads):
            x[:, h * FW : (h + 1) * FW] = x_refs[h][...]

    o_ref[0] = mm(x[...], w_ref[...]).astype(BF)


def partials(merged, out_weight, groups, after):
    rows, heads = merged[0].shape[0], len(merged)
    feats, width = out_weight.shape[0], out_weight.shape[1] // groups
    return pl.pallas_call(
        functools.partial(partial_kernel, heads),
        grid=(groups,),
        in_specs=[full(m.shape) for m in merged]
        + [pl.BlockSpec((feats, width), lambda d: (0, d))]
        + [ANY] * len(after),
        out_specs=pl.BlockSpec((1, rows, width), lambda d: (d, 0, 0)),
        out_shape=jax.ShapeDtypeStruct((groups, rows, width), BF),
        scratch_shapes=[pltpu.VMEM((rows, feats), BF)],
        compiler_params=room(24),
        cost_estimate=cost(1 * rows / 512),
    )(*merged, out_weight, *after)


def stack_kernel(n, *refs):
    o_ref = refs[-1]
    at = 0
    for r in refs[:n]:
        o_ref[pl.ds(at, r.shape[0])] = r[...]
        at += r.shape[0]


def stack(parts, after):
    shape = (sum(p.shape[0] for p in parts),) + parts[0].shape[1:]
    return pl.pallas_call(
        functools.partial(stack_kernel, len(parts)),
        grid=(1,),
        in_specs=[full(p.shape) for p in parts] + [ANY] * len(after),
        out_specs=full(shape),
        out_shape=jax.ShapeDtypeStruct(shape, BF),
        compiler_params=room(20),
        cost_estimate=cost(0.1),
    )(*parts, *after)


def ring_kernel(t, n, at, tail, wave, ids_ref, right_hbm, left_hbm, p_hbm, *refs):
    ro_ref, lo_ref, x_hbm, got, own, sem, xsem = refs[-7:]
    width = right_hbm.shape[1]
    cols = pl.ds(wave * width, width)
    copies = [
        pltpu.make_async_copy(right_hbm, got.at[0], sem.at[0]),
        pltpu.make_async_copy(p_hbm.at[ids_ref[at], :, cols], own.at[0], sem.at[1]),
        pltpu.make_async_copy(left_hbm, got.at[1], sem.at[2]),
        pltpu.make_async_copy(p_hbm.at[ids_ref[at + 1], :, cols], own.at[1], sem.at[3]),
    ]
    for c in copies:
        c.start()
    zero = jnp.zeros((), BF)
    for i, ref in enumerate((ro_ref, lo_ref)):
        copies[2 * i].wait()
        copies[2 * i + 1].wait()
        ref[...] = got[i] + jnp.where(ids_ref[at + 2 + i] > 0, own[i], zero)
    for i, (slot, here) in enumerate(((t - 1, t <= ids_ref[tail]), (n - 1 - t, t < n - ids_ref[tail]))):

        @pl.when(here)
        def _():
            keep = pltpu.make_async_copy(got.at[i], x_hbm.at[slot, :, cols], xsem.at[i])
            keep.start()
            keep.wait()


def ring_step(t, n, ids, at, tail, wave, right, left, partial, x, after):
    out = jax.ShapeDtypeStruct(right.shape, BF)
    kept = jax.ShapeDtypeStruct((n - 1, right.shape[0], partial.shape[2]), BF)
    more = ([] if x is None else [x]) + after
    return pl.pallas_call(
        functools.partial(ring_kernel, t, n, at, tail, wave),
        grid=(1,),
        in_specs=[SMEM] + [ANY] * (3 + len(more)),
        out_specs=[full(right.shape)] * 2 + [ANY],
        out_shape=[out, out, kept],
        input_output_aliases={} if x is None else {4: 2},
        scratch_shapes=[
            pltpu.VMEM((2,) + right.shape, BF),
            pltpu.VMEM((2,) + right.shape, BF),
            pltpu.SemaphoreType.DMA((4,)),
            pltpu.SemaphoreType.DMA((2,)),
        ],
        compiler_params=room(12),
        cost_estimate=cost(30),
    )(ids, right, left, partial, *more)


def gathered_kernel(n, heads, parts, at, ids_ref, *refs):
    own_refs, refs = refs[:heads], refs[heads:]
    x_hbm, refs = refs[0], refs[1:]
    w_ref, near_ref, far_ref = refs[:3]
    o_ref, x, cols, acc, xsem, wsem = refs[-6:]
    share = near_ref.shape[2]
    near = near_ref.shape[0]

    def each(steps, do):
        for t in steps:
            do(t, pltpu.make_async_copy(x_hbm.at[t], x.at[t], xsem.at[t]))
            for p in range(parts):
                src = near_ref.at[p, t] if p < near else far_ref.at[p - near, t]
                to = ids_ref[at + 1 + p] * share
                to = pl.ds(pl.multiple_of(to, share), share)
                do(t, pltpu.make_async_copy(src, cols.at[t, to, :], wsem.at[t, p]))

    each(range(n - 1), lambda t, c: c.start())
    acc[...] = mm(joined(own_refs), w_ref[...])
    for t in range(n - 1):
        each((t,), lambda t, c: c.wait())
        if t < n - 2:
            acc[...] += mm(x[t], cols[t])
        else:
            o_ref[...] = (acc[...] + mm(x[t], cols[t])).astype(BF)


def gathered(ids, at, merged, x, out_weight, near, far, rows_all, after):
    n, heads, parts = x.shape[0] + 1, len(merged), near.shape[0] + far.shape[0]
    rows, feats = merged[0].shape[0], out_weight.shape[0]
    width = out_weight.shape[1] // n
    return pl.pallas_call(
        functools.partial(gathered_kernel, n, heads, parts, at),
        grid_spec=pltpu.PrefetchScalarGridSpec(
            num_scalar_prefetch=1,
            grid=(1,),
            in_specs=[full(m.shape) for m in merged]
            + [ANY]
            + [pl.BlockSpec((feats, width), lambda i, s: (0, s[at])), ANY, ANY]
            + [ANY] * len(after),
            out_specs=pl.BlockSpec((rows, width), lambda i, s: (0, 0)),
            scratch_shapes=[
                pltpu.VMEM((n - 1, rows, feats), BF),
                pltpu.VMEM((n - 1, feats, width), BF),
                pltpu.VMEM((rows, width), F32),
                pltpu.SemaphoreType.DMA((n - 1,)),
                pltpu.SemaphoreType.DMA((n - 1, parts)),
            ],
        ),
        out_shape=jax.ShapeDtypeStruct((rows_all, width), BF),
        compiler_params=room(48),
        cost_estimate=cost(9 * rows / 512),
    )(
        ids, *merged, x, out_weight, near, far, *after
    )


def finish_kernel(at, wave, ids_ref, right_hbm, left_hbm, p_hbm, out_in, o_hbm, got, own, sem):
    del out_in
    rows, width = own.shape
    cols = pl.ds(wave * width, width)
    copies = [
        pltpu.make_async_copy(right_hbm, got.at[0], sem.at[0]),
        pltpu.make_async_copy(left_hbm, got.at[1], sem.at[1]),
        pltpu.make_async_copy(p_hbm.at[ids_ref[at], :, cols], own, sem.at[2]),
    ]
    for c in copies:
        c.start()
    for c in copies:
        c.wait()
    total = own[...].astype(F32) + (got[0].astype(F32) + got[1].astype(F32))
    own[...] = total.astype(BF)
    last = pl.ds(o_hbm.shape[0] - rows, rows)
    out = pltpu.make_async_copy(own, o_hbm.at[last, cols], sem.at[3])
    out.start()
    out.wait()


def finish(ids, at, wave, right, left, partial, out):
    return pl.pallas_call(
        functools.partial(finish_kernel, at, wave),
        grid=(1,),
        in_specs=[SMEM] + [ANY] * 4,
        out_specs=ANY,
        out_shape=jax.ShapeDtypeStruct(out.shape, BF),
        input_output_aliases={4: 0},
        scratch_shapes=[
            pltpu.VMEM((2,) + right.shape, BF),
            pltpu.VMEM(right.shape, BF),
            pltpu.SemaphoreType.DMA((4,)),
        ],
        compiler_params=room(12),
        cost_estimate=cost(30),
    )(ids, right, left, partial, out)


def scalars(*xs):
    return jnp.stack([jnp.asarray(x, jnp.int32) for x in xs])


def shards(query, keys, values, lr_code, fast_weights, out_weight):
    rows, feats = query.shape
    contexts, groups = lax.axis_size("ctx"), lax.axis_size("head")
    c, z = lax.axis_index("ctx"), lax.axis_index("head")
    tokens_all = rows * contexts
    heads = fast_weights.shape[0]
    bits = [1 << i for i in range(contexts.bit_length() - 1)]
    bit_of = {b: (c // b) % 2 for b in bits}
    order = [[bits[1 + h % 2]] for h in range(heads)]
    order = [o + [b for b in bits[1:] if b != o[0]] for o in order]
    spread = bits[2::-1]
    places = [0]
    for b in spread:
        places = places + [p ^ b for p in places]
    share, width = feats // len(places), out_weight.shape[1] // groups
    ids = [bit_of[1], c == 0] + [bit_of[o[0]] for o in order]
    step_at = [len(ids) + 4 * (t - 1) for t in range(groups)]
    for t in range(1, groups):
        ids += [(z - t) % groups, (z + t) % groups, t > z, t > groups - 1 - z]
    tail_at = len(ids)
    ids += [z] + [(c % len(places)) ^ p for p in places]
    strip_at = len(ids)
    for s in range(1, groups):
        ids += [c % len(places), (z + s) % groups]
    ids = scalars(*ids)

    keep, other = [], []
    for h in range(heads):
        g = grads(
            h,
            strip_at,
            ids,
            lr_code.T,
            keys,
            values,
            fast_weights,
            out_weight,
            [(share, width)] * (groups - 1),
            keep[-1:],
        )
        keep.append(g[0])
        other.append(swap(g[1], 1))
        if h == 0:
            rim = shift(g[2], "ctx", 1)
            strips = [rotate(x, "head", s + 1) for s, x in enumerate(g[3:])]
    split_up = []
    for h in range(heads):
        before = [split_up[0][1], rim] if h else []
        split_up.append(split(h, ids, keep[h], other[h], before))
    away = [swap(split_up[h][1], order[h][0]) for h in range(heads)]

    per_head = 2
    pieces = []

    def attend(after):
        i = len(pieces)
        pieces.append(attention(i, FW // per_head, ids, query, keys, values, rim, after))
        return pieces[-1]

    att = attend([s[1] for s in split_up] + strips[1:2])
    pull, far = [], []
    for h in range(heads):
        p = total(split_up[h][0], away[h], [att] + pull)
        for b in order[h][1:-1]:
            p = total(p, swap(p, b), [])
        pull.append(p)
        far.append(swap(p, order[h][-1]))
        att = attend([p] + (strips[:1] if h == heads - 1 else []))
    while len(pieces) < per_head * heads:
        att = attend([att])
    both = [x for h in range(heads) for x in (pull[h], far[h])]
    new = renorm(ids, tokens_all, fast_weights, both, [att] + strips[2:])

    cut = rows // 2
    merged, rest, weights = [], [], None
    for h in range(heads):
        b = order[h][0]
        near = swap(new[h], b)
        blocks = [new[h], near, swap(new[h], 1), swap(near, 1)]
        own = pieces[h * per_head : (h + 1) * per_head]
        m, r, weights = apply(h, heads, ids, query, own, blocks, cut, weights, [])
        merged.append(m)
        rest.append(r)
    to_right = [[shift(m, "head", 1) for m in merged]]
    to_left = [[shift(m, "head", -1) for m in merged]]

    near = stack([s[None] for s in strips], [merged[-1]])
    partial = partials(rest, out_weight, groups, [near])
    near = near.reshape((1,) + near.shape)
    after = near
    x = None
    for t in range(1, groups):
        right, left = [], []
        for h in range(heads):
            r, l, x = ring_step(
                t,
                groups,
                ids,
                step_at[t],
                tail_at,
                h,
                to_right[t - 1][h],
                to_left[t - 1][h],
                partial,
                x,
                [after],
            )
            after = l
            right.append(shift(r, "head", 1))
            left.append(shift(l, "head", -1))
            due = {(1, heads - 1): spread[:1], (groups - 1, heads - 1): spread[1:-1]}
            for b in due.get((t, h), []):
                near = stack([near, swap(near, b)], [after])
        to_right.append(right)
        to_left.append(left)
    out = gathered(
        ids,
        tail_at,
        merged,
        x,
        out_weight,
        near,
        swap(near, 1),
        rows,
        [after],
    )
    for h in range(heads):
        out = finish(ids, tail_at, h, to_right[-1][h], to_left[-1][h], partial, out)
    return (out, weights)


def solution(mesh):
    placed = (
        P("ctx", "head"),
        P("ctx", "head"),
        P("ctx", "head"),
        P("ctx", "head"),
        P("head", None, None, None),
        P("head", None),
    )
    return jax.shard_map(
        shards,
        mesh=mesh,
        in_specs=placed,
        out_specs=(P("ctx", "head"), P("head", None, None, None)),
        check_vma=False,
    )
```

```python
import functools
import math

import jax
import jax.numpy as jnp
from jax import lax
from jax.experimental import pallas as pl
from jax.experimental.pallas import tpu as pltpu
from jax.sharding import PartitionSpec as P

FW = 512
HEAD_DIM = 128
WINDOW = 256
LANES = 128
PER = FW // LANES
BLOCKS = 3 * PER
HALF = BLOCKS // 2
THIRD = BLOCKS // 4
TAIL = 16

base_rate = 0.05
BF = jnp.bfloat16
F32 = jnp.float32
NT = (((1,), (1,)), ((), ()))

CORE, FIRST, NEAR = 0, 1, 2

ANY = pl.BlockSpec(memory_space=pl.ANY)
SMEM = pl.BlockSpec(memory_space=pltpu.SMEM)


def room(mib):
    return pltpu.CompilerParams(vmem_limit_bytes=mib * 2**20)


def mm(a, b):
    return jnp.dot(a, b, preferred_element_type=F32)


def shift(block, axis, distance):
    n = lax.axis_size(axis)
    return lax.ppermute(block, axis, [(i, i + distance) for i in range(n) if 0 <= i + distance < n])


def rotate(block, axis, distance):
    n = lax.axis_size(axis)
    return lax.ppermute(block, axis, [(i, (i + distance) % n) for i in range(n)])


def swap(block, bit):
    n = lax.axis_size("ctx")
    return lax.ppermute(block, "ctx", [(i, i ^ bit) for i in range(n)])


def sigmoid(x):
    return 0.5 * jnp.tanh(0.5 * x) + 0.5


def full(shape):
    return pl.BlockSpec(shape, lambda *_: (0,) * len(shape))


def cost(microseconds):
    return pl.CostEstimate(
        flops=int(microseconds * 0.12e9), bytes_accessed=0, transcendentals=0
    )


def strip_copy(ids_ref, at, w_hbm, o_ref, sem):
    share, width = o_ref.shape
    rows = pl.ds(pl.multiple_of(ids_ref[at] * share, share), share)
    cols = pl.ds(pl.multiple_of(ids_ref[at + 1] * width, width), width)
    return pltpu.make_async_copy(w_hbm.at[rows, cols], o_ref, sem)


def split_rows(x):
    hi = x.astype(BF).astype(F32)
    mid = (x - hi).astype(BF).astype(F32)
    lo = x - hi - mid
    row = lax.broadcasted_iota(jnp.int32, (TAIL, LANES), 0)
    return jnp.where(row == 0, hi, jnp.where(row == 1, mid, jnp.where(row == 2, lo, 0.0))).astype(BF)


def join_rows(tail):
    return jnp.sum(tail.astype(F32), axis=0, keepdims=True)


def grads_kernel(h, at, ids_ref, code_ref, k_ref, v_ref, w_ref, *refs):
    lhs, rhs, sem = refs[-3:]
    copies = []
    if h == 0:
        k_hbm, v_hbm, ow_hbm, keep_ref, send_ref, rim_ref = refs[:6]
        last = pl.ds(k_hbm.shape[0] - WINDOW, WINDOW)
        copies = [
            pltpu.make_async_copy(k_hbm.at[last, :], rim_ref.at[pl.ds(0, WINDOW), :], sem.at[0]),
            pltpu.make_async_copy(
                v_hbm.at[last, :], rim_ref.at[pl.ds(WINDOW, WINDOW), :], sem.at[1]
            ),
        ] + [
            strip_copy(ids_ref, at + 2 * i, ow_hbm, strip_ref, sem.at[2 + i])
            for i, strip_ref in enumerate(refs[6:-3])
        ]
    else:
        keep_ref, send_ref = refs[-5:-3]
    for copy in copies:
        copy.start()
    rows = k_ref.shape[0]
    tile = min(256, rows)
    wide = 2 * LANES
    codes = code_ref[h : h + 1, :].astype(F32) * 2.0 ** (-14)
    for t in range(rows // tile):
        sl = pl.ds(t * tile, tile)
        k = k_ref[sl, :]
        rate = jnp.broadcast_to(codes[:, t * tile : (t + 1) * tile], (LANES, tile)).T
        rate = jnp.concatenate([rate] * PER, axis=1)
        push = (rate * v_ref[sl, :].astype(F32)).astype(BF)
        rhs[sl, 2 * FW :] = push
        for j in range(FW // wide):
            cs = slice(j * wide, (j + 1) * wide)
            gate = mm(k, w_ref[0, 0, :, cs])
            up = mm(k, w_ref[0, 1, :, cs])
            back = lax.dot_general(push, w_ref[0, 2, cs, :], NT, preferred_element_type=F32)
            s = sigmoid(gate)
            gs = gate * s
            lhs[FW + j * wide : FW + (j + 1) * wide, sl] = (gs * up).astype(BF).T
            rhs[sl, cs] = (back * up * (s + gs * (1.0 - s))).astype(BF)
            rhs[sl, FW + j * wide : FW + (j + 1) * wide] = (back * gs).astype(BF)
    lhs[:FW, :] = k_ref[...].T
    tail = split_rows(jnp.broadcast_to(jnp.sum(codes, axis=1, keepdims=True), (1, LANES)))
    pairs = HALF // 2
    for ref, half in ((send_ref, 1 - ids_ref[CORE]), (keep_ref, ids_ref[CORE])):
        ref[pl.ds(HALF * FW, TAIL), :] = tail
        for i in range(pairs):
            pair = half * pairs + i
            left = (pair >= 2 * FW // wide).astype(jnp.int32) * FW
            left = lhs[pl.ds(pl.multiple_of(left, FW), FW), :]
            right = rhs[:, pl.ds(pl.multiple_of(pair * wide, wide), wide)]
            r = mm(left, right).astype(BF)
            ref[pl.ds(2 * i * FW, FW), :] = r[:, :LANES]
            ref[pl.ds((2 * i + 1) * FW, FW), :] = r[:, LANES:]
    for copy in copies:
        copy.wait()


def grads(h, at, ids, codes, keys, values, fast_weights, out_weight, strips, after):
    rows, feats = keys.shape
    shape = (HALF * FW + TAIL, LANES)
    outs = [shape, shape] + ([(2 * WINDOW, feats)] + strips if h == 0 else [])
    more = [keys, values, out_weight] if h == 0 else after
    col = pl.BlockSpec((rows, FW), lambda i: (0, h))
    return pl.pallas_call(
        functools.partial(grads_kernel, h, at),
        grid=(1,),
        in_specs=[
            SMEM,
            full(codes.shape),
            col,
            col,
            pl.BlockSpec((1, 3, FW, FW), lambda i: (h, 0, 0, 0)),
        ]
        + [ANY] * len(more),
        out_specs=[full(x) for x in outs],
        out_shape=[jax.ShapeDtypeStruct(x, BF) for x in outs],
        scratch_shapes=[
            pltpu.VMEM((2 * FW, rows), BF),
            pltpu.VMEM((rows, 3 * FW), BF),
            pltpu.SemaphoreType.DMA((2 + len(strips),)),
        ],
        compiler_params=room(58),
        cost_estimate=cost(8 * rows / 1024),
    )(ids, codes, keys, values, fast_weights, *more)


def fetch(refs, scratch, sem):
    copies = [pltpu.make_async_copy(r, scratch.at[i], sem.at[i]) for i, r in enumerate(refs)]
    for c in copies:
        c.start()
    for c in copies:
        c.wait()


def pair(x):
    return [pltpu.VMEM((2,) + x.shape, x.dtype), pltpu.SemaphoreType.DMA((2,))]


def split_kernel(h, ids_ref, keep_hbm, other_hbm, *refs):
    keep_out, send_out, both, sem = refs[-4:]
    fetch((keep_hbm, other_hbm), both, sem)
    keep_ref, other_ref = both.at[0], both.at[1]
    n = THIRD * FW
    bit = ids_ref[NEAR + h]
    mine = pl.ds(pl.multiple_of(bit * n, n), n)
    theirs = pl.ds(pl.multiple_of((1 - bit) * n, n), n)
    keep_out[pl.ds(0, n), :] = keep_ref[mine, :] + other_ref[mine, :]
    send_out[pl.ds(0, n), :] = keep_ref[theirs, :] + other_ref[theirs, :]
    tail = pl.ds(HALF * FW, TAIL)
    rate = split_rows(join_rows(keep_ref[tail, :]) + join_rows(other_ref[tail, :]))
    keep_out[pl.ds(n, TAIL), :] = rate
    send_out[pl.ds(n, TAIL), :] = rate


def split(h, ids, keep, other, after):
    shape = (THIRD * FW + TAIL, LANES)
    out = jax.ShapeDtypeStruct(shape, BF)
    return pl.pallas_call(
        functools.partial(split_kernel, h),
        grid=(1,),
        in_specs=[SMEM] + [ANY] * (2 + len(after)),
        out_specs=[full(shape), full(shape)],
        out_shape=[out, out],
        scratch_shapes=pair(keep),
        compiler_params=room(12),
        cost_estimate=cost(0.9),
    )(ids, keep, other, *after)


def total_kernel(a_hbm, b_hbm, *rest):
    o_ref, both, sem = rest[-3:]
    fetch((a_hbm, b_hbm), both, sem)
    a_ref, b_ref = both.at[0], both.at[1]
    n = THIRD * FW
    o_ref[pl.ds(0, n), :] = a_ref[pl.ds(0, n), :] + b_ref[pl.ds(0, n), :]
    tail = pl.ds(n, TAIL)
    o_ref[tail, :] = split_rows(join_rows(a_ref[tail, :]) + join_rows(b_ref[tail, :]))


def total(a, b, after):
    return pl.pallas_call(
        total_kernel,
        grid=(1,),
        in_specs=[ANY] * (2 + len(after)),
        out_specs=full(a.shape),
        out_shape=jax.ShapeDtypeStruct(a.shape, BF),
        scratch_shapes=pair(a),
        compiler_params=room(8),
        cost_estimate=cost(0.5),
    )(a, b, *after)


def renorm_kernel(heads, tokens_all, ids_ref, base_ref, *refs):
    outs, (both, sem) = refs[-2 - heads : -2], refs[-2:]
    fetch(refs[: 2 * heads], both, sem)
    tail = pl.ds(THIRD * FW, TAIL)
    for h in range(heads):
        a_ref, b_ref = both.at[2 * h], both.at[2 * h + 1]
        start = ids_ref[CORE] * HALF + ids_ref[NEAR + h] * THIRD
        rate_sum = join_rows(a_ref[tail, :]) + join_rows(b_ref[tail, :])
        step = base_rate / (math.sqrt(tokens_all) * (rate_sum / tokens_all))
        for i in range(THIRD):
            sl = pl.ds(i * FW, FW)
            pull = a_ref[sl, :].astype(F32) + b_ref[sl, :].astype(F32)
            at = start + i
            col = pl.ds(pl.multiple_of((at % PER) * LANES, LANES), LANES)
            base = base_ref[h, at // PER, :, col].astype(F32)
            updated = base + step * pull
            old = jnp.sqrt(jnp.sum(base * base, axis=0, keepdims=True) + 1e-06)
            new = jnp.sqrt(jnp.sum(updated * updated, axis=0, keepdims=True) + 1e-06)
            outs[h][i] = (updated * (old / new)).astype(BF)


def renorm(ids, tokens_all, fast_weights, pulls, after):
    heads, one = fast_weights.shape[0], pulls[0].shape
    shape = (THIRD, FW, LANES)
    return pl.pallas_call(
        functools.partial(renorm_kernel, heads, tokens_all),
        grid=(1,),
        in_specs=[SMEM, full(fast_weights.shape)] + [ANY] * (len(pulls) + len(after)),
        out_specs=[full(shape)] * heads,
        out_shape=[jax.ShapeDtypeStruct(shape, BF)] * heads,
        scratch_shapes=[
            pltpu.VMEM((2 * heads,) + one, BF),
            pltpu.SemaphoreType.DMA((2 * heads,)),
        ],
        compiler_params=room(24),
        cost_estimate=cost(2.1),
    )(ids, fast_weights, *pulls, *after)


def attn_kernel(ids_ref, q_ref, k_ref, v_ref, rim_ref, *rest):
    o_ref = rest[-1]
    rows = q_ref.shape[0]
    w, d = WINDOW, HEAD_DIM
    row = lax.broadcasted_iota(jnp.int32, (w, w), 0)
    col = lax.broadcasted_iota(jnp.int32, (w, w), 1)
    own = col <= row
    factor = math.log2(math.e) / math.sqrt(d)
    has_prev = ids_ref[FIRST] == 0
    ones = jnp.ones((2 * w, LANES), BF)
    for h in range(q_ref.shape[1] // d):
        cs = slice(h * d, (h + 1) * d)
        for b in range(rows // w):
            sl = pl.ds(b * w, w)
            if b == 0:
                k2 = jnp.concatenate([rim_ref[:w, cs], k_ref[sl, cs]], axis=0)
                v2 = jnp.concatenate([rim_ref[w:, cs], v_ref[sl, cs]], axis=0)
            else:
                both = pl.ds((b - 1) * w, 2 * w)
                k2, v2 = k_ref[both, cs], v_ref[both, cs]
            s2 = lax.dot_general(q_ref[sl, cs], k2, NT, preferred_element_type=F32)
            prev = s2[:, :w]
            if b == 0:
                prev = jnp.where(has_prev, prev, -1e30)
            s = jnp.where(own, s2[:, w:], prev)
            e = jnp.exp2((s - jnp.max(s, axis=1, keepdims=True)) * factor).astype(BF)
            zero = jnp.zeros_like(e)
            e2 = jnp.concatenate([jnp.where(own, zero, e), jnp.where(own, e, zero)], axis=1)
            o = mm(e2, jnp.concatenate([v2, ones], axis=1))
            o_ref[sl, cs] = (o[:, :d] / o[:, d:]).astype(o_ref.dtype)


def attention(piece, width, ids, query, keys, values, rim, after):
    rows = query.shape[0]
    col = pl.BlockSpec((rows, width), lambda i: (0, piece))
    of_rim = pl.BlockSpec((2 * WINDOW, width), lambda i: (0, piece))
    return pl.pallas_call(
        attn_kernel,
        grid=(1,),
        in_specs=[SMEM, col, col, col, of_rim] + [ANY] * len(after),
        out_specs=full((rows, width)),
        out_shape=jax.ShapeDtypeStruct((rows, width), BF),
        compiler_params=room(16),
        cost_estimate=cost(2.1 * rows * width / 2**18),
    )(ids, query, keys, values, rim, *after)


def apply_tile(q, att, weights, act):
    wide = 2 * LANES
    rows = q.shape[0]
    for j in range(FW // wide):
        cs = slice(j * wide, (j + 1) * wide)
        gate = mm(q, weights[0, :, cs])
        up = mm(q, weights[1, :, cs])
        act[:rows, cs] = (gate * sigmoid(gate) * up).astype(BF)
    y = mm(act[:rows, :], weights[2])
    y = y * lax.rsqrt(jnp.mean(y * y, axis=1, keepdims=True) + 1e-06)
    return (att.astype(F32) + y).astype(BF)


def apply_kernel(h, pieces, ids_ref, q_hbm, *refs):
    att_hbm, refs = refs[:pieces], refs[pieces:]
    blocks = refs[:4]
    lo_ref, hi_ref, nw_hbm, q, att, nw, act, sem, bsem, osem = refs[-10:]
    rows = q.shape[0]
    core, near = ids_ref[CORE], ids_ref[NEAR + h]
    copies = [pltpu.make_async_copy(q_hbm.at[:, pl.ds(h * FW, FW)], q, sem.at[0])]
    for i, a in enumerate(att_hbm):
        to = att.at[:, pl.ds(i * a.shape[1], a.shape[1])]
        copies.append(pltpu.make_async_copy(a, to, sem.at[1 + i]))
    for n, src in enumerate(blocks):
        half, third = core ^ (n // 2), near ^ (n % 2)
        for i in range(THIRD):
            b = half * HALF + third * THIRD + i
            col = pl.ds(pl.multiple_of((b % PER) * LANES, LANES), LANES)
            dst = nw.at[b // PER, :, col]
            copies.append(pltpu.make_async_copy(src.at[i], dst, bsem.at[n, i]))
    for c in copies:
        c.start()
    for c in copies:
        c.wait()
    out = pltpu.make_async_copy(nw, nw_hbm.at[h], osem)
    out.start()
    cut = lo_ref.shape[0]
    for ref, start in ((lo_ref, 0), (hi_ref, cut)):
        sl = pl.ds(start, ref.shape[0])
        ref[...] = apply_tile(q[sl, :], att[sl, :], nw, act)
    out.wait()


def apply(h, heads, ids, query, attended, blocks, cut, whole, after):
    rows, pieces = query.shape[0], len(attended)
    shape = (heads, 3, FW, FW)
    extra = ([] if whole is None else [whole]) + after
    alias = {} if whole is None else {2 + pieces + len(blocks): 2}
    sizes = [(cut, FW), (rows - cut, FW)]
    return pl.pallas_call(
        functools.partial(apply_kernel, h, pieces),
        grid=(1,),
        in_specs=[SMEM] + [ANY] * (1 + pieces + len(blocks) + len(extra)),
        out_specs=[full(x) for x in sizes] + [ANY],
        out_shape=[jax.ShapeDtypeStruct(x, BF) for x in sizes + [shape]],
        input_output_aliases=alias,
        scratch_shapes=[
            pltpu.VMEM((rows, FW), BF),
            pltpu.VMEM((rows, FW), BF),
            pltpu.VMEM((3, FW, FW), BF),
            pltpu.VMEM((max(cut, rows - cut), FW), BF),
            pltpu.SemaphoreType.DMA((1 + pieces,)),
            pltpu.SemaphoreType.DMA((4, THIRD)),
            pltpu.SemaphoreType.DMA,
        ],
        compiler_params=room(20),
        cost_estimate=cost(3.3 * rows / 1024),
    )(ids, query, *attended, *blocks, *extra)


def joined(refs):
    return jnp.concatenate([r[...] for r in refs], axis=1)


def partial_kernel(heads, *refs):
    x_refs, w_ref = refs[:heads], refs[heads]
    o_ref, x = refs[-2:]

    @pl.when(pl.program_id(0) == 0)
    def _():
        for h in range(heads):
            x[:, h * FW : (h + 1) * FW] = x_refs[h][...]

    o_ref[0] = mm(x[...], w_ref[...]).astype(BF)


def partials(merged, out_weight, groups, after):
    rows, heads = merged[0].shape[0], len(merged)
    feats, width = out_weight.shape[0], out_weight.shape[1] // groups
    return pl.pallas_call(
        functools.partial(partial_kernel, heads),
        grid=(groups,),
        in_specs=[full(m.shape) for m in merged]
        + [pl.BlockSpec((feats, width), lambda d: (0, d))]
        + [ANY] * len(after),
        out_specs=pl.BlockSpec((1, rows, width), lambda d: (d, 0, 0)),
        out_shape=jax.ShapeDtypeStruct((groups, rows, width), BF),
        scratch_shapes=[pltpu.VMEM((rows, feats), BF)],
        compiler_params=room(24),
        cost_estimate=cost(1 * rows / 512),
    )(*merged, out_weight, *after)


def stack_kernel(n, *refs):
    o_ref = refs[-1]
    at = 0
    for r in refs[:n]:
        o_ref[pl.ds(at, r.shape[0])] = r[...]
        at += r.shape[0]


def stack(parts, after):
    shape = (sum(p.shape[0] for p in parts),) + parts[0].shape[1:]
    return pl.pallas_call(
        functools.partial(stack_kernel, len(parts)),
        grid=(1,),
        in_specs=[full(p.shape) for p in parts] + [ANY] * len(after),
        out_specs=full(shape),
        out_shape=jax.ShapeDtypeStruct(shape, BF),
        compiler_params=room(20),
        cost_estimate=cost(0.1),
    )(*parts, *after)


def ring_kernel(t, n, at, tail, wave, ids_ref, right_hbm, left_hbm, p_hbm, *refs):
    ro_ref, lo_ref, x_hbm, got, own, sem, xsem = refs[-7:]
    width = right_hbm.shape[1]
    cols = pl.ds(wave * width, width)
    copies = [
        pltpu.make_async_copy(right_hbm, got.at[0], sem.at[0]),
        pltpu.make_async_copy(p_hbm.at[ids_ref[at], :, cols], own.at[0], sem.at[1]),
        pltpu.make_async_copy(left_hbm, got.at[1], sem.at[2]),
        pltpu.make_async_copy(p_hbm.at[ids_ref[at + 1], :, cols], own.at[1], sem.at[3]),
    ]
    for c in copies:
        c.start()
    zero = jnp.zeros((), BF)
    for i, ref in enumerate((ro_ref, lo_ref)):
        copies[2 * i].wait()
        copies[2 * i + 1].wait()
        ref[...] = got[i] + jnp.where(ids_ref[at + 2 + i] > 0, own[i], zero)
    for i, (slot, here) in enumerate(((t - 1, t <= ids_ref[tail]), (n - 1 - t, t < n - ids_ref[tail]))):

        @pl.when(here)
        def _():
            keep = pltpu.make_async_copy(got.at[i], x_hbm.at[slot, :, cols], xsem.at[i])
            keep.start()
            keep.wait()


def ring_step(t, n, ids, at, tail, wave, right, left, partial, x, after):
    out = jax.ShapeDtypeStruct(right.shape, BF)
    kept = jax.ShapeDtypeStruct((n - 1, right.shape[0], partial.shape[2]), BF)
    more = ([] if x is None else [x]) + after
    return pl.pallas_call(
        functools.partial(ring_kernel, t, n, at, tail, wave),
        grid=(1,),
        in_specs=[SMEM] + [ANY] * (3 + len(more)),
        out_specs=[full(right.shape)] * 2 + [ANY],
        out_shape=[out, out, kept],
        input_output_aliases={} if x is None else {4: 2},
        scratch_shapes=[
            pltpu.VMEM((2,) + right.shape, BF),
            pltpu.VMEM((2,) + right.shape, BF),
            pltpu.SemaphoreType.DMA((4,)),
            pltpu.SemaphoreType.DMA((2,)),
        ],
        compiler_params=room(12),
        cost_estimate=cost(30),
    )(ids, right, left, partial, *more)


def gathered_kernel(n, heads, parts, at, ids_ref, *refs):
    w_pieces = len(parts)
    own_refs, refs = refs[:heads], refs[heads:]
    x_hbm, refs = refs[0], refs[1:]
    w_ref, piece_refs = refs[0], refs[1 : 1 + w_pieces]
    o_ref, x, cols, acc, xsem, wsem = refs[-6:]
    share = piece_refs[0].shape[2]
    sources = [r.at[i] for r, k in zip(piece_refs, parts) for i in range(k)]

    def each(steps, do):
        for t in steps:
            do(t, pltpu.make_async_copy(x_hbm.at[t], x.at[t], xsem.at[t]))
            for p, source in enumerate(sources):
                to = ids_ref[at + 1 + p] * share
                to = pl.ds(pl.multiple_of(to, share), share)
                do(t, pltpu.make_async_copy(source.at[t], cols.at[t, to, :], wsem.at[t, p]))

    each(range(n - 1), lambda t, c: c.start())
    acc[...] = mm(joined(own_refs), w_ref[...])
    for t in range(n - 1):
        each((t,), lambda t, c: c.wait())
        if t < n - 2:
            acc[...] += mm(x[t], cols[t])
        else:
            o_ref[...] = (acc[...] + mm(x[t], cols[t])).astype(BF)


def gathered(ids, at, merged, x, out_weight, spread, rows_all, after):
    n, heads, parts = x.shape[0] + 1, len(merged), [p.shape[0] for p in spread]
    rows, feats = merged[0].shape[0], out_weight.shape[0]
    width = out_weight.shape[1] // n
    return pl.pallas_call(
        functools.partial(gathered_kernel, n, heads, parts, at),
        grid_spec=pltpu.PrefetchScalarGridSpec(
            num_scalar_prefetch=1,
            grid=(1,),
            in_specs=[full(m.shape) for m in merged]
            + [ANY]
            + [pl.BlockSpec((feats, width), lambda i, s: (0, s[at]))]
            + [ANY] * len(spread)
            + [ANY] * len(after),
            out_specs=pl.BlockSpec((rows, width), lambda i, s: (0, 0)),
            scratch_shapes=[
                pltpu.VMEM((n - 1, rows, feats), BF),
                pltpu.VMEM((n - 1, feats, width), BF),
                pltpu.VMEM((rows, width), F32),
                pltpu.SemaphoreType.DMA((n - 1,)),
                pltpu.SemaphoreType.DMA((n - 1, sum(parts))),
            ],
        ),
        out_shape=jax.ShapeDtypeStruct((rows_all, width), BF),
        compiler_params=room(48),
        cost_estimate=cost(9 * rows / 512),
    )(
        ids, *merged, x, out_weight, *spread, *after
    )


def finish_kernel(at, wave, ids_ref, right_hbm, left_hbm, p_hbm, out_in, o_hbm, got, own, sem):
    del out_in
    rows, width = own.shape
    cols = pl.ds(wave * width, width)
    copies = [
        pltpu.make_async_copy(right_hbm, got.at[0], sem.at[0]),
        pltpu.make_async_copy(left_hbm, got.at[1], sem.at[1]),
        pltpu.make_async_copy(p_hbm.at[ids_ref[at], :, cols], own, sem.at[2]),
    ]
    for c in copies:
        c.start()
    for c in copies:
        c.wait()
    total = own[...].astype(F32) + (got[0].astype(F32) + got[1].astype(F32))
    own[...] = total.astype(BF)
    last = pl.ds(o_hbm.shape[0] - rows, rows)
    out = pltpu.make_async_copy(own, o_hbm.at[last, cols], sem.at[3])
    out.start()
    out.wait()


def finish(ids, at, wave, right, left, partial, out):
    return pl.pallas_call(
        functools.partial(finish_kernel, at, wave),
        grid=(1,),
        in_specs=[SMEM] + [ANY] * 4,
        out_specs=ANY,
        out_shape=jax.ShapeDtypeStruct(out.shape, BF),
        input_output_aliases={4: 0},
        scratch_shapes=[
            pltpu.VMEM((2,) + right.shape, BF),
            pltpu.VMEM(right.shape, BF),
            pltpu.SemaphoreType.DMA((4,)),
        ],
        compiler_params=room(12),
        cost_estimate=cost(30),
    )(ids, right, left, partial, out)


def scalars(*xs):
    return jnp.stack([jnp.asarray(x, jnp.int32) for x in xs])


def shards(query, keys, values, lr_code, fast_weights, out_weight):
    rows, feats = query.shape
    contexts, groups = lax.axis_size("ctx"), lax.axis_size("head")
    c, z = lax.axis_index("ctx"), lax.axis_index("head")
    tokens_all = rows * contexts
    heads = fast_weights.shape[0]
    bits = [1 << i for i in range(contexts.bit_length() - 1)]
    bit_of = {b: (c // b) % 2 for b in bits}
    order = [[bits[1 + h % 2]] for h in range(heads)]
    order = [o + [b for b in bits[1:] if b != o[0]] for o in order]
    spread = bits[2::-1]
    places = [0]
    for b in spread:
        places = places + [p ^ b for p in places]
    share, width = feats // len(places), out_weight.shape[1] // groups
    ids = [bit_of[1], c == 0] + [bit_of[o[0]] for o in order]
    step_at = [len(ids) + 4 * (t - 1) for t in range(groups)]
    for t in range(1, groups):
        ids += [(z - t) % groups, (z + t) % groups, t > z, t > groups - 1 - z]
    tail_at = len(ids)
    ids += [z] + [(c % len(places)) ^ p for p in places]
    strip_at = len(ids)
    for s in range(1, groups):
        ids += [c % len(places), (z + s) % groups]
    ids = scalars(*ids)

    keep, other = [], []
    for h in range(heads):
        g = grads(
            h,
            strip_at,
            ids,
            lr_code.T,
            keys,
            values,
            fast_weights,
            out_weight,
            [(share, width)] * (groups - 1),
            keep[-1:],
        )
        keep.append(g[0])
        other.append(swap(g[1], 1))
        if h == 0:
            rim = shift(g[2], "ctx", 1)
            strips = [rotate(x, "head", s + 1) for s, x in enumerate(g[3:])]
    split_up = []
    for h in range(heads):
        before = [split_up[0][1], rim] if h else []
        split_up.append(split(h, ids, keep[h], other[h], before))
    away = [swap(split_up[h][1], order[h][0]) for h in range(heads)]

    per_head = 2
    pieces = []

    def attend(after):
        i = len(pieces)
        pieces.append(attention(i, FW // per_head, ids, query, keys, values, rim, after))
        return pieces[-1]

    att = attend([s[1] for s in split_up])
    pull, far = [], []
    for h in range(heads):
        more = strips[1:2] if h == heads - 1 else []
        p = total(split_up[h][0], away[h], [att] + pull + more)
        for b in order[h][1:-1]:
            p = total(p, swap(p, b), [])
        pull.append(p)
        far.append(swap(p, order[h][-1]))
        att = attend([p])
    while len(pieces) < per_head * heads:
        att = attend([att])
    both = [x for h in range(heads) for x in (pull[h], far[h])]
    new = renorm(ids, tokens_all, fast_weights, both, [att, strips[0]] + strips[2:])

    cut = rows // 2
    merged, rest, weights = [], [], None
    for h in range(heads):
        b = order[h][0]
        near = swap(new[h], b)
        blocks = [new[h], near, swap(new[h], 1), swap(near, 1)]
        own = pieces[h * per_head : (h + 1) * per_head]
        m, r, weights = apply(h, heads, ids, query, own, blocks, cut, weights, [])
        merged.append(m)
        rest.append(r)
    to_right = [[shift(m, "head", 1) for m in merged]]
    to_left = [[shift(m, "head", -1) for m in merged]]

    near = stack([s[None] for s in strips], [merged[-1]])
    partial = partials(rest, out_weight, groups, [near])
    near = near.reshape((1,) + near.shape)
    after = near
    x = None
    for t in range(1, groups):
        right, left = [], []
        for h in range(heads):
            r, l, x = ring_step(
                t,
                groups,
                ids,
                step_at[t],
                tail_at,
                h,
                to_right[t - 1][h],
                to_left[t - 1][h],
                partial,
                x,
                [after],
            )
            after = l
            right.append(shift(r, "head", 1))
            left.append(shift(l, "head", -1))
            if (t, h) == (1, heads - 1):
                near = stack([near, swap(near, spread[0])], [after])
        to_right.append(right)
        to_left.append(left)
    spread_out = [near]
    for b in spread[1:]:
        spread_out += [swap(p, b) for p in spread_out]
    out = gathered(
        ids,
        tail_at,
        merged,
        x,
        out_weight,
        spread_out,
        rows,
        [after],
    )
    for h in range(heads):
        out = finish(ids, tail_at, h, to_right[-1][h], to_left[-1][h], partial, out)
    return (out, weights)


def solution(mesh):
    placed = (
        P("ctx", "head"),
        P("ctx", "head"),
        P("ctx", "head"),
        P("ctx", "head"),
        P("head", None, None, None),
        P("head", None),
    )
    return jax.shard_map(
        shards,
        mesh=mesh,
        in_specs=placed,
        out_specs=(P("ctx", "head"), P("head", None, None, None)),
        check_vma=False,
    )
```

```python
import functools
import math

import jax
import jax.numpy as jnp
from jax import lax
from jax.experimental import pallas as pl
from jax.experimental.pallas import tpu as pltpu
from jax.sharding import PartitionSpec as P

FW = 512
HEAD_DIM = 128
WINDOW = 256
LANES = 128
PER = FW // LANES
BLOCKS = 3 * PER
HALF = BLOCKS // 2
THIRD = BLOCKS // 4
TAIL = 16

base_rate = 0.05
BF = jnp.bfloat16
F32 = jnp.float32
NT = (((1,), (1,)), ((), ()))

CORE, FIRST, NEAR = 0, 1, 2

ANY = pl.BlockSpec(memory_space=pl.ANY)
SMEM = pl.BlockSpec(memory_space=pltpu.SMEM)


def room(mib):
    return pltpu.CompilerParams(vmem_limit_bytes=mib * 2**20)


def mm(a, b):
    return jnp.dot(a, b, preferred_element_type=F32)


def shift(block, axis, distance):
    n = lax.axis_size(axis)
    return lax.ppermute(block, axis, [(i, i + distance) for i in range(n) if 0 <= i + distance < n])


def rotate(block, axis, distance):
    n = lax.axis_size(axis)
    return lax.ppermute(block, axis, [(i, (i + distance) % n) for i in range(n)])


def swap(block, bit):
    n = lax.axis_size("ctx")
    return lax.ppermute(block, "ctx", [(i, i ^ bit) for i in range(n)])


def sigmoid(x):
    return 0.5 * jnp.tanh(0.5 * x) + 0.5


def full(shape):
    return pl.BlockSpec(shape, lambda *_: (0,) * len(shape))


def cost(microseconds):
    return pl.CostEstimate(
        flops=int(microseconds * 0.12e9), bytes_accessed=0, transcendentals=0
    )


def strip_copy(ids_ref, at, w_hbm, o_ref, sem):
    share, width = o_ref.shape
    rows = pl.ds(pl.multiple_of(ids_ref[at] * share, share), share)
    cols = pl.ds(pl.multiple_of(ids_ref[at + 1] * width, width), width)
    return pltpu.make_async_copy(w_hbm.at[rows, cols], o_ref, sem)


def split_rows(x):
    hi = x.astype(BF).astype(F32)
    mid = (x - hi).astype(BF).astype(F32)
    lo = x - hi - mid
    row = lax.broadcasted_iota(jnp.int32, (TAIL, LANES), 0)
    return jnp.where(row == 0, hi, jnp.where(row == 1, mid, jnp.where(row == 2, lo, 0.0))).astype(BF)


def join_rows(tail):
    return jnp.sum(tail.astype(F32), axis=0, keepdims=True)


def grads_kernel(h, at, ids_ref, code_ref, k_ref, v_ref, w_ref, *refs):
    lhs, rhs, sem = refs[-3:]
    copies = []
    if h == 0:
        k_hbm, v_hbm, ow_hbm, keep_ref, send_ref, rim_ref = refs[:6]
        last = pl.ds(k_hbm.shape[0] - WINDOW, WINDOW)
        copies = [
            pltpu.make_async_copy(k_hbm.at[last, :], rim_ref.at[pl.ds(0, WINDOW), :], sem.at[0]),
            pltpu.make_async_copy(
                v_hbm.at[last, :], rim_ref.at[pl.ds(WINDOW, WINDOW), :], sem.at[1]
            ),
        ] + [
            strip_copy(ids_ref, at + 2 * i, ow_hbm, strip_ref, sem.at[2 + i])
            for i, strip_ref in enumerate(refs[6:-3])
        ]
    else:
        keep_ref, send_ref = refs[-5:-3]
    for copy in copies:
        copy.start()
    rows = k_ref.shape[0]
    tile = min(256, rows)
    wide = 2 * LANES
    codes = code_ref[h : h + 1, :].astype(F32) * 2.0 ** (-14)
    for t in range(rows // tile):
        sl = pl.ds(t * tile, tile)
        k = k_ref[sl, :]
        rate = jnp.broadcast_to(codes[:, t * tile : (t + 1) * tile], (LANES, tile)).T
        rate = jnp.concatenate([rate] * PER, axis=1)
        push = (rate * v_ref[sl, :].astype(F32)).astype(BF)
        rhs[sl, 2 * FW :] = push
        for j in range(FW // wide):
            cs = slice(j * wide, (j + 1) * wide)
            gate = mm(k, w_ref[0, 0, :, cs])
            up = mm(k, w_ref[0, 1, :, cs])
            back = lax.dot_general(push, w_ref[0, 2, cs, :], NT, preferred_element_type=F32)
            s = sigmoid(gate)
            gs = gate * s
            lhs[FW + j * wide : FW + (j + 1) * wide, sl] = (gs * up).astype(BF).T
            rhs[sl, cs] = (back * up * (s + gs * (1.0 - s))).astype(BF)
            rhs[sl, FW + j * wide : FW + (j + 1) * wide] = (back * gs).astype(BF)
    lhs[:FW, :] = k_ref[...].T
    tail = split_rows(jnp.broadcast_to(jnp.sum(codes, axis=1, keepdims=True), (1, LANES)))
    pairs = HALF // 2
    for ref, half in ((send_ref, 1 - ids_ref[CORE]), (keep_ref, ids_ref[CORE])):
        ref[pl.ds(HALF * FW, TAIL), :] = tail
        for i in range(pairs):
            pair = half * pairs + i
            left = (pair >= 2 * FW // wide).astype(jnp.int32) * FW
            left = lhs[pl.ds(pl.multiple_of(left, FW), FW), :]
            right = rhs[:, pl.ds(pl.multiple_of(pair * wide, wide), wide)]
            r = mm(left, right).astype(BF)
            ref[pl.ds(2 * i * FW, FW), :] = r[:, :LANES]
            ref[pl.ds((2 * i + 1) * FW, FW), :] = r[:, LANES:]
    for copy in copies:
        copy.wait()


def grads(h, at, ids, codes, keys, values, fast_weights, out_weight, strips, after):
    rows, feats = keys.shape
    shape = (HALF * FW + TAIL, LANES)
    outs = [shape, shape] + ([(2 * WINDOW, feats)] + strips if h == 0 else [])
    more = [keys, values, out_weight] if h == 0 else after
    col = pl.BlockSpec((rows, FW), lambda i: (0, h))
    return pl.pallas_call(
        functools.partial(grads_kernel, h, at),
        grid=(1,),
        in_specs=[
            SMEM,
            full(codes.shape),
            col,
            col,
            pl.BlockSpec((1, 3, FW, FW), lambda i: (h, 0, 0, 0)),
        ]
        + [ANY] * len(more),
        out_specs=[full(x) for x in outs],
        out_shape=[jax.ShapeDtypeStruct(x, BF) for x in outs],
        scratch_shapes=[
            pltpu.VMEM((2 * FW, rows), BF),
            pltpu.VMEM((rows, 3 * FW), BF),
            pltpu.SemaphoreType.DMA((2 + len(strips),)),
        ],
        compiler_params=room(58),
        cost_estimate=cost(8 * rows / 1024),
    )(ids, codes, keys, values, fast_weights, *more)


def fetch(refs, scratch, sem):
    copies = [pltpu.make_async_copy(r, scratch.at[i], sem.at[i]) for i, r in enumerate(refs)]
    for c in copies:
        c.start()
    for c in copies:
        c.wait()


def pair(x):
    return [pltpu.VMEM((2,) + x.shape, x.dtype), pltpu.SemaphoreType.DMA((2,))]


def split_kernel(h, ids_ref, keep_hbm, other_hbm, *refs):
    keep_out, send_out, both, sem = refs[-4:]
    fetch((keep_hbm, other_hbm), both, sem)
    keep_ref, other_ref = both.at[0], both.at[1]
    n = THIRD * FW
    bit = ids_ref[NEAR + h]
    mine = pl.ds(pl.multiple_of(bit * n, n), n)
    theirs = pl.ds(pl.multiple_of((1 - bit) * n, n), n)
    keep_out[pl.ds(0, n), :] = keep_ref[mine, :] + other_ref[mine, :]
    send_out[pl.ds(0, n), :] = keep_ref[theirs, :] + other_ref[theirs, :]
    tail = pl.ds(HALF * FW, TAIL)
    rate = split_rows(join_rows(keep_ref[tail, :]) + join_rows(other_ref[tail, :]))
    keep_out[pl.ds(n, TAIL), :] = rate
    send_out[pl.ds(n, TAIL), :] = rate


def split(h, ids, keep, other, after):
    shape = (THIRD * FW + TAIL, LANES)
    out = jax.ShapeDtypeStruct(shape, BF)
    return pl.pallas_call(
        functools.partial(split_kernel, h),
        grid=(1,),
        in_specs=[SMEM] + [ANY] * (2 + len(after)),
        out_specs=[full(shape), full(shape)],
        out_shape=[out, out],
        scratch_shapes=pair(keep),
        compiler_params=room(12),
        cost_estimate=cost(0.9),
    )(ids, keep, other, *after)


def total_kernel(a_hbm, b_hbm, *rest):
    o_ref, both, sem = rest[-3:]
    fetch((a_hbm, b_hbm), both, sem)
    a_ref, b_ref = both.at[0], both.at[1]
    n = THIRD * FW
    o_ref[pl.ds(0, n), :] = a_ref[pl.ds(0, n), :] + b_ref[pl.ds(0, n), :]
    tail = pl.ds(n, TAIL)
    o_ref[tail, :] = split_rows(join_rows(a_ref[tail, :]) + join_rows(b_ref[tail, :]))


def total(a, b, after):
    return pl.pallas_call(
        total_kernel,
        grid=(1,),
        in_specs=[ANY] * (2 + len(after)),
        out_specs=full(a.shape),
        out_shape=jax.ShapeDtypeStruct(a.shape, BF),
        scratch_shapes=pair(a),
        compiler_params=room(8),
        cost_estimate=cost(0.5),
    )(a, b, *after)


def renorm_kernel(heads, tokens_all, ids_ref, base_ref, *refs):
    outs, (both, sem) = refs[-2 - heads : -2], refs[-2:]
    fetch(refs[: 2 * heads], both, sem)
    tail = pl.ds(THIRD * FW, TAIL)
    for h in range(heads):
        a_ref, b_ref = both.at[2 * h], both.at[2 * h + 1]
        start = ids_ref[CORE] * HALF + ids_ref[NEAR + h] * THIRD
        rate_sum = join_rows(a_ref[tail, :]) + join_rows(b_ref[tail, :])
        step = base_rate / (math.sqrt(tokens_all) * (rate_sum / tokens_all))
        for i in range(THIRD):
            sl = pl.ds(i * FW, FW)
            pull = a_ref[sl, :].astype(F32) + b_ref[sl, :].astype(F32)
            at = start + i
            col = pl.ds(pl.multiple_of((at % PER) * LANES, LANES), LANES)
            base = base_ref[h, at // PER, :, col].astype(F32)
            updated = base + step * pull
            old = jnp.sqrt(jnp.sum(base * base, axis=0, keepdims=True) + 1e-06)
            new = jnp.sqrt(jnp.sum(updated * updated, axis=0, keepdims=True) + 1e-06)
            outs[h][i] = (updated * (old / new)).astype(BF)


def renorm(ids, tokens_all, fast_weights, pulls, after):
    heads, one = fast_weights.shape[0], pulls[0].shape
    shape = (THIRD, FW, LANES)
    return pl.pallas_call(
        functools.partial(renorm_kernel, heads, tokens_all),
        grid=(1,),
        in_specs=[SMEM, full(fast_weights.shape)] + [ANY] * (len(pulls) + len(after)),
        out_specs=[full(shape)] * heads,
        out_shape=[jax.ShapeDtypeStruct(shape, BF)] * heads,
        scratch_shapes=[
            pltpu.VMEM((2 * heads,) + one, BF),
            pltpu.SemaphoreType.DMA((2 * heads,)),
        ],
        compiler_params=room(24),
        cost_estimate=cost(2.1),
    )(ids, fast_weights, *pulls, *after)


def attn_kernel(ids_ref, q_ref, k_ref, v_ref, rim_ref, *rest):
    o_ref = rest[-1]
    rows = q_ref.shape[0]
    w, d = WINDOW, HEAD_DIM
    row = lax.broadcasted_iota(jnp.int32, (w, w), 0)
    col = lax.broadcasted_iota(jnp.int32, (w, w), 1)
    own = col <= row
    factor = math.log2(math.e) / math.sqrt(d)
    has_prev = ids_ref[FIRST] == 0
    ones = jnp.ones((2 * w, LANES), BF)
    for h in range(q_ref.shape[1] // d):
        cs = slice(h * d, (h + 1) * d)
        for b in range(rows // w):
            sl = pl.ds(b * w, w)
            if b == 0:
                k2 = jnp.concatenate([rim_ref[:w, cs], k_ref[sl, cs]], axis=0)
                v2 = jnp.concatenate([rim_ref[w:, cs], v_ref[sl, cs]], axis=0)
            else:
                both = pl.ds((b - 1) * w, 2 * w)
                k2, v2 = k_ref[both, cs], v_ref[both, cs]
            s2 = lax.dot_general(q_ref[sl, cs], k2, NT, preferred_element_type=F32)
            prev = s2[:, :w]
            if b == 0:
                prev = jnp.where(has_prev, prev, -1e30)
            s = jnp.where(own, s2[:, w:], prev)
            e = jnp.exp2((s - jnp.max(s, axis=1, keepdims=True)) * factor).astype(BF)
            zero = jnp.zeros_like(e)
            e2 = jnp.concatenate([jnp.where(own, zero, e), jnp.where(own, e, zero)], axis=1)
            o = mm(e2, jnp.concatenate([v2, ones], axis=1))
            o_ref[sl, cs] = (o[:, :d] / o[:, d:]).astype(o_ref.dtype)


def attention(piece, width, ids, query, keys, values, rim, after):
    rows = query.shape[0]
    col = pl.BlockSpec((rows, width), lambda i: (0, piece))
    of_rim = pl.BlockSpec((2 * WINDOW, width), lambda i: (0, piece))
    return pl.pallas_call(
        attn_kernel,
        grid=(1,),
        in_specs=[SMEM, col, col, col, of_rim] + [ANY] * len(after),
        out_specs=full((rows, width)),
        out_shape=jax.ShapeDtypeStruct((rows, width), BF),
        compiler_params=room(16),
        cost_estimate=cost(2.1 * rows * width / 2**18),
    )(ids, query, keys, values, rim, *after)


def apply_tile(q, att, weights, act):
    wide = 2 * LANES
    rows = q.shape[0]
    for j in range(FW // wide):
        cs = slice(j * wide, (j + 1) * wide)
        gate = mm(q, weights[0, :, cs])
        up = mm(q, weights[1, :, cs])
        act[:rows, cs] = (gate * sigmoid(gate) * up).astype(BF)
    y = mm(act[:rows, :], weights[2])
    y = y * lax.rsqrt(jnp.mean(y * y, axis=1, keepdims=True) + 1e-06)
    return (att.astype(F32) + y).astype(BF)


def apply_kernel(h, pieces, ids_ref, q_hbm, *refs):
    att_hbm, refs = refs[:pieces], refs[pieces:]
    blocks = refs[:4]
    lo_ref, hi_ref, nw_hbm, q, att, nw, act, sem, bsem, osem = refs[-10:]
    rows = q.shape[0]
    core, near = ids_ref[CORE], ids_ref[NEAR + h]
    copies = [pltpu.make_async_copy(q_hbm.at[:, pl.ds(h * FW, FW)], q, sem.at[0])]
    for i, a in enumerate(att_hbm):
        to = att.at[:, pl.ds(i * a.shape[1], a.shape[1])]
        copies.append(pltpu.make_async_copy(a, to, sem.at[1 + i]))
    for n, src in enumerate(blocks):
        half, third = core ^ (n // 2), near ^ (n % 2)
        for i in range(THIRD):
            b = half * HALF + third * THIRD + i
            col = pl.ds(pl.multiple_of((b % PER) * LANES, LANES), LANES)
            dst = nw.at[b // PER, :, col]
            copies.append(pltpu.make_async_copy(src.at[i], dst, bsem.at[n, i]))
    for c in copies:
        c.start()
    for c in copies:
        c.wait()
    out = pltpu.make_async_copy(nw, nw_hbm.at[h], osem)
    out.start()
    cut = lo_ref.shape[0]
    for ref, start in ((lo_ref, 0), (hi_ref, cut)):
        sl = pl.ds(start, ref.shape[0])
        ref[...] = apply_tile(q[sl, :], att[sl, :], nw, act)
    out.wait()


def apply(h, heads, ids, query, attended, blocks, cut, whole, after):
    rows, pieces = query.shape[0], len(attended)
    shape = (heads, 3, FW, FW)
    extra = ([] if whole is None else [whole]) + after
    alias = {} if whole is None else {2 + pieces + len(blocks): 2}
    sizes = [(cut, FW), (rows - cut, FW)]
    return pl.pallas_call(
        functools.partial(apply_kernel, h, pieces),
        grid=(1,),
        in_specs=[SMEM] + [ANY] * (1 + pieces + len(blocks) + len(extra)),
        out_specs=[full(x) for x in sizes] + [ANY],
        out_shape=[jax.ShapeDtypeStruct(x, BF) for x in sizes + [shape]],
        input_output_aliases=alias,
        scratch_shapes=[
            pltpu.VMEM((rows, FW), BF),
            pltpu.VMEM((rows, FW), BF),
            pltpu.VMEM((3, FW, FW), BF),
            pltpu.VMEM((max(cut, rows - cut), FW), BF),
            pltpu.SemaphoreType.DMA((1 + pieces,)),
            pltpu.SemaphoreType.DMA((4, THIRD)),
            pltpu.SemaphoreType.DMA,
        ],
        compiler_params=room(20),
        cost_estimate=cost(3.3 * rows / 1024),
    )(ids, query, *attended, *blocks, *extra)


def joined(refs):
    return jnp.concatenate([r[...] for r in refs], axis=1)


def partial_kernel(heads, *refs):
    x_refs, w_ref = refs[:heads], refs[heads]
    o_ref, x = refs[-2:]

    @pl.when(pl.program_id(0) == 0)
    def _():
        for h in range(heads):
            x[:, h * FW : (h + 1) * FW] = x_refs[h][...]

    o_ref[0] = mm(x[...], w_ref[...]).astype(BF)


def partials(merged, out_weight, groups, after):
    rows, heads = merged[0].shape[0], len(merged)
    feats, width = out_weight.shape[0], out_weight.shape[1] // groups
    return pl.pallas_call(
        functools.partial(partial_kernel, heads),
        grid=(groups,),
        in_specs=[full(m.shape) for m in merged]
        + [pl.BlockSpec((feats, width), lambda d: (0, d))]
        + [ANY] * len(after),
        out_specs=pl.BlockSpec((1, rows, width), lambda d: (d, 0, 0)),
        out_shape=jax.ShapeDtypeStruct((groups, rows, width), BF),
        scratch_shapes=[pltpu.VMEM((rows, feats), BF)],
        compiler_params=room(24),
        cost_estimate=cost(1 * rows / 512),
    )(*merged, out_weight, *after)


def stack_kernel(n, *refs):
    o_ref = refs[-1]
    at = 0
    for r in refs[:n]:
        o_ref[pl.ds(at, r.shape[0])] = r[...]
        at += r.shape[0]


def stack(parts, after):
    shape = (sum(p.shape[0] for p in parts),) + parts[0].shape[1:]
    return pl.pallas_call(
        functools.partial(stack_kernel, len(parts)),
        grid=(1,),
        in_specs=[full(p.shape) for p in parts] + [ANY] * len(after),
        out_specs=full(shape),
        out_shape=jax.ShapeDtypeStruct(shape, BF),
        compiler_params=room(20),
        cost_estimate=cost(0.1),
    )(*parts, *after)


def ring_kernel(t, n, at, tail, wave, ids_ref, right_hbm, left_hbm, p_hbm, *refs):
    ro_ref, lo_ref, x_hbm, got, own, sem, xsem = refs[-7:]
    width = right_hbm.shape[1]
    cols = pl.ds(wave * width, width)
    copies = [
        pltpu.make_async_copy(right_hbm, got.at[0], sem.at[0]),
        pltpu.make_async_copy(p_hbm.at[ids_ref[at], :, cols], own.at[0], sem.at[1]),
        pltpu.make_async_copy(left_hbm, got.at[1], sem.at[2]),
        pltpu.make_async_copy(p_hbm.at[ids_ref[at + 1], :, cols], own.at[1], sem.at[3]),
    ]
    for c in copies:
        c.start()
    zero = jnp.zeros((), BF)
    for i, ref in enumerate((ro_ref, lo_ref)):
        copies[2 * i].wait()
        copies[2 * i + 1].wait()
        ref[...] = got[i] + jnp.where(ids_ref[at + 2 + i] > 0, own[i], zero)
    for i, (slot, here) in enumerate(((t - 1, t <= ids_ref[tail]), (n - 1 - t, t < n - ids_ref[tail]))):

        @pl.when(here)
        def _():
            keep = pltpu.make_async_copy(got.at[i], x_hbm.at[slot, :, cols], xsem.at[i])
            keep.start()
            keep.wait()


def ring_step(t, n, ids, at, tail, wave, right, left, partial, x, after):
    out = jax.ShapeDtypeStruct(right.shape, BF)
    kept = jax.ShapeDtypeStruct((n - 1, right.shape[0], partial.shape[2]), BF)
    more = ([] if x is None else [x]) + after
    return pl.pallas_call(
        functools.partial(ring_kernel, t, n, at, tail, wave),
        grid=(1,),
        in_specs=[SMEM] + [ANY] * (3 + len(more)),
        out_specs=[full(right.shape)] * 2 + [ANY],
        out_shape=[out, out, kept],
        input_output_aliases={} if x is None else {4: 2},
        scratch_shapes=[
            pltpu.VMEM((2,) + right.shape, BF),
            pltpu.VMEM((2,) + right.shape, BF),
            pltpu.SemaphoreType.DMA((4,)),
            pltpu.SemaphoreType.DMA((2,)),
        ],
        compiler_params=room(12),
        cost_estimate=cost(30),
    )(ids, right, left, partial, *more)


def gathered_kernel(n, heads, parts, at, ids_ref, *refs):
    own_refs, refs = refs[:heads], refs[heads:]
    x_hbm, refs = refs[0], refs[1:]
    w_ref, near_ref, far_ref = refs[:3]
    o_ref, x, cols, acc, xsem, wsem = refs[-6:]
    share = near_ref.shape[2]
    near = near_ref.shape[0]

    def each(steps, do):
        for t in steps:
            do(t, pltpu.make_async_copy(x_hbm.at[t], x.at[t], xsem.at[t]))
            for p in range(parts):
                src = near_ref.at[p, t] if p < near else far_ref.at[p - near, t]
                to = ids_ref[at + 1 + p] * share
                to = pl.ds(pl.multiple_of(to, share), share)
                do(t, pltpu.make_async_copy(src, cols.at[t, to, :], wsem.at[t, p]))

    each(range(n - 1), lambda t, c: c.start())
    acc[...] = mm(joined(own_refs), w_ref[...])
    for t in range(n - 1):
        each((t,), lambda t, c: c.wait())
        if t < n - 2:
            acc[...] += mm(x[t], cols[t])
        else:
            o_ref[...] = (acc[...] + mm(x[t], cols[t])).astype(BF)


def gathered(ids, at, merged, x, out_weight, near, far, rows_all, after):
    n, heads, parts = x.shape[0] + 1, len(merged), near.shape[0] + far.shape[0]
    rows, feats = merged[0].shape[0], out_weight.shape[0]
    width = out_weight.shape[1] // n
    return pl.pallas_call(
        functools.partial(gathered_kernel, n, heads, parts, at),
        grid_spec=pltpu.PrefetchScalarGridSpec(
            num_scalar_prefetch=1,
            grid=(1,),
            in_specs=[full(m.shape) for m in merged]
            + [ANY]
            + [pl.BlockSpec((feats, width), lambda i, s: (0, s[at])), ANY, ANY]
            + [ANY] * len(after),
            out_specs=pl.BlockSpec((rows, width), lambda i, s: (0, 0)),
            scratch_shapes=[
                pltpu.VMEM((n - 1, rows, feats), BF),
                pltpu.VMEM((n - 1, feats, width), BF),
                pltpu.VMEM((rows, width), F32),
                pltpu.SemaphoreType.DMA((n - 1,)),
                pltpu.SemaphoreType.DMA((n - 1, parts)),
            ],
        ),
        out_shape=jax.ShapeDtypeStruct((rows_all, width), BF),
        compiler_params=room(48),
        cost_estimate=cost(9 * rows / 512),
    )(
        ids, *merged, x, out_weight, near, far, *after
    )


def finish_kernel(at, wave, ids_ref, right_hbm, left_hbm, p_hbm, out_in, o_hbm, got, own, sem):
    del out_in
    rows, width = own.shape
    cols = pl.ds(wave * width, width)
    copies = [
        pltpu.make_async_copy(right_hbm, got.at[0], sem.at[0]),
        pltpu.make_async_copy(left_hbm, got.at[1], sem.at[1]),
        pltpu.make_async_copy(p_hbm.at[ids_ref[at], :, cols], own, sem.at[2]),
    ]
    for c in copies:
        c.start()
    for c in copies:
        c.wait()
    total = own[...].astype(F32) + (got[0].astype(F32) + got[1].astype(F32))
    own[...] = total.astype(BF)
    last = pl.ds(o_hbm.shape[0] - rows, rows)
    out = pltpu.make_async_copy(own, o_hbm.at[last, cols], sem.at[3])
    out.start()
    out.wait()


def finish(ids, at, wave, right, left, partial, out):
    return pl.pallas_call(
        functools.partial(finish_kernel, at, wave),
        grid=(1,),
        in_specs=[SMEM] + [ANY] * 4,
        out_specs=ANY,
        out_shape=jax.ShapeDtypeStruct(out.shape, BF),
        input_output_aliases={4: 0},
        scratch_shapes=[
            pltpu.VMEM((2,) + right.shape, BF),
            pltpu.VMEM(right.shape, BF),
            pltpu.SemaphoreType.DMA((4,)),
        ],
        compiler_params=room(12),
        cost_estimate=cost(30),
    )(ids, right, left, partial, out)


def scalars(*xs):
    return jnp.stack([jnp.asarray(x, jnp.int32) for x in xs])


def shards(query, keys, values, lr_code, fast_weights, out_weight):
    rows, feats = query.shape
    contexts, groups = lax.axis_size("ctx"), lax.axis_size("head")
    c, z = lax.axis_index("ctx"), lax.axis_index("head")
    tokens_all = rows * contexts
    heads = fast_weights.shape[0]
    bits = [1 << i for i in range(contexts.bit_length() - 1)]
    bit_of = {b: (c // b) % 2 for b in bits}
    order = [[bits[1 + h % 2]] for h in range(heads)]
    order = [o + [b for b in bits[1:] if b != o[0]] for o in order]
    spread = bits[2::-1]
    places = [0]
    for b in spread:
        places = places + [p ^ b for p in places]
    share, width = feats // len(places), out_weight.shape[1] // groups
    ids = [bit_of[1], c == 0] + [bit_of[o[0]] for o in order]
    step_at = [len(ids) + 4 * (t - 1) for t in range(groups)]
    for t in range(1, groups):
        ids += [(z - t) % groups, (z + t) % groups, t > z, t > groups - 1 - z]
    tail_at = len(ids)
    ids += [z] + [(c % len(places)) ^ p for p in places]
    strip_at = len(ids)
    for s in range(1, groups):
        ids += [c % len(places), (z + s) % groups]
    ids = scalars(*ids)

    keep, other = [], []
    for h in range(heads):
        g = grads(
            h,
            strip_at,
            ids,
            lr_code.T,
            keys,
            values,
            fast_weights,
            out_weight,
            [(share, width)] * (groups - 1),
            keep[-1:],
        )
        keep.append(g[0])
        other.append(swap(g[1], 1))
        if h == 0:
            rim = shift(g[2], "ctx", 1)
            strips = [rotate(x, "head", s + 1) for s, x in enumerate(g[3:])]
    split_up = []
    for h in range(heads):
        before = [split_up[0][1], rim] if h else []
        split_up.append(split(h, ids, keep[h], other[h], before))
    away = [swap(split_up[h][1], order[h][0]) for h in range(heads)]

    per_head = 2
    pieces = []

    def attend(after):
        i = len(pieces)
        pieces.append(attention(i, FW // per_head, ids, query, keys, values, rim, after))
        return pieces[-1]

    att = attend([s[1] for s in split_up])
    pull, far = [], []
    for h in range(heads):
        more = strips[1:2] if h == heads - 1 else []
        p = total(split_up[h][0], away[h], [att] + pull + more)
        for b in order[h][1:-1]:
            p = total(p, swap(p, b), [])
        pull.append(p)
        far.append(swap(p, order[h][-1]))
        att = attend([p])
        if h == 0:
            att = attend([att])
    while len(pieces) < per_head * heads:
        att = attend([att])
    both = [x for h in range(heads) for x in (pull[h], far[h])]
    new = renorm(ids, tokens_all, fast_weights, both, [att, strips[0]] + strips[2:])

    cut = rows // 2
    merged, rest, weights = [], [], None
    for h in range(heads):
        b = order[h][0]
        near = swap(new[h], b)
        blocks = [new[h], near, swap(new[h], 1), swap(near, 1)]
        own = pieces[h * per_head : (h + 1) * per_head]
        m, r, weights = apply(h, heads, ids, query, own, blocks, cut, weights, [])
        merged.append(m)
        rest.append(r)
    to_right = [[shift(m, "head", 1) for m in merged]]
    to_left = [[shift(m, "head", -1) for m in merged]]

    near = stack([s[None] for s in strips], [merged[-1]])
    partial = partials(rest, out_weight, groups, [near])
    near = near.reshape((1,) + near.shape)
    after = near
    x = None
    for t in range(1, groups):
        right, left = [], []
        for h in range(heads):
            r, l, x = ring_step(
                t,
                groups,
                ids,
                step_at[t],
                tail_at,
                h,
                to_right[t - 1][h],
                to_left[t - 1][h],
                partial,
                x,
                [after],
            )
            after = l
            right.append(shift(r, "head", 1))
            left.append(shift(l, "head", -1))
            due = {(1, heads - 1): spread[:1], (groups - 1, heads - 1): spread[1:-1]}
            for b in due.get((t, h), []):
                near = stack([near, swap(near, b)], [after])
        to_right.append(right)
        to_left.append(left)
    out = gathered(
        ids,
        tail_at,
        merged,
        x,
        out_weight,
        near,
        swap(near, 1),
        rows,
        [after],
    )
    for h in range(heads):
        out = finish(ids, tail_at, h, to_right[-1][h], to_left[-1][h], partial, out)
    return (out, weights)


def solution(mesh):
    placed = (
        P("ctx", "head"),
        P("ctx", "head"),
        P("ctx", "head"),
        P("ctx", "head"),
        P("head", None, None, None),
        P("head", None),
    )
    return jax.shard_map(
        shards,
        mesh=mesh,
        in_specs=placed,
        out_specs=(P("ctx", "head"), P("head", None, None, None)),
        check_vma=False,
    )
```

```python
import functools
import math

import jax
import jax.numpy as jnp
from jax import lax
from jax.experimental import pallas as pl
from jax.experimental.pallas import tpu as pltpu
from jax.sharding import PartitionSpec as P

FW = 512
HEAD_DIM = 128
WINDOW = 256
LANES = 128
PER = FW // LANES
BLOCKS = 3 * PER
HALF = BLOCKS // 2
THIRD = BLOCKS // 4
TAIL = 16

base_rate = 0.05
BF = jnp.bfloat16
F32 = jnp.float32
NT = (((1,), (1,)), ((), ()))

CORE, FIRST, NEAR = 0, 1, 2

ANY = pl.BlockSpec(memory_space=pl.ANY)
SMEM = pl.BlockSpec(memory_space=pltpu.SMEM)


def room(mib):
    return pltpu.CompilerParams(vmem_limit_bytes=mib * 2**20)


def mm(a, b):
    return jnp.dot(a, b, preferred_element_type=F32)


def shift(block, axis, distance):
    n = lax.axis_size(axis)
    return lax.ppermute(block, axis, [(i, i + distance) for i in range(n) if 0 <= i + distance < n])


def rotate(block, axis, distance):
    n = lax.axis_size(axis)
    return lax.ppermute(block, axis, [(i, (i + distance) % n) for i in range(n)])


def swap(block, bit):
    n = lax.axis_size("ctx")
    return lax.ppermute(block, "ctx", [(i, i ^ bit) for i in range(n)])


def sigmoid(x):
    return 0.5 * jnp.tanh(0.5 * x) + 0.5


def full(shape):
    return pl.BlockSpec(shape, lambda *_: (0,) * len(shape))


def cost(microseconds):
    return pl.CostEstimate(
        flops=int(microseconds * 0.12e9), bytes_accessed=0, transcendentals=0
    )


def strip_copy(ids_ref, at, w_hbm, o_ref, sem):
    share, width = o_ref.shape
    rows = pl.ds(pl.multiple_of(ids_ref[at] * share, share), share)
    cols = pl.ds(pl.multiple_of(ids_ref[at + 1] * width, width), width)
    return pltpu.make_async_copy(w_hbm.at[rows, cols], o_ref, sem)


def split_rows(x):
    hi = x.astype(BF).astype(F32)
    mid = (x - hi).astype(BF).astype(F32)
    lo = x - hi - mid
    row = lax.broadcasted_iota(jnp.int32, (TAIL, LANES), 0)
    return jnp.where(row == 0, hi, jnp.where(row == 1, mid, jnp.where(row == 2, lo, 0.0))).astype(BF)


def join_rows(tail):
    return jnp.sum(tail.astype(F32), axis=0, keepdims=True)


def grads_kernel(h, at, ids_ref, code_ref, k_ref, v_ref, w_ref, *refs):
    lhs, rhs, sem = refs[-3:]
    copies = []
    if h == 0:
        k_hbm, v_hbm, ow_hbm, keep_ref, send_ref, rim_ref = refs[:6]
        last = pl.ds(k_hbm.shape[0] - WINDOW, WINDOW)
        copies = [
            pltpu.make_async_copy(k_hbm.at[last, :], rim_ref.at[pl.ds(0, WINDOW), :], sem.at[0]),
            pltpu.make_async_copy(
                v_hbm.at[last, :], rim_ref.at[pl.ds(WINDOW, WINDOW), :], sem.at[1]
            ),
        ] + [
            strip_copy(ids_ref, at + 2 * i, ow_hbm, strip_ref, sem.at[2 + i])
            for i, strip_ref in enumerate(refs[6:-3])
        ]
    else:
        keep_ref, send_ref = refs[-5:-3]
    for copy in copies:
        copy.start()
    rows = k_ref.shape[0]
    tile = min(256, rows)
    wide = 2 * LANES
    codes = code_ref[h : h + 1, :].astype(F32) * 2.0 ** (-14)
    for t in range(rows // tile):
        sl = pl.ds(t * tile, tile)
        k = k_ref[sl, :]
        rate = jnp.broadcast_to(codes[:, t * tile : (t + 1) * tile], (LANES, tile)).T
        rate = jnp.concatenate([rate] * PER, axis=1)
        push = (rate * v_ref[sl, :].astype(F32)).astype(BF)
        rhs[sl, 2 * FW :] = push
        for j in range(FW // wide):
            cs = slice(j * wide, (j + 1) * wide)
            gate = mm(k, w_ref[0, 0, :, cs])
            up = mm(k, w_ref[0, 1, :, cs])
            back = lax.dot_general(push, w_ref[0, 2, cs, :], NT, preferred_element_type=F32)
            s = sigmoid(gate)
            gs = gate * s
            lhs[FW + j * wide : FW + (j + 1) * wide, sl] = (gs * up).astype(BF).T
            rhs[sl, cs] = (back * up * (s + gs * (1.0 - s))).astype(BF)
            rhs[sl, FW + j * wide : FW + (j + 1) * wide] = (back * gs).astype(BF)
    lhs[:FW, :] = k_ref[...].T
    tail = split_rows(jnp.broadcast_to(jnp.sum(codes, axis=1, keepdims=True), (1, LANES)))
    pairs = HALF // 2
    for ref, half in ((send_ref, 1 - ids_ref[CORE]), (keep_ref, ids_ref[CORE])):
        ref[pl.ds(HALF * FW, TAIL), :] = tail
        for i in range(pairs):
            pair = half * pairs + i
            left = (pair >= 2 * FW // wide).astype(jnp.int32) * FW
            left = lhs[pl.ds(pl.multiple_of(left, FW), FW), :]
            right = rhs[:, pl.ds(pl.multiple_of(pair * wide, wide), wide)]
            r = mm(left, right).astype(BF)
            ref[pl.ds(2 * i * FW, FW), :] = r[:, :LANES]
            ref[pl.ds((2 * i + 1) * FW, FW), :] = r[:, LANES:]
    for copy in copies:
        copy.wait()


def grads(h, at, ids, codes, keys, values, fast_weights, out_weight, strips, after):
    rows, feats = keys.shape
    shape = (HALF * FW + TAIL, LANES)
    outs = [shape, shape] + ([(2 * WINDOW, feats)] + strips if h == 0 else [])
    more = [keys, values, out_weight] if h == 0 else after
    col = pl.BlockSpec((rows, FW), lambda i: (0, h))
    return pl.pallas_call(
        functools.partial(grads_kernel, h, at),
        grid=(1,),
        in_specs=[
            SMEM,
            full(codes.shape),
            col,
            col,
            pl.BlockSpec((1, 3, FW, FW), lambda i: (h, 0, 0, 0)),
        ]
        + [ANY] * len(more),
        out_specs=[full(x) for x in outs],
        out_shape=[jax.ShapeDtypeStruct(x, BF) for x in outs],
        scratch_shapes=[
            pltpu.VMEM((2 * FW, rows), BF),
            pltpu.VMEM((rows, 3 * FW), BF),
            pltpu.SemaphoreType.DMA((2 + len(strips),)),
        ],
        compiler_params=room(58),
        cost_estimate=cost(8 * rows / 1024),
    )(ids, codes, keys, values, fast_weights, *more)


def fetch(refs, scratch, sem):
    copies = [pltpu.make_async_copy(r, scratch.at[i], sem.at[i]) for i, r in enumerate(refs)]
    for c in copies:
        c.start()
    for c in copies:
        c.wait()


def pair(x):
    return [pltpu.VMEM((2,) + x.shape, x.dtype), pltpu.SemaphoreType.DMA((2,))]


def split_kernel(h, ids_ref, keep_hbm, other_hbm, *refs):
    keep_out, send_out, both, sem = refs[-4:]
    fetch((keep_hbm, other_hbm), both, sem)
    keep_ref, other_ref = both.at[0], both.at[1]
    n = THIRD * FW
    bit = ids_ref[NEAR + h]
    mine = pl.ds(pl.multiple_of(bit * n, n), n)
    theirs = pl.ds(pl.multiple_of((1 - bit) * n, n), n)
    keep_out[pl.ds(0, n), :] = keep_ref[mine, :] + other_ref[mine, :]
    send_out[pl.ds(0, n), :] = keep_ref[theirs, :] + other_ref[theirs, :]
    tail = pl.ds(HALF * FW, TAIL)
    rate = split_rows(join_rows(keep_ref[tail, :]) + join_rows(other_ref[tail, :]))
    keep_out[pl.ds(n, TAIL), :] = rate
    send_out[pl.ds(n, TAIL), :] = rate


def split(h, ids, keep, other, after):
    shape = (THIRD * FW + TAIL, LANES)
    out = jax.ShapeDtypeStruct(shape, BF)
    return pl.pallas_call(
        functools.partial(split_kernel, h),
        grid=(1,),
        in_specs=[SMEM] + [ANY] * (2 + len(after)),
        out_specs=[full(shape), full(shape)],
        out_shape=[out, out],
        scratch_shapes=pair(keep),
        compiler_params=room(12),
        cost_estimate=cost(0.9),
    )(ids, keep, other, *after)


def total_kernel(a_hbm, b_hbm, *rest):
    o_ref, both, sem = rest[-3:]
    fetch((a_hbm, b_hbm), both, sem)
    a_ref, b_ref = both.at[0], both.at[1]
    n = THIRD * FW
    o_ref[pl.ds(0, n), :] = a_ref[pl.ds(0, n), :] + b_ref[pl.ds(0, n), :]
    tail = pl.ds(n, TAIL)
    o_ref[tail, :] = split_rows(join_rows(a_ref[tail, :]) + join_rows(b_ref[tail, :]))


def total(a, b, after):
    return pl.pallas_call(
        total_kernel,
        grid=(1,),
        in_specs=[ANY] * (2 + len(after)),
        out_specs=full(a.shape),
        out_shape=jax.ShapeDtypeStruct(a.shape, BF),
        scratch_shapes=pair(a),
        compiler_params=room(8),
        cost_estimate=cost(0.5),
    )(a, b, *after)


def renorm_kernel(heads, tokens_all, ids_ref, base_ref, *refs):
    outs, (both, sem) = refs[-2 - heads : -2], refs[-2:]
    fetch(refs[: 2 * heads], both, sem)
    tail = pl.ds(THIRD * FW, TAIL)
    for h in range(heads):
        a_ref, b_ref = both.at[2 * h], both.at[2 * h + 1]
        start = ids_ref[CORE] * HALF + ids_ref[NEAR + h] * THIRD
        rate_sum = join_rows(a_ref[tail, :]) + join_rows(b_ref[tail, :])
        step = base_rate / (math.sqrt(tokens_all) * (rate_sum / tokens_all))
        for i in range(THIRD):
            sl = pl.ds(i * FW, FW)
            pull = a_ref[sl, :].astype(F32) + b_ref[sl, :].astype(F32)
            at = start + i
            col = pl.ds(pl.multiple_of((at % PER) * LANES, LANES), LANES)
            base = base_ref[h, at // PER, :, col].astype(F32)
            updated = base + step * pull
            old = jnp.sqrt(jnp.sum(base * base, axis=0, keepdims=True) + 1e-06)
            new = jnp.sqrt(jnp.sum(updated * updated, axis=0, keepdims=True) + 1e-06)
            outs[h][i] = (updated * (old / new)).astype(BF)


def renorm(ids, tokens_all, fast_weights, pulls, after):
    heads, one = fast_weights.shape[0], pulls[0].shape
    shape = (THIRD, FW, LANES)
    return pl.pallas_call(
        functools.partial(renorm_kernel, heads, tokens_all),
        grid=(1,),
        in_specs=[SMEM, full(fast_weights.shape)] + [ANY] * (len(pulls) + len(after)),
        out_specs=[full(shape)] * heads,
        out_shape=[jax.ShapeDtypeStruct(shape, BF)] * heads,
        scratch_shapes=[
            pltpu.VMEM((2 * heads,) + one, BF),
            pltpu.SemaphoreType.DMA((2 * heads,)),
        ],
        compiler_params=room(24),
        cost_estimate=cost(2.1),
    )(ids, fast_weights, *pulls, *after)


def attn_kernel(ids_ref, q_ref, k_ref, v_ref, rim_ref, *rest):
    o_ref = rest[-1]
    rows = q_ref.shape[0]
    w, d = WINDOW, HEAD_DIM
    row = lax.broadcasted_iota(jnp.int32, (w, w), 0)
    col = lax.broadcasted_iota(jnp.int32, (w, w), 1)
    own = col <= row
    factor = math.log2(math.e) / math.sqrt(d)
    has_prev = ids_ref[FIRST] == 0
    ones = jnp.ones((2 * w, LANES), BF)
    for h in range(q_ref.shape[1] // d):
        cs = slice(h * d, (h + 1) * d)
        for b in range(rows // w):
            sl = pl.ds(b * w, w)
            if b == 0:
                k2 = jnp.concatenate([rim_ref[:w, cs], k_ref[sl, cs]], axis=0)
                v2 = jnp.concatenate([rim_ref[w:, cs], v_ref[sl, cs]], axis=0)
            else:
                both = pl.ds((b - 1) * w, 2 * w)
                k2, v2 = k_ref[both, cs], v_ref[both, cs]
            s2 = lax.dot_general(q_ref[sl, cs], k2, NT, preferred_element_type=F32)
            prev = s2[:, :w]
            if b == 0:
                prev = jnp.where(has_prev, prev, -1e30)
            s = jnp.where(own, s2[:, w:], prev)
            e = jnp.exp2((s - jnp.max(s, axis=1, keepdims=True)) * factor).astype(BF)
            zero = jnp.zeros_like(e)
            e2 = jnp.concatenate([jnp.where(own, zero, e), jnp.where(own, e, zero)], axis=1)
            o = mm(e2, jnp.concatenate([v2, ones], axis=1))
            o_ref[sl, cs] = (o[:, :d] / o[:, d:]).astype(o_ref.dtype)


def attention(piece, width, ids, query, keys, values, rim, after):
    rows = query.shape[0]
    col = pl.BlockSpec((rows, width), lambda i: (0, piece))
    of_rim = pl.BlockSpec((2 * WINDOW, width), lambda i: (0, piece))
    return pl.pallas_call(
        attn_kernel,
        grid=(1,),
        in_specs=[SMEM, col, col, col, of_rim] + [ANY] * len(after),
        out_specs=full((rows, width)),
        out_shape=jax.ShapeDtypeStruct((rows, width), BF),
        compiler_params=room(16),
        cost_estimate=cost(2.1 * rows * width / 2**18),
    )(ids, query, keys, values, rim, *after)


def apply_tile(q, att, weights, act):
    wide = 2 * LANES
    rows = q.shape[0]
    for j in range(FW // wide):
        cs = slice(j * wide, (j + 1) * wide)
        gate = mm(q, weights[0, :, cs])
        up = mm(q, weights[1, :, cs])
        act[:rows, cs] = (gate * sigmoid(gate) * up).astype(BF)
    y = mm(act[:rows, :], weights[2])
    y = y * lax.rsqrt(jnp.mean(y * y, axis=1, keepdims=True) + 1e-06)
    return (att.astype(F32) + y).astype(BF)


def apply_kernel(h, pieces, ids_ref, q_hbm, *refs):
    att_hbm, refs = refs[:pieces], refs[pieces:]
    blocks = refs[:4]
    lo_ref, hi_ref, nw_hbm, q, att, nw, act, sem, bsem, osem = refs[-10:]
    rows = q.shape[0]
    core, near = ids_ref[CORE], ids_ref[NEAR + h]
    copies = [pltpu.make_async_copy(q_hbm.at[:, pl.ds(h * FW, FW)], q, sem.at[0])]
    for i, a in enumerate(att_hbm):
        to = att.at[:, pl.ds(i * a.shape[1], a.shape[1])]
        copies.append(pltpu.make_async_copy(a, to, sem.at[1 + i]))
    for n, src in enumerate(blocks):
        half, third = core ^ (n // 2), near ^ (n % 2)
        for i in range(THIRD):
            b = half * HALF + third * THIRD + i
            col = pl.ds(pl.multiple_of((b % PER) * LANES, LANES), LANES)
            dst = nw.at[b // PER, :, col]
            copies.append(pltpu.make_async_copy(src.at[i], dst, bsem.at[n, i]))
    for c in copies:
        c.start()
    for c in copies:
        c.wait()
    out = pltpu.make_async_copy(nw, nw_hbm.at[h], osem)
    out.start()
    cut = lo_ref.shape[0]
    for ref, start in ((lo_ref, 0), (hi_ref, cut)):
        sl = pl.ds(start, ref.shape[0])
        ref[...] = apply_tile(q[sl, :], att[sl, :], nw, act)
    out.wait()


def apply(h, heads, ids, query, attended, blocks, cut, whole, after):
    rows, pieces = query.shape[0], len(attended)
    shape = (heads, 3, FW, FW)
    extra = ([] if whole is None else [whole]) + after
    alias = {} if whole is None else {2 + pieces + len(blocks): 2}
    sizes = [(cut, FW), (rows - cut, FW)]
    return pl.pallas_call(
        functools.partial(apply_kernel, h, pieces),
        grid=(1,),
        in_specs=[SMEM] + [ANY] * (1 + pieces + len(blocks) + len(extra)),
        out_specs=[full(x) for x in sizes] + [ANY],
        out_shape=[jax.ShapeDtypeStruct(x, BF) for x in sizes + [shape]],
        input_output_aliases=alias,
        scratch_shapes=[
            pltpu.VMEM((rows, FW), BF),
            pltpu.VMEM((rows, FW), BF),
            pltpu.VMEM((3, FW, FW), BF),
            pltpu.VMEM((max(cut, rows - cut), FW), BF),
            pltpu.SemaphoreType.DMA((1 + pieces,)),
            pltpu.SemaphoreType.DMA((4, THIRD)),
            pltpu.SemaphoreType.DMA,
        ],
        compiler_params=room(20),
        cost_estimate=cost(3.3 * rows / 1024),
    )(ids, query, *attended, *blocks, *extra)


def joined(refs):
    return jnp.concatenate([r[...] for r in refs], axis=1)


def partial_kernel(heads, *refs):
    x_refs, w_ref = refs[:heads], refs[heads]
    o_ref, x = refs[-2:]

    @pl.when(pl.program_id(0) == 0)
    def _():
        for h in range(heads):
            x[:, h * FW : (h + 1) * FW] = x_refs[h][...]

    o_ref[0] = mm(x[...], w_ref[...]).astype(BF)


def partials(merged, out_weight, groups, after):
    rows, heads = merged[0].shape[0], len(merged)
    feats, width = out_weight.shape[0], out_weight.shape[1] // groups
    return pl.pallas_call(
        functools.partial(partial_kernel, heads),
        grid=(groups,),
        in_specs=[full(m.shape) for m in merged]
        + [pl.BlockSpec((feats, width), lambda d: (0, d))]
        + [ANY] * len(after),
        out_specs=pl.BlockSpec((1, rows, width), lambda d: (d, 0, 0)),
        out_shape=jax.ShapeDtypeStruct((groups, rows, width), BF),
        scratch_shapes=[pltpu.VMEM((rows, feats), BF)],
        compiler_params=room(24),
        cost_estimate=cost(1 * rows / 512),
    )(*merged, out_weight, *after)


def stack_kernel(n, *refs):
    o_ref = refs[-1]
    at = 0
    for r in refs[:n]:
        o_ref[pl.ds(at, r.shape[0])] = r[...]
        at += r.shape[0]


def stack(parts, after):
    shape = (sum(p.shape[0] for p in parts),) + parts[0].shape[1:]
    return pl.pallas_call(
        functools.partial(stack_kernel, len(parts)),
        grid=(1,),
        in_specs=[full(p.shape) for p in parts] + [ANY] * len(after),
        out_specs=full(shape),
        out_shape=jax.ShapeDtypeStruct(shape, BF),
        compiler_params=room(20),
        cost_estimate=cost(0.1),
    )(*parts, *after)


def ring_kernel(t, n, at, tail, wave, ids_ref, right_hbm, left_hbm, p_hbm, *refs):
    ro_ref, lo_ref, x_hbm, got, own, sem, xsem = refs[-7:]
    width = right_hbm.shape[1]
    cols = pl.ds(wave * width, width)
    copies = [
        pltpu.make_async_copy(right_hbm, got.at[0], sem.at[0]),
        pltpu.make_async_copy(p_hbm.at[ids_ref[at], :, cols], own.at[0], sem.at[1]),
        pltpu.make_async_copy(left_hbm, got.at[1], sem.at[2]),
        pltpu.make_async_copy(p_hbm.at[ids_ref[at + 1], :, cols], own.at[1], sem.at[3]),
    ]
    for c in copies:
        c.start()
    zero = jnp.zeros((), BF)
    for i, ref in enumerate((ro_ref, lo_ref)):
        copies[2 * i].wait()
        copies[2 * i + 1].wait()
        ref[...] = got[i] + jnp.where(ids_ref[at + 2 + i] > 0, own[i], zero)
    for i, (slot, here) in enumerate(((t - 1, t <= ids_ref[tail]), (n - 1 - t, t < n - ids_ref[tail]))):

        @pl.when(here)
        def _():
            keep = pltpu.make_async_copy(got.at[i], x_hbm.at[slot, :, cols], xsem.at[i])
            keep.start()
            keep.wait()


def ring_step(t, n, ids, at, tail, wave, right, left, partial, x, after):
    out = jax.ShapeDtypeStruct(right.shape, BF)
    kept = jax.ShapeDtypeStruct((n - 1, right.shape[0], partial.shape[2]), BF)
    more = ([] if x is None else [x]) + after
    return pl.pallas_call(
        functools.partial(ring_kernel, t, n, at, tail, wave),
        grid=(1,),
        in_specs=[SMEM] + [ANY] * (3 + len(more)),
        out_specs=[full(right.shape)] * 2 + [ANY],
        out_shape=[out, out, kept],
        input_output_aliases={} if x is None else {4: 2},
        scratch_shapes=[
            pltpu.VMEM((2,) + right.shape, BF),
            pltpu.VMEM((2,) + right.shape, BF),
            pltpu.SemaphoreType.DMA((4,)),
            pltpu.SemaphoreType.DMA((2,)),
        ],
        compiler_params=room(12),
        cost_estimate=cost(30),
    )(ids, right, left, partial, *more)


def gathered_kernel(n, heads, parts, at, ids_ref, *refs):
    own_refs, refs = refs[:heads], refs[heads:]
    x_hbm, refs = refs[0], refs[1:]
    w_ref, near_ref, far_ref = refs[:3]
    o_ref, x, cols, acc, xsem, wsem = refs[-6:]
    share = near_ref.shape[2]
    near = near_ref.shape[0]

    def each(steps, do):
        for t in steps:
            do(t, pltpu.make_async_copy(x_hbm.at[t], x.at[t], xsem.at[t]))
            for p in range(parts):
                src = near_ref.at[p, t] if p < near else far_ref.at[p - near, t]
                to = ids_ref[at + 1 + p] * share
                to = pl.ds(pl.multiple_of(to, share), share)
                do(t, pltpu.make_async_copy(src, cols.at[t, to, :], wsem.at[t, p]))

    each(range(n - 1), lambda t, c: c.start())
    acc[...] = mm(joined(own_refs), w_ref[...])
    for t in range(n - 1):
        each((t,), lambda t, c: c.wait())
        if t < n - 2:
            acc[...] += mm(x[t], cols[t])
        else:
            o_ref[...] = (acc[...] + mm(x[t], cols[t])).astype(BF)


def gathered(ids, at, merged, x, out_weight, near, far, rows_all, after):
    n, heads, parts = x.shape[0] + 1, len(merged), near.shape[0] + far.shape[0]
    rows, feats = merged[0].shape[0], out_weight.shape[0]
    width = out_weight.shape[1] // n
    return pl.pallas_call(
        functools.partial(gathered_kernel, n, heads, parts, at),
        grid_spec=pltpu.PrefetchScalarGridSpec(
            num_scalar_prefetch=1,
            grid=(1,),
            in_specs=[full(m.shape) for m in merged]
            + [ANY]
            + [pl.BlockSpec((feats, width), lambda i, s: (0, s[at])), ANY, ANY]
            + [ANY] * len(after),
            out_specs=pl.BlockSpec((rows, width), lambda i, s: (0, 0)),
            scratch_shapes=[
                pltpu.VMEM((n - 1, rows, feats), BF),
                pltpu.VMEM((n - 1, feats, width), BF),
                pltpu.VMEM((rows, width), F32),
                pltpu.SemaphoreType.DMA((n - 1,)),
                pltpu.SemaphoreType.DMA((n - 1, parts)),
            ],
        ),
        out_shape=jax.ShapeDtypeStruct((rows_all, width), BF),
        compiler_params=room(48),
        cost_estimate=cost(9 * rows / 512),
    )(
        ids, *merged, x, out_weight, near, far, *after
    )


def finish_kernel(at, wave, ids_ref, right_hbm, left_hbm, p_hbm, out_in, o_hbm, got, own, sem):
    del out_in
    rows, width = own.shape
    cols = pl.ds(wave * width, width)
    copies = [
        pltpu.make_async_copy(right_hbm, got.at[0], sem.at[0]),
        pltpu.make_async_copy(left_hbm, got.at[1], sem.at[1]),
        pltpu.make_async_copy(p_hbm.at[ids_ref[at], :, cols], own, sem.at[2]),
    ]
    for c in copies:
        c.start()
    for c in copies:
        c.wait()
    total = own[...].astype(F32) + (got[0].astype(F32) + got[1].astype(F32))
    own[...] = total.astype(BF)
    last = pl.ds(o_hbm.shape[0] - rows, rows)
    out = pltpu.make_async_copy(own, o_hbm.at[last, cols], sem.at[3])
    out.start()
    out.wait()


def finish(ids, at, wave, right, left, partial, out):
    return pl.pallas_call(
        functools.partial(finish_kernel, at, wave),
        grid=(1,),
        in_specs=[SMEM] + [ANY] * 4,
        out_specs=ANY,
        out_shape=jax.ShapeDtypeStruct(out.shape, BF),
        input_output_aliases={4: 0},
        scratch_shapes=[
            pltpu.VMEM((2,) + right.shape, BF),
            pltpu.VMEM(right.shape, BF),
            pltpu.SemaphoreType.DMA((4,)),
        ],
        compiler_params=room(12),
        cost_estimate=cost(30),
    )(ids, right, left, partial, out)


def scalars(*xs):
    return jnp.stack([jnp.asarray(x, jnp.int32) for x in xs])


def shards(query, keys, values, lr_code, fast_weights, out_weight):
    rows, feats = query.shape
    contexts, groups = lax.axis_size("ctx"), lax.axis_size("head")
    c, z = lax.axis_index("ctx"), lax.axis_index("head")
    tokens_all = rows * contexts
    heads = fast_weights.shape[0]
    bits = [1 << i for i in range(contexts.bit_length() - 1)]
    bit_of = {b: (c // b) % 2 for b in bits}
    order = [[bits[1 + h % 2]] for h in range(heads)]
    order = [o + [b for b in bits[1:] if b != o[0]] for o in order]
    spread = bits[2::-1]
    places = [0]
    for b in spread:
        places = places + [p ^ b for p in places]
    share, width = feats // len(places), out_weight.shape[1] // groups
    ids = [bit_of[1], c == 0] + [bit_of[o[0]] for o in order]
    step_at = [len(ids) + 4 * (t - 1) for t in range(groups)]
    for t in range(1, groups):
        ids += [(z - t) % groups, (z + t) % groups, t > z, t > groups - 1 - z]
    tail_at = len(ids)
    ids += [z] + [(c % len(places)) ^ p for p in places]
    strip_at = len(ids)
    for s in range(1, groups):
        ids += [c % len(places), (z + s) % groups]
    ids = scalars(*ids)

    keep, other = [], []
    for h in range(heads):
        g = grads(
            h,
            strip_at,
            ids,
            lr_code.T,
            keys,
            values,
            fast_weights,
            out_weight,
            [(share, width)] * (groups - 1),
            keep[-1:],
        )
        keep.append(g[0])
        other.append(swap(g[1], 1))
        if h == 0:
            rim = shift(g[2], "ctx", 1)
            strips = [rotate(x, "head", s + 1) for s, x in enumerate(g[3:])]
    split_up = []
    for h in range(heads):
        before = [split_up[0][1], rim] if h else []
        split_up.append(split(h, ids, keep[h], other[h], before))
    away = [swap(split_up[h][1], order[h][0]) for h in range(heads)]

    per_head = 2
    pieces = []

    def attend(after):
        i = len(pieces)
        pieces.append(attention(i, FW // per_head, ids, query, keys, values, rim, after))
        return pieces[-1]

    att = attend([s[1] for s in split_up])
    pull, far = [], []
    for h in range(heads):
        more = strips[1:2] if h == heads - 1 else []
        p = total(split_up[h][0], away[h], [att] + pull + more)
        for b in order[h][1:-1]:
            p = total(p, swap(p, b), [])
        pull.append(p)
        far.append(swap(p, order[h][-1]))
        att = attend([p])
        if h == 0:
            att = attend([att])
    while len(pieces) < per_head * heads:
        att = attend([att])
    both = [x for h in range(heads) for x in (pull[h], far[h])]
    new = renorm(ids, tokens_all, fast_weights, both, [att, strips[0]] + strips[2:])

    cut = rows // 2
    merged, rest, weights = [], [], None
    for h in range(heads):
        b = order[h][0]
        near = swap(new[h], b)
        blocks = [new[h], near, swap(new[h], 1), swap(near, 1)]
        own = pieces[h * per_head : (h + 1) * per_head]
        m, r, weights = apply(h, heads, ids, query, own, blocks, cut, weights, [])
        merged.append(m)
        rest.append(r)
    to_right = [[shift(m, "head", 1) for m in merged]]
    to_left = [[shift(m, "head", -1) for m in merged]]

    near = stack([s[None] for s in strips], [merged[-1]])
    partial = partials(rest, out_weight, groups, [near])
    near = near.reshape((1,) + near.shape)
    after = near
    x = None
    for t in range(1, groups):
        right, left = [], []
        for h in range(heads):
            r, l, x = ring_step(
                t,
                groups,
                ids,
                step_at[t],
                tail_at,
                h,
                to_right[t - 1][h],
                to_left[t - 1][h],
                partial,
                x,
                [after],
            )
            after = l
            right.append(shift(r, "head", 1))
            left.append(shift(l, "head", -1))
            due = {(1, heads - 1): spread[:1], (groups - 2, heads - 1): spread[1:-1]}
            for b in due.get((t, h), []):
                near = stack([near, swap(near, b)], [after])
        to_right.append(right)
        to_left.append(left)
    out = gathered(
        ids,
        tail_at,
        merged,
        x,
        out_weight,
        near,
        swap(near, 1),
        rows,
        [after],
    )
    for h in range(heads):
        out = finish(ids, tail_at, h, to_right[-1][h], to_left[-1][h], partial, out)
    return (out, weights)


def solution(mesh):
    placed = (
        P("ctx", "head"),
        P("ctx", "head"),
        P("ctx", "head"),
        P("ctx", "head"),
        P("head", None, None, None),
        P("head", None),
    )
    return jax.shard_map(
        shards,
        mesh=mesh,
        in_specs=placed,
        out_specs=(P("ctx", "head"), P("head", None, None, None)),
        check_vma=False,
    )
```

```python
import functools
import math

import jax
import jax.numpy as jnp
from jax import lax
from jax.experimental import pallas as pl
from jax.experimental.pallas import tpu as pltpu
from jax.sharding import PartitionSpec as P

FW = 512
HEAD_DIM = 128
WINDOW = 256
LANES = 128
PER = FW // LANES
BLOCKS = 3 * PER
HALF = BLOCKS // 2
THIRD = BLOCKS // 4
TAIL = 16

base_rate = 0.05
BF = jnp.bfloat16
F32 = jnp.float32
NT = (((1,), (1,)), ((), ()))

CORE, FIRST, NEAR = 0, 1, 2

ANY = pl.BlockSpec(memory_space=pl.ANY)
SMEM = pl.BlockSpec(memory_space=pltpu.SMEM)


def room(mib):
    return pltpu.CompilerParams(vmem_limit_bytes=mib * 2**20)


def mm(a, b):
    return jnp.dot(a, b, preferred_element_type=F32)


def shift(block, axis, distance):
    n = lax.axis_size(axis)
    return lax.ppermute(block, axis, [(i, i + distance) for i in range(n) if 0 <= i + distance < n])


def rotate(block, axis, distance):
    n = lax.axis_size(axis)
    return lax.ppermute(block, axis, [(i, (i + distance) % n) for i in range(n)])


def swap(block, bit):
    n = lax.axis_size("ctx")
    return lax.ppermute(block, "ctx", [(i, i ^ bit) for i in range(n)])


def sigmoid(x):
    return 0.5 * jnp.tanh(0.5 * x) + 0.5


def full(shape):
    return pl.BlockSpec(shape, lambda *_: (0,) * len(shape))


def cost(microseconds):
    return pl.CostEstimate(
        flops=int(microseconds * 0.12e9), bytes_accessed=0, transcendentals=0
    )


def strip_copy(ids_ref, at, w_hbm, o_ref, sem):
    share, width = o_ref.shape
    rows = pl.ds(pl.multiple_of(ids_ref[at] * share, share), share)
    cols = pl.ds(pl.multiple_of(ids_ref[at + 1] * width, width), width)
    return pltpu.make_async_copy(w_hbm.at[rows, cols], o_ref, sem)


def split_rows(x):
    hi = x.astype(BF).astype(F32)
    mid = (x - hi).astype(BF).astype(F32)
    lo = x - hi - mid
    row = lax.broadcasted_iota(jnp.int32, (TAIL, LANES), 0)
    return jnp.where(row == 0, hi, jnp.where(row == 1, mid, jnp.where(row == 2, lo, 0.0))).astype(BF)


def join_rows(tail):
    return jnp.sum(tail.astype(F32), axis=0, keepdims=True)


def grads_kernel(h, at, ids_ref, code_ref, k_ref, v_ref, w_ref, *refs):
    copies, outs = [], []
    if h == 0:
        k_hbm, v_hbm, ow_hbm, keep_ref, send_ref = refs[:5]
        n = (len(refs) - 9) // 2
        out_hbm, held, (lhs, rhs, sem, osem) = refs[5 : 5 + n], refs[5 + n : 5 + 2 * n], refs[-4:]
        last = pl.ds(k_hbm.shape[0] - WINDOW, WINDOW)
        copies = [
            pltpu.make_async_copy(k_hbm.at[last, :], held[0].at[pl.ds(0, WINDOW), :], sem.at[0]),
            pltpu.make_async_copy(
                v_hbm.at[last, :], held[0].at[pl.ds(WINDOW, WINDOW), :], sem.at[1]
            ),
        ] + [
            strip_copy(ids_ref, at + 2 * i, ow_hbm, strip_ref, sem.at[2 + i])
            for i, strip_ref in enumerate(held[1:])
        ]
        outs = [pltpu.make_async_copy(a, b, osem.at[i]) for i, (a, b) in enumerate(zip(held, out_hbm))]
    else:
        keep_ref, send_ref, lhs, rhs = refs[-4:]
    for copy in copies:
        copy.start()
    rows = k_ref.shape[0]
    tile = min(256, rows)
    wide = 2 * LANES
    codes = code_ref[h : h + 1, :].astype(F32) * 2.0 ** (-14)
    for t in range(rows // tile):
        sl = pl.ds(t * tile, tile)
        k = k_ref[sl, :]
        rate = jnp.broadcast_to(codes[:, t * tile : (t + 1) * tile], (LANES, tile)).T
        rate = jnp.concatenate([rate] * PER, axis=1)
        push = (rate * v_ref[sl, :].astype(F32)).astype(BF)
        rhs[sl, 2 * FW :] = push
        for j in range(FW // wide):
            cs = slice(j * wide, (j + 1) * wide)
            gate = mm(k, w_ref[0, 0, :, cs])
            up = mm(k, w_ref[0, 1, :, cs])
            back = lax.dot_general(push, w_ref[0, 2, cs, :], NT, preferred_element_type=F32)
            s = sigmoid(gate)
            gs = gate * s
            lhs[FW + j * wide : FW + (j + 1) * wide, sl] = (gs * up).astype(BF).T
            rhs[sl, cs] = (back * up * (s + gs * (1.0 - s))).astype(BF)
            rhs[sl, FW + j * wide : FW + (j + 1) * wide] = (back * gs).astype(BF)
        if t == 0:
            for copy in copies:
                copy.wait()
            for copy in outs:
                copy.start()
    lhs[:FW, :] = k_ref[...].T
    tail = split_rows(jnp.broadcast_to(jnp.sum(codes, axis=1, keepdims=True), (1, LANES)))
    pairs = HALF // 2
    for ref, half in ((send_ref, 1 - ids_ref[CORE]), (keep_ref, ids_ref[CORE])):
        ref[pl.ds(HALF * FW, TAIL), :] = tail
        for i in range(pairs):
            pair = half * pairs + i
            left = (pair >= 2 * FW // wide).astype(jnp.int32) * FW
            left = lhs[pl.ds(pl.multiple_of(left, FW), FW), :]
            right = rhs[:, pl.ds(pl.multiple_of(pair * wide, wide), wide)]
            r = mm(left, right).astype(BF)
            ref[pl.ds(2 * i * FW, FW), :] = r[:, :LANES]
            ref[pl.ds((2 * i + 1) * FW, FW), :] = r[:, LANES:]
    for copy in outs:
        copy.wait()


def grads(h, at, ids, codes, keys, values, fast_weights, out_weight, strips, after):
    rows, feats = keys.shape
    shape = (HALF * FW + TAIL, LANES)
    outs = [shape, shape] + ([(2 * WINDOW, feats)] + strips if h == 0 else [])
    more = [keys, values, out_weight] if h == 0 else after
    col = pl.BlockSpec((rows, FW), lambda i: (0, h))
    return pl.pallas_call(
        functools.partial(grads_kernel, h, at),
        grid=(1,),
        in_specs=[
            SMEM,
            full(codes.shape),
            col,
            col,
            pl.BlockSpec((1, 3, FW, FW), lambda i: (h, 0, 0, 0)),
        ]
        + [ANY] * len(more),
        out_specs=[full(x) for x in outs[:2]] + [ANY] * len(outs[2:]),
        out_shape=[jax.ShapeDtypeStruct(x, BF) for x in outs],
        scratch_shapes=[pltpu.VMEM(x, BF) for x in outs[2:]]
        + [pltpu.VMEM((2 * FW, rows), BF), pltpu.VMEM((rows, 3 * FW), BF)]
        + [pltpu.SemaphoreType.DMA((2 + i,)) for i in (len(strips), 0) if h == 0 and i]
        + [pltpu.SemaphoreType.DMA((1 + len(strips),)) for _ in range(1) if h == 0],
        compiler_params=room(58),
        cost_estimate=cost(8 * rows / 1024),
    )(ids, codes, keys, values, fast_weights, *more)


def fetch(refs, scratch, sem):
    copies = [pltpu.make_async_copy(r, scratch.at[i], sem.at[i]) for i, r in enumerate(refs)]
    for c in copies:
        c.start()
    for c in copies:
        c.wait()


def pair(x):
    return [pltpu.VMEM((2,) + x.shape, x.dtype), pltpu.SemaphoreType.DMA((2,))]


def split_kernel(h, ids_ref, keep_hbm, other_hbm, *refs):
    keep_out, send_out, both, sem = refs[-4:]
    fetch((keep_hbm, other_hbm), both, sem)
    keep_ref, other_ref = both.at[0], both.at[1]
    n = THIRD * FW
    bit = ids_ref[NEAR + h]
    mine = pl.ds(pl.multiple_of(bit * n, n), n)
    theirs = pl.ds(pl.multiple_of((1 - bit) * n, n), n)
    keep_out[pl.ds(0, n), :] = keep_ref[mine, :] + other_ref[mine, :]
    send_out[pl.ds(0, n), :] = keep_ref[theirs, :] + other_ref[theirs, :]
    tail = pl.ds(HALF * FW, TAIL)
    rate = split_rows(join_rows(keep_ref[tail, :]) + join_rows(other_ref[tail, :]))
    keep_out[pl.ds(n, TAIL), :] = rate
    send_out[pl.ds(n, TAIL), :] = rate


def split(h, ids, keep, other, after):
    shape = (THIRD * FW + TAIL, LANES)
    out = jax.ShapeDtypeStruct(shape, BF)
    return pl.pallas_call(
        functools.partial(split_kernel, h),
        grid=(1,),
        in_specs=[SMEM] + [ANY] * (2 + len(after)),
        out_specs=[full(shape), full(shape)],
        out_shape=[out, out],
        scratch_shapes=pair(keep),
        compiler_params=room(12),
        cost_estimate=cost(0.9),
    )(ids, keep, other, *after)


def total_kernel(a_hbm, b_hbm, *rest):
    o_ref, both, sem = rest[-3:]
    fetch((a_hbm, b_hbm), both, sem)
    a_ref, b_ref = both.at[0], both.at[1]
    n = THIRD * FW
    o_ref[pl.ds(0, n), :] = a_ref[pl.ds(0, n), :] + b_ref[pl.ds(0, n), :]
    tail = pl.ds(n, TAIL)
    o_ref[tail, :] = split_rows(join_rows(a_ref[tail, :]) + join_rows(b_ref[tail, :]))


def total(a, b, after):
    return pl.pallas_call(
        total_kernel,
        grid=(1,),
        in_specs=[ANY] * (2 + len(after)),
        out_specs=full(a.shape),
        out_shape=jax.ShapeDtypeStruct(a.shape, BF),
        scratch_shapes=pair(a),
        compiler_params=room(8),
        cost_estimate=cost(0.5),
    )(a, b, *after)


def renorm_kernel(heads, tokens_all, ids_ref, base_ref, *refs):
    outs, (both, sem) = refs[-2 - heads : -2], refs[-2:]
    fetch(refs[: 2 * heads], both, sem)
    tail = pl.ds(THIRD * FW, TAIL)
    for h in range(heads):
        a_ref, b_ref = both.at[2 * h], both.at[2 * h + 1]
        start = ids_ref[CORE] * HALF + ids_ref[NEAR + h] * THIRD
        rate_sum = join_rows(a_ref[tail, :]) + join_rows(b_ref[tail, :])
        step = base_rate / (math.sqrt(tokens_all) * (rate_sum / tokens_all))
        for i in range(THIRD):
            sl = pl.ds(i * FW, FW)
            pull = a_ref[sl, :].astype(F32) + b_ref[sl, :].astype(F32)
            at = start + i
            col = pl.ds(pl.multiple_of((at % PER) * LANES, LANES), LANES)
            base = base_ref[h, at // PER, :, col].astype(F32)
            updated = base + step * pull
            old = jnp.sqrt(jnp.sum(base * base, axis=0, keepdims=True) + 1e-06)
            new = jnp.sqrt(jnp.sum(updated * updated, axis=0, keepdims=True) + 1e-06)
            outs[h][i] = (updated * (old / new)).astype(BF)


def renorm(ids, tokens_all, fast_weights, pulls, after):
    heads, one = fast_weights.shape[0], pulls[0].shape
    shape = (THIRD, FW, LANES)
    return pl.pallas_call(
        functools.partial(renorm_kernel, heads, tokens_all),
        grid=(1,),
        in_specs=[SMEM, full(fast_weights.shape)] + [ANY] * (len(pulls) + len(after)),
        out_specs=[full(shape)] * heads,
        out_shape=[jax.ShapeDtypeStruct(shape, BF)] * heads,
        scratch_shapes=[
            pltpu.VMEM((2 * heads,) + one, BF),
            pltpu.SemaphoreType.DMA((2 * heads,)),
        ],
        compiler_params=room(24),
        cost_estimate=cost(2.1),
    )(ids, fast_weights, *pulls, *after)


def attn_kernel(ids_ref, q_ref, k_ref, v_ref, rim_ref, *rest):
    o_ref = rest[-1]
    rows = q_ref.shape[0]
    w, d = WINDOW, HEAD_DIM
    row = lax.broadcasted_iota(jnp.int32, (w, w), 0)
    col = lax.broadcasted_iota(jnp.int32, (w, w), 1)
    own = col <= row
    factor = math.log2(math.e) / math.sqrt(d)
    has_prev = ids_ref[FIRST] == 0
    ones = jnp.ones((2 * w, LANES), BF)
    for h in range(q_ref.shape[1] // d):
        cs = slice(h * d, (h + 1) * d)
        for b in range(rows // w):
            sl = pl.ds(b * w, w)
            if b == 0:
                k2 = jnp.concatenate([rim_ref[:w, cs], k_ref[sl, cs]], axis=0)
                v2 = jnp.concatenate([rim_ref[w:, cs], v_ref[sl, cs]], axis=0)
            else:
                both = pl.ds((b - 1) * w, 2 * w)
                k2, v2 = k_ref[both, cs], v_ref[both, cs]
            s2 = lax.dot_general(q_ref[sl, cs], k2, NT, preferred_element_type=F32)
            prev = s2[:, :w]
            if b == 0:
                prev = jnp.where(has_prev, prev, -1e30)
            s = jnp.where(own, s2[:, w:], prev)
            e = jnp.exp2((s - jnp.max(s, axis=1, keepdims=True)) * factor).astype(BF)
            zero = jnp.zeros_like(e)
            e2 = jnp.concatenate([jnp.where(own, zero, e), jnp.where(own, e, zero)], axis=1)
            o = mm(e2, jnp.concatenate([v2, ones], axis=1))
            o_ref[sl, cs] = (o[:, :d] / o[:, d:]).astype(o_ref.dtype)


def attention(piece, width, ids, query, keys, values, rim, after):
    rows = query.shape[0]
    col = pl.BlockSpec((rows, width), lambda i: (0, piece))
    of_rim = pl.BlockSpec((2 * WINDOW, width), lambda i: (0, piece))
    return pl.pallas_call(
        attn_kernel,
        grid=(1,),
        in_specs=[SMEM, col, col, col, of_rim] + [ANY] * len(after),
        out_specs=full((rows, width)),
        out_shape=jax.ShapeDtypeStruct((rows, width), BF),
        compiler_params=room(16),
        cost_estimate=cost(2.1 * rows * width / 2**18),
    )(ids, query, keys, values, rim, *after)


def apply_tile(q, att, weights, act):
    wide = 2 * LANES
    rows = q.shape[0]
    for j in range(FW // wide):
        cs = slice(j * wide, (j + 1) * wide)
        gate = mm(q, weights[0, :, cs])
        up = mm(q, weights[1, :, cs])
        act[:rows, cs] = (gate * sigmoid(gate) * up).astype(BF)
    y = mm(act[:rows, :], weights[2])
    y = y * lax.rsqrt(jnp.mean(y * y, axis=1, keepdims=True) + 1e-06)
    return (att.astype(F32) + y).astype(BF)


def apply_kernel(h, pieces, ids_ref, q_hbm, *refs):
    att_hbm, refs = refs[:pieces], refs[pieces:]
    blocks = refs[:4]
    lo_ref, hi_ref, nw_hbm, q, att, nw, act, sem, bsem, osem = refs[-10:]
    rows = q.shape[0]
    core, near = ids_ref[CORE], ids_ref[NEAR + h]
    copies = [pltpu.make_async_copy(q_hbm.at[:, pl.ds(h * FW, FW)], q, sem.at[0])]
    for i, a in enumerate(att_hbm):
        to = att.at[:, pl.ds(i * a.shape[1], a.shape[1])]
        copies.append(pltpu.make_async_copy(a, to, sem.at[1 + i]))
    for n, src in enumerate(blocks):
        half, third = core ^ (n // 2), near ^ (n % 2)
        for i in range(THIRD):
            b = half * HALF + third * THIRD + i
            col = pl.ds(pl.multiple_of((b % PER) * LANES, LANES), LANES)
            dst = nw.at[b // PER, :, col]
            copies.append(pltpu.make_async_copy(src.at[i], dst, bsem.at[n, i]))
    for c in copies:
        c.start()
    for c in copies:
        c.wait()
    out = pltpu.make_async_copy(nw, nw_hbm.at[h], osem)
    out.start()
    cut = lo_ref.shape[0]
    for ref, start in ((lo_ref, 0), (hi_ref, cut)):
        sl = pl.ds(start, ref.shape[0])
        ref[...] = apply_tile(q[sl, :], att[sl, :], nw, act)
    out.wait()


def apply(h, heads, ids, query, attended, blocks, cut, whole, after):
    rows, pieces = query.shape[0], len(attended)
    shape = (heads, 3, FW, FW)
    extra = ([] if whole is None else [whole]) + after
    alias = {} if whole is None else {2 + pieces + len(blocks): 2}
    sizes = [(cut, FW), (rows - cut, FW)]
    return pl.pallas_call(
        functools.partial(apply_kernel, h, pieces),
        grid=(1,),
        in_specs=[SMEM] + [ANY] * (1 + pieces + len(blocks) + len(extra)),
        out_specs=[full(x) for x in sizes] + [ANY],
        out_shape=[jax.ShapeDtypeStruct(x, BF) for x in sizes + [shape]],
        input_output_aliases=alias,
        scratch_shapes=[
            pltpu.VMEM((rows, FW), BF),
            pltpu.VMEM((rows, FW), BF),
            pltpu.VMEM((3, FW, FW), BF),
            pltpu.VMEM((max(cut, rows - cut), FW), BF),
            pltpu.SemaphoreType.DMA((1 + pieces,)),
            pltpu.SemaphoreType.DMA((4, THIRD)),
            pltpu.SemaphoreType.DMA,
        ],
        compiler_params=room(20),
        cost_estimate=cost(3.3 * rows / 1024),
    )(ids, query, *attended, *blocks, *extra)


def joined(refs):
    return jnp.concatenate([r[...] for r in refs], axis=1)


def partial_kernel(heads, *refs):
    x_refs, w_ref = refs[:heads], refs[heads]
    o_ref, x = refs[-2:]

    @pl.when(pl.program_id(0) == 0)
    def _():
        for h in range(heads):
            x[:, h * FW : (h + 1) * FW] = x_refs[h][...]

    o_ref[0] = mm(x[...], w_ref[...]).astype(BF)


def partials(merged, out_weight, groups, after):
    rows, heads = merged[0].shape[0], len(merged)
    feats, width = out_weight.shape[0], out_weight.shape[1] // groups
    return pl.pallas_call(
        functools.partial(partial_kernel, heads),
        grid=(groups,),
        in_specs=[full(m.shape) for m in merged]
        + [pl.BlockSpec((feats, width), lambda d: (0, d))]
        + [ANY] * len(after),
        out_specs=pl.BlockSpec((1, rows, width), lambda d: (d, 0, 0)),
        out_shape=jax.ShapeDtypeStruct((groups, rows, width), BF),
        scratch_shapes=[pltpu.VMEM((rows, feats), BF)],
        compiler_params=room(24),
        cost_estimate=cost(1 * rows / 512),
    )(*merged, out_weight, *after)


def stack_kernel(n, *refs):
    o_ref = refs[-1]
    at = 0
    for r in refs[:n]:
        o_ref[pl.ds(at, r.shape[0])] = r[...]
        at += r.shape[0]


def stack(parts, after):
    shape = (sum(p.shape[0] for p in parts),) + parts[0].shape[1:]
    return pl.pallas_call(
        functools.partial(stack_kernel, len(parts)),
        grid=(1,),
        in_specs=[full(p.shape) for p in parts] + [ANY] * len(after),
        out_specs=full(shape),
        out_shape=jax.ShapeDtypeStruct(shape, BF),
        compiler_params=room(20),
        cost_estimate=cost(0.1),
    )(*parts, *after)


def ring_kernel(t, n, at, tail, wave, ids_ref, right_hbm, left_hbm, p_hbm, *refs):
    ro_ref, lo_ref, x_hbm, got, own, sem, xsem = refs[-7:]
    width = right_hbm.shape[1]
    cols = pl.ds(wave * width, width)
    copies = [
        pltpu.make_async_copy(right_hbm, got.at[0], sem.at[0]),
        pltpu.make_async_copy(p_hbm.at[ids_ref[at], :, cols], own.at[0], sem.at[1]),
        pltpu.make_async_copy(left_hbm, got.at[1], sem.at[2]),
        pltpu.make_async_copy(p_hbm.at[ids_ref[at + 1], :, cols], own.at[1], sem.at[3]),
    ]
    for c in copies:
        c.start()
    zero = jnp.zeros((), BF)
    for i, ref in enumerate((ro_ref, lo_ref)):
        copies[2 * i].wait()
        copies[2 * i + 1].wait()
        ref[...] = got[i] + jnp.where(ids_ref[at + 2 + i] > 0, own[i], zero)
    for i, (slot, here) in enumerate(((t - 1, t <= ids_ref[tail]), (n - 1 - t, t < n - ids_ref[tail]))):

        @pl.when(here)
        def _():
            keep = pltpu.make_async_copy(got.at[i], x_hbm.at[slot, :, cols], xsem.at[i])
            keep.start()
            keep.wait()


def ring_step(t, n, ids, at, tail, wave, right, left, partial, x, after):
    out = jax.ShapeDtypeStruct(right.shape, BF)
    kept = jax.ShapeDtypeStruct((n - 1, right.shape[0], partial.shape[2]), BF)
    more = ([] if x is None else [x]) + after
    return pl.pallas_call(
        functools.partial(ring_kernel, t, n, at, tail, wave),
        grid=(1,),
        in_specs=[SMEM] + [ANY] * (3 + len(more)),
        out_specs=[full(right.shape)] * 2 + [ANY],
        out_shape=[out, out, kept],
        input_output_aliases={} if x is None else {4: 2},
        scratch_shapes=[
            pltpu.VMEM((2,) + right.shape, BF),
            pltpu.VMEM((2,) + right.shape, BF),
            pltpu.SemaphoreType.DMA((4,)),
            pltpu.SemaphoreType.DMA((2,)),
        ],
        compiler_params=room(12),
        cost_estimate=cost(30),
    )(ids, right, left, partial, *more)


def gathered_kernel(n, heads, parts, at, ids_ref, *refs):
    own_refs, refs = refs[:heads], refs[heads:]
    x_hbm, refs = refs[0], refs[1:]
    w_ref, near_ref, far_ref = refs[:3]
    o_ref, x, cols, acc, xsem, wsem = refs[-6:]
    share = near_ref.shape[2]
    near = near_ref.shape[0]

    def each(steps, do):
        for t in steps:
            do(t, pltpu.make_async_copy(x_hbm.at[t], x.at[t], xsem.at[t]))
            for p in range(parts):
                src = near_ref.at[p, t] if p < near else far_ref.at[p - near, t]
                to = ids_ref[at + 1 + p] * share
                to = pl.ds(pl.multiple_of(to, share), share)
                do(t, pltpu.make_async_copy(src, cols.at[t, to, :], wsem.at[t, p]))

    each(range(n - 1), lambda t, c: c.start())
    acc[...] = mm(joined(own_refs), w_ref[...])
    for t in range(n - 1):
        each((t,), lambda t, c: c.wait())
        if t < n - 2:
            acc[...] += mm(x[t], cols[t])
        else:
            o_ref[...] = (acc[...] + mm(x[t], cols[t])).astype(BF)


def gathered(ids, at, merged, x, out_weight, near, far, rows_all, after):
    n, heads, parts = x.shape[0] + 1, len(merged), near.shape[0] + far.shape[0]
    rows, feats = merged[0].shape[0], out_weight.shape[0]
    width = out_weight.shape[1] // n
    return pl.pallas_call(
        functools.partial(gathered_kernel, n, heads, parts, at),
        grid_spec=pltpu.PrefetchScalarGridSpec(
            num_scalar_prefetch=1,
            grid=(1,),
            in_specs=[full(m.shape) for m in merged]
            + [ANY]
            + [pl.BlockSpec((feats, width), lambda i, s: (0, s[at])), ANY, ANY]
            + [ANY] * len(after),
            out_specs=pl.BlockSpec((rows, width), lambda i, s: (0, 0)),
            scratch_shapes=[
                pltpu.VMEM((n - 1, rows, feats), BF),
                pltpu.VMEM((n - 1, feats, width), BF),
                pltpu.VMEM((rows, width), F32),
                pltpu.SemaphoreType.DMA((n - 1,)),
                pltpu.SemaphoreType.DMA((n - 1, parts)),
            ],
        ),
        out_shape=jax.ShapeDtypeStruct((rows_all, width), BF),
        compiler_params=room(48),
        cost_estimate=cost(9 * rows / 512),
    )(
        ids, *merged, x, out_weight, near, far, *after
    )


def finish_kernel(at, wave, ids_ref, right_hbm, left_hbm, p_hbm, out_in, o_hbm, got, own, sem):
    del out_in
    rows, width = own.shape
    cols = pl.ds(wave * width, width)
    copies = [
        pltpu.make_async_copy(right_hbm, got.at[0], sem.at[0]),
        pltpu.make_async_copy(left_hbm, got.at[1], sem.at[1]),
        pltpu.make_async_copy(p_hbm.at[ids_ref[at], :, cols], own, sem.at[2]),
    ]
    for c in copies:
        c.start()
    for c in copies:
        c.wait()
    total = own[...].astype(F32) + (got[0].astype(F32) + got[1].astype(F32))
    own[...] = total.astype(BF)
    last = pl.ds(o_hbm.shape[0] - rows, rows)
    out = pltpu.make_async_copy(own, o_hbm.at[last, cols], sem.at[3])
    out.start()
    out.wait()


def finish(ids, at, wave, right, left, partial, out):
    return pl.pallas_call(
        functools.partial(finish_kernel, at, wave),
        grid=(1,),
        in_specs=[SMEM] + [ANY] * 4,
        out_specs=ANY,
        out_shape=jax.ShapeDtypeStruct(out.shape, BF),
        input_output_aliases={4: 0},
        scratch_shapes=[
            pltpu.VMEM((2,) + right.shape, BF),
            pltpu.VMEM(right.shape, BF),
            pltpu.SemaphoreType.DMA((4,)),
        ],
        compiler_params=room(12),
        cost_estimate=cost(30),
    )(ids, right, left, partial, out)


def scalars(*xs):
    return jnp.stack([jnp.asarray(x, jnp.int32) for x in xs])


def shards(query, keys, values, lr_code, fast_weights, out_weight):
    rows, feats = query.shape
    contexts, groups = lax.axis_size("ctx"), lax.axis_size("head")
    c, z = lax.axis_index("ctx"), lax.axis_index("head")
    tokens_all = rows * contexts
    heads = fast_weights.shape[0]
    bits = [1 << i for i in range(contexts.bit_length() - 1)]
    bit_of = {b: (c // b) % 2 for b in bits}
    order = [[bits[1 + h % 2]] for h in range(heads)]
    order = [o + [b for b in bits[1:] if b != o[0]] for o in order]
    spread = bits[2::-1]
    places = [0]
    for b in spread:
        places = places + [p ^ b for p in places]
    share, width = feats // len(places), out_weight.shape[1] // groups
    ids = [bit_of[1], c == 0] + [bit_of[o[0]] for o in order]
    step_at = [len(ids) + 4 * (t - 1) for t in range(groups)]
    for t in range(1, groups):
        ids += [(z - t) % groups, (z + t) % groups, t > z, t > groups - 1 - z]
    tail_at = len(ids)
    ids += [z] + [(c % len(places)) ^ p for p in places]
    strip_at = len(ids)
    for s in range(1, groups):
        ids += [c % len(places), (z + s) % groups]
    ids = scalars(*ids)

    keep, other = [], []
    for h in range(heads):
        g = grads(
            h,
            strip_at,
            ids,
            lr_code.T,
            keys,
            values,
            fast_weights,
            out_weight,
            [(share, width)] * (groups - 1),
            keep[-1:],
        )
        keep.append(g[0])
        other.append(swap(g[1], 1))
        if h == 0:
            rim = shift(g[2], "ctx", 1)
            strips = [rotate(x, "head", s + 1) for s, x in enumerate(g[3:])]
    split_up = []
    for h in range(heads):
        before = [split_up[0][1], rim] if h else []
        split_up.append(split(h, ids, keep[h], other[h], before))
    away = [swap(split_up[h][1], order[h][0]) for h in range(heads)]

    per_head = 2
    pieces = []

    def attend(after):
        i = len(pieces)
        pieces.append(attention(i, FW // per_head, ids, query, keys, values, rim, after))
        return pieces[-1]

    att = attend([s[1] for s in split_up])
    pull, far = [], []
    for h in range(heads):
        more = strips[1:2] if h == heads - 1 else []
        p = total(split_up[h][0], away[h], [att] + pull + more)
        for b in order[h][1:-1]:
            p = total(p, swap(p, b), [])
        pull.append(p)
        far.append(swap(p, order[h][-1]))
        att = attend([p])
        if h == 0:
            att = attend([att])
    while len(pieces) < per_head * heads:
        att = attend([att])
    both = [x for h in range(heads) for x in (pull[h], far[h])]
    new = renorm(ids, tokens_all, fast_weights, both, [att, strips[0]] + strips[2:])

    cut = rows // 2
    merged, rest, weights = [], [], None
    for h in range(heads):
        b = order[h][0]
        near = swap(new[h], b)
        blocks = [new[h], near, swap(new[h], 1), swap(near, 1)]
        own = pieces[h * per_head : (h + 1) * per_head]
        m, r, weights = apply(h, heads, ids, query, own, blocks, cut, weights, [])
        merged.append(m)
        rest.append(r)
    to_right = [[shift(m, "head", 1) for m in merged]]
    to_left = [[shift(m, "head", -1) for m in merged]]

    near = stack([s[None] for s in strips], [merged[-1]])
    partial = partials(rest, out_weight, groups, [near])
    near = near.reshape((1,) + near.shape)
    after = near
    x = None
    for t in range(1, groups):
        right, left = [], []
        for h in range(heads):
            r, l, x = ring_step(
                t,
                groups,
                ids,
                step_at[t],
                tail_at,
                h,
                to_right[t - 1][h],
                to_left[t - 1][h],
                partial,
                x,
                [after],
            )
            after = l
            right.append(shift(r, "head", 1))
            left.append(shift(l, "head", -1))
            due = {(1, heads - 1): spread[:1], (groups - 1, heads - 1): spread[1:-1]}
            for b in due.get((t, h), []):
                near = stack([near, swap(near, b)], [after])
        to_right.append(right)
        to_left.append(left)
    out = gathered(
        ids,
        tail_at,
        merged,
        x,
        out_weight,
        near,
        swap(near, 1),
        rows,
        [after],
    )
    for h in range(heads):
        out = finish(ids, tail_at, h, to_right[-1][h], to_left[-1][h], partial, out)
    return (out, weights)


def solution(mesh):
    placed = (
        P("ctx", "head"),
        P("ctx", "head"),
        P("ctx", "head"),
        P("ctx", "head"),
        P("head", None, None, None),
        P("head", None),
    )
    return jax.shard_map(
        shards,
        mesh=mesh,
        in_specs=placed,
        out_specs=(P("ctx", "head"), P("head", None, None, None)),
        check_vma=False,
    )
```
